128 devices in a mesh: row: 4 (over z_hi, core), col: 32 (over y, x, z_lo).
Axes of the slice: x: 4, y: 4, z: 4 (z_hi: 2, z_lo: 2; z = z_hi * 2 + z_lo), core: 2. Of those that a mesh axis runs over, the one named last changes fastest.
Arguments:
- field: bfloat16 [128, 2048, 512], P('row', 'col'), may hold values from -6 to 6
- w_expand: bfloat16 [512, 2048], replicated, may hold values from -0.25 to 0.25
- dw_kernel: float32 [3, 3, 2048], replicated, may hold values from -2 to 2
- w_project: bfloat16 [2048, 512], replicated, may hold values from -0.125 to 0.125
- qkv_block: bfloat16 [512, 1536], replicated, may hold values from -5 to 5
- out_block: bfloat16 [512, 512], replicated, may hold values from -0.25 to 0.25
- qkv_grid: bfloat16 [512, 1536], replicated, may hold values from -5 to 5
- out_grid: bfloat16 [512, 512], replicated, may hold values from -0.25 to 0.25
Outputs:
- result: bfloat16 [128, 2048, 512], P('row', 'col')
The draws below stay inside these ranges and needn't reach their ends.
All inputs are finite; a program needn't handle non-finite values.
Results may differ from the reference program's by a relative error of at most 0.011.
Values may be sent and summed in bfloat16 or wider, within the bound.
No kernel may reach another device: no remote copies, remote signals or barrier semaphores. Data moves between devices by JAX's collectives and lax.ppermute only.
A program may use at most 128 MiB of HBM per device.

```python
import jax
import jax.numpy as jnp
from jax import lax

C = 512
HEADS = 16
EXPAND = 2048
H = 128
W = 2048


def draw_qkv_block(key, part):
    key = jax.random.fold_in(key, 11)
    return (jax.random.truncated_normal(key, -4.0, 4.0, (C, 3 * C), jnp.float32) * C ** (-0.5)).astype(jnp.bfloat16)


def draw_qkv_grid(key, part):
    key = jax.random.fold_in(key, 23)
    return (jax.random.truncated_normal(key, -4.0, 4.0, (C, 3 * C), jnp.float32) * C ** (-0.5)).astype(jnp.bfloat16)


def block_levels(rng, extent, cuts, low, high):
    level, own = 1.0, jax.random.fold_in(rng, 6)
    for axis_at, shards_of in cuts:
        heights = jnp.exp(jax.random.uniform(jax.random.fold_in(own, axis_at), (shards_of,), jnp.float32, low / len(cuts), high / len(cuts)))
        level = level * jnp.repeat(heights, extent[axis_at] // shards_of).reshape([-1 if axis == axis_at else 1 for axis in range(len(extent))])
    return level


def gaussian(own_key, shape, spread, most, pieces=(), dtype=jnp.bfloat16):
    entries = spread * jax.random.normal(own_key, shape, jnp.float32)
    if pieces:
        entries = entries * block_levels(own_key, shape, pieces, -0.22, 0.18)
    return jnp.clip(entries, -most, most).astype(dtype)


def setup_inputs(seed: int = 0) -> dict:
    streams_of = jax.random.split(jax.random.key(seed), 9)
    return {
        "field": gaussian(streams_of[0], (H, W, C), 1.0, 6.0, ((0, 4), (1, 32))),
        "w_expand": gaussian(streams_of[1], (C, EXPAND), C ** -0.5, 0.25),
        "dw_kernel": gaussian(streams_of[2], (3, 3, EXPAND), 9 ** -0.5, 2.0, (), jnp.float32),
        "w_project": gaussian(streams_of[3], (EXPAND, C), EXPAND ** -0.5, 0.125),
        "qkv_block": draw_qkv_block(jax.random.fold_in(streams_of[8], 71), 0),
        "out_block": gaussian(streams_of[5], (C, C), C ** -0.5, 0.25),
        "qkv_grid": draw_qkv_grid(jax.random.fold_in(streams_of[8], 71), 0),
        "out_grid": gaussian(streams_of[7], (C, C), C ** -0.5, 0.25),
    }


def layer_norm(v):
    mean = lax.optimization_barrier(jnp.mean(v, axis=-1, keepdims=True))
    cent = v - mean
    var = lax.optimization_barrier(jnp.mean(cent * cent, axis=-1, keepdims=True))
    return cent * lax.rsqrt(var + 1e-05)

def expand(rows, w_expand):
    normed = layer_norm(rows.astype(jnp.float32)).astype(jnp.bfloat16)
    pre = jnp.einsum('rwc,cd->rwd', normed.astype(jnp.float32), w_expand.astype(jnp.float32))
    return jax.nn.gelu(pre, approximate=False).astype(jnp.bfloat16)

def attend(tokens, qkv, out_proj):
    groups, count, width = tokens.shape
    head_dim = width // HEADS
    normed = layer_norm(tokens.astype(jnp.float32)).astype(jnp.bfloat16)
    proj = jnp.einsum('gtc,cd->gtd', normed.astype(jnp.float32), qkv.astype(jnp.float32)).astype(jnp.bfloat16)
    query = proj[:, :, :width].reshape(groups, count, HEADS, head_dim).astype(jnp.float32)
    keys = proj[:, :, width:2 * width].reshape(groups, count, HEADS, head_dim).astype(jnp.float32)
    values = proj[:, :, 2 * width:].reshape(groups, count, HEADS, head_dim).astype(jnp.float32)
    scores = jnp.einsum('gqhd,gkhd->ghqk', query, keys) * head_dim ** (-0.5)
    scores = scores - lax.optimization_barrier(jnp.max(scores, axis=-1, keepdims=True))
    weights = jnp.exp(scores)
    weights = (weights / lax.optimization_barrier(jnp.sum(weights, axis=-1, keepdims=True))).astype(jnp.bfloat16)
    context = jnp.einsum('ghqk,gkhd->gqhd', weights.astype(jnp.float32), values).astype(jnp.bfloat16)
    context = context.reshape(groups, count, width)
    update = jnp.einsum('gtc,cd->gtd', context.astype(jnp.float32), out_proj.astype(jnp.float32))
    return (tokens.astype(jnp.float32) + update).astype(jnp.bfloat16)

def reference(field, w_expand, dw_kernel, w_project, qkv_block, out_block, qkv_grid, out_grid):
    height, width, chans = field.shape
    band = 8
    padded = jnp.pad(field, ((1, 1), (1, 1), (0, 0)))

    def one_band(index):
        start = (index * band).astype(jnp.int32)
        rows = lax.dynamic_slice_in_dim(padded, start, band + 2, 0)
        hidden = expand(rows, w_expand)
        acc = jnp.zeros((band, width, hidden.shape[2]), jnp.float32)
        for da in range(3):
            for db in range(3):
                acc = acc + hidden[da:da + band, db:db + width].astype(jnp.float32) * dw_kernel[da, db]
        spatial = jax.nn.gelu(acc, approximate=False).astype(jnp.bfloat16)
        own = lax.dynamic_slice_in_dim(field, start, band, 0)
        proj = jnp.einsum('rwd,dc->rwc', spatial.astype(jnp.float32), w_project.astype(jnp.float32))
        return (own.astype(jnp.float32) + proj).astype(jnp.bfloat16)
    mixed = lax.map(one_band, jnp.arange(height // band).astype(jnp.int32)).reshape(height, width, chans)
    blocks = mixed.reshape(height // 8, 8, width // 8, 8, chans).transpose(0, 2, 1, 3, 4)
    blocks = blocks.reshape(height // 8, width // 8, 64, chans)
    blocks = lax.map(lambda grp: attend(grp, qkv_block, out_block), blocks)
    blocked = blocks.reshape(height // 8, width // 8, 8, 8, chans).transpose(0, 2, 1, 3, 4).reshape(height, width, chans)
    stride_h = height // 8
    stride_w = width // 8
    grid = blocked.reshape(8, stride_h, 8, stride_w, chans).transpose(1, 3, 0, 2, 4)
    grid = grid.reshape(stride_h, stride_w, 64, chans)
    grid = lax.map(lambda grp: attend(grp, qkv_grid, out_grid), grid)
    grid = grid.reshape(stride_h, stride_w, 8, 8, chans).transpose(2, 0, 3, 1, 4)
    return grid.reshape(height, width, chans)
```

```python
import functools

import jax
import jax.numpy as jnp
import numpy as np
from jax import lax
from jax.experimental import pallas as pl
from jax.experimental.pallas import tpu as pltpu
from jax.sharding import PartitionSpec as P

BF16 = jnp.bfloat16
F32 = jnp.float32
HEAD = 32
CHANS = 512
WIDE = 2048
CB = 512
VMEM_LIMIT = 56 * 2**20
SCALE_LOG2 = float(HEAD**-0.5 * np.log2(np.e))


def layer_norm(v):
    mean = jnp.mean(v, axis=-1, keepdims=True)
    cent = v - mean
    var = jnp.mean(cent * cent, axis=-1, keepdims=True)
    return (cent * lax.rsqrt(var + 1e-05)).astype(BF16)


def gelu(v):
    half = 0.5 * v
    return half + half * lax.erf(v * 0.7071067811865476)


def mm(a, b):
    return lax.dot_general(a, b, (((1,), (0,)), ((), ())), preferred_element_type=F32)


def mm_nt(a, b):
    return lax.dot_general(a, b, (((1,), (1,)), ((), ())), preferred_element_type=F32)


def permutation(dims, order):
    count = int(np.prod(dims))
    source = np.arange(count).reshape(dims).transpose(order).reshape(-1)
    matrix = np.zeros((count, count), np.float32)
    matrix[np.arange(count), source] = 1.0
    return jnp.asarray(matrix, BF16)


def whole(shape):
    zeros = (0,) * len(shape)
    return pl.BlockSpec(shape, lambda *_: zeros)


def params():
    return pltpu.CompilerParams(vmem_limit_bytes=VMEM_LIMIT)


def expand_kernel(x_ref, w_ref, perm_ref, xp_ref, hid_ref, normed):
    for pair in range(2):
        rows = x_ref[:, 2 * pair : 2 * pair + 2].reshape(256, CHANS)
        moved = mm(perm_ref[...], rows)
        xp_ref[2 * pair : 2 * pair + 2] = moved.astype(BF16).reshape(2, 8, 16, CHANS)
        normed[256 * pair : 256 * pair + 256] = layer_norm(moved)
    for at in range(0, WIDE, 256):
        pre = mm(normed[...], w_ref[:, at : at + 256])
        hid_ref[:, :, :, at : at + 256] = gelu(pre).astype(BF16).reshape(4, 8, 16, 256)


def expand(field, w_expand, part):
    return pl.pallas_call(
        expand_kernel,
        grid=(2,),
        in_specs=[
            pl.BlockSpec((2, 4, 64, CHANS), lambda s: (0, 2 * part + s, 0, 0)),
            whole((CHANS, WIDE)),
            whole((256, 256)),
        ],
        out_specs=[
            pl.BlockSpec((4, 8, 16, CHANS), lambda s: (s, 0, 0, 0)),
            pl.BlockSpec((4, 8, 16, WIDE), lambda s: (s, 0, 0, 0)),
        ],
        out_shape=[
            jax.ShapeDtypeStruct((8, 8, 16, CHANS), BF16),
            jax.ShapeDtypeStruct((8, 8, 16, WIDE), BF16),
        ],
        scratch_shapes=[pltpu.VMEM((512, CHANS), BF16)],
        compiler_params=params(),
        cost_estimate=pl.CostEstimate(
            flops=2 * 1024 * CHANS * WIDE, bytes_accessed=8 * 2**20, transcendentals=1024 * WIDE
        ),
        name="expand",
    )(field.reshape(2, 16, 64, CHANS), w_expand, permutation((2, 2, 8, 8), (1, 3, 0, 2)))


def mix_kernel(
    part, hid_ref, prev_ref, next_ref, xp_ref, top_ref, bot_ref, left_ref, right_ref, we_ref, dw_ref, wp_ref, perm_ref,
    out_ref, pad, normed, rim, spatial, acc,
):
    step = pl.program_id(0)

    @pl.when(step == 0)
    def _():
        both = jnp.concatenate([layer_norm(top_ref[...].astype(F32)), layer_norm(bot_ref[...].astype(F32))], axis=0)
        normed[0:128] = mm(perm_ref[...], both).astype(BF16)
        normed[128:176] = layer_norm(left_ref[...].astype(F32))
        normed[176:224] = layer_norm(right_ref[...].astype(F32))
        acc[...] = jnp.zeros_like(acc)

    for at in range(0, CB, 256):
        rim[:, at : at + 256] = gelu(mm(normed[...], we_ref[:, at : at + 256])).astype(BF16).astype(F32)
    pad[1:9, 1:9] = hid_ref[...]
    for j in range(8):
        before = prev_ref[0, j]
        after = next_ref[0, j]
        if part == 0:
            before = jnp.concatenate([rim[16 * j : 16 * j + 8], before.astype(F32)[0:8]], axis=0).astype(BF16)
        else:
            after = jnp.concatenate([after.astype(F32)[8:16], rim[16 * j + 8 : 16 * j + 16]], axis=0).astype(BF16)
        pad[0, 1 + j] = before
        pad[9, 1 + j] = after
    sub = lax.broadcasted_iota(jnp.int32, (8, CB), 0)
    for row in range(10):
        at = 128 + 8 * part + row
        last = pad[row, 8].astype(F32)
        first = pad[row, 1].astype(F32)
        west, east = [], []
        for b in range(2):
            turned = pltpu.roll(last[8 * b : 8 * b + 8], 1, 0)
            west.append(jnp.where(sub == 0, rim[at + 16 * b : at + 16 * b + 1], turned))
            turned = pltpu.roll(first[8 * b : 8 * b + 8], 7, 0)
            east.append(jnp.where(sub == 7, rim[at + 48 + 16 * b : at + 48 + 16 * b + 1], turned))
        pad[row, 0] = jnp.concatenate(west, axis=0).astype(BF16)
        pad[row, 9] = jnp.concatenate(east, axis=0).astype(BF16)

    for pair in range(4):
        for lane in range(0, CB, 128):
            taps = [dw_ref[t : t + 1, lane : lane + 128].astype(BF16) for t in range(9)]
            for i in (2 * pair, 2 * pair + 1):
                for j in range(8):
                    total = None
                    for t in range(9):
                        term = pad[i + t // 3, j + t % 3, :, lane : lane + 128] * taps[t]
                        total = term if total is None else total + term
                    spatial[i, j, :, lane : lane + 128] = gelu(total.astype(F32)).astype(BF16)
        rows = slice(256 * pair, 256 * pair + 256)
        acc[rows] += mm(spatial[2 * pair : 2 * pair + 2].reshape(256, CB), wp_ref[...])

    @pl.when(step == WIDE // CB - 1)
    def _():
        x = xp_ref[...].reshape(1024, CHANS).astype(F32)
        out_ref[...] = (x + acc[...]).astype(BF16).reshape(64, 16, CHANS)


def mix(part, hid, hid_other, xp, rims, w_expand, dw, w_project):
    edges = (7, 0)
    hid_spec = pl.BlockSpec((8, 8, 16, CB), lambda s: (0, 0, 0, s))
    edge_spec = [pl.BlockSpec((1, 8, 16, CB), lambda s, e=e: (e, 0, 0, s)) for e in edges]
    return pl.pallas_call(
        functools.partial(mix_kernel, part),
        grid=(WIDE // CB,),
        in_specs=[
            hid_spec,
            edge_spec[0],
            edge_spec[1],
            whole((8, 8, 16, CHANS)),
            whole((64, CHANS)),
            whole((64, CHANS)),
            whole((48, CHANS)),
            whole((48, CHANS)),
            pl.BlockSpec((CHANS, CB), lambda s: (0, s)),
            pl.BlockSpec((9, CB), lambda s: (0, s)),
            pl.BlockSpec((CB, CHANS), lambda s: (s, 0)),
            whole((128, 128)),
        ],
        out_specs=whole((64, 16, CHANS)),
        out_shape=jax.ShapeDtypeStruct((64, 16, CHANS), BF16),
        scratch_shapes=[
            pltpu.VMEM((10, 10, 16, CB), BF16),
            pltpu.VMEM((224, CHANS), BF16),
            pltpu.VMEM((224, CB), F32),
            pltpu.VMEM((8, 8, 16, CB), BF16),
            pltpu.VMEM((1024, CHANS), F32),
        ],
        compiler_params=params(),
        cost_estimate=pl.CostEstimate(
            flops=2 * 1024 * CHANS * WIDE, bytes_accessed=8 * 2**20, transcendentals=1024 * WIDE
        ),
        name="mix",
    )(hid, hid_other, hid_other, xp, *rims, w_expand, dw, w_project, permutation((2, 8, 8), (2, 0, 1)))


def segment_max(scores):
    low = lax.broadcasted_iota(jnp.int32, (1, 128), 1) < 64
    found = []
    for at in range(0, scores.shape[1], 128):
        v = scores[:, at : at + 128]
        first = jnp.max(jnp.where(low, v, -jnp.inf), axis=-1, keepdims=True)
        second = jnp.max(jnp.where(low, -jnp.inf, v), axis=-1, keepdims=True)
        found.append(jnp.where(low, first, second))
    return jnp.concatenate(found, axis=1)


def attend_kernel(home, x_ref, wqkv_ref, wo_ref, turn_ref, mask_ref, out_ref, grouped, proj, context):
    for t in range(4):
        moved = mm(turn_ref[...], x_ref[16 * t : 16 * t + 16].reshape(256, CHANS))
        grouped[:, 16 * t : 16 * t + 16] = moved.astype(BF16).reshape(16, 16, CHANS)
    mask = mask_ref[...]
    for b in range(2):
        x = grouped[8 * b : 8 * b + 8].reshape(512, CHANS).astype(F32)
        proj[...] = mm(layer_norm(x), wqkv_ref[...]).astype(BF16)
        for g in range(8):
            rows = slice(64 * g, 64 * g + 64)
            for at in range(0, CHANS, 128):
                query = proj[rows, at : at + 128]
                keys = jnp.concatenate([proj[rows, CHANS + at : CHANS + at + 128]] * 4, axis=0) * mask
                values = jnp.concatenate([proj[rows, 2 * CHANS + at : 2 * CHANS + at + 128]] * 4, axis=0) * mask
                scores = mm_nt(query, keys)
                weights = jnp.exp2((scores - segment_max(scores)) * SCALE_LOG2).astype(BF16)
                both = mm(weights, jnp.concatenate([values, mask], axis=1))
                context[rows, at : at + 128] = (both[:, :128] / both[:, 128:]).astype(BF16)
        done = x + mm(context[...], wo_ref[...])
        if home:
            grouped[8 * b : 8 * b + 8] = done.astype(BF16).reshape(8, 64, CHANS)
        else:
            done = done.reshape(4, 2, 8, 8, CHANS)
            for i in range(8):
                out_ref[i, :, b] = done[:, :, i].reshape(4, 16, CHANS).astype(BF16)
    if home:
        for t in range(4):
            moved = mm(turn_ref[...], grouped[:, 16 * t : 16 * t + 16].reshape(256, CHANS))
            out_ref[16 * t : 16 * t + 16] = moved.astype(BF16).reshape(16, 16, CHANS)


def attend(home, x, qkv, out_proj):
    heads = jnp.asarray(np.arange(256)[:, None] // 64 == np.arange(128)[None] // 32, BF16)
    shape = (64, 16, CHANS) if home else (8, 4, 2, 16, CHANS)
    return pl.pallas_call(
        functools.partial(attend_kernel, home),
        grid=(1,),
        in_specs=[
            whole((64, 16, CHANS)),
            whole((CHANS, 3 * CHANS)),
            whole((CHANS, CHANS)),
            whole((256, 256)),
            whole((256, 128)),
        ],
        out_specs=whole(shape),
        out_shape=jax.ShapeDtypeStruct(shape, BF16),
        scratch_shapes=[
            pltpu.VMEM((16, 64, CHANS), BF16),
            pltpu.VMEM((512, 3 * CHANS), BF16),
            pltpu.VMEM((512, CHANS), BF16),
        ],
        compiler_params=params(),
        cost_estimate=pl.CostEstimate(
            flops=8 * 1024 * CHANS * CHANS, bytes_accessed=4 * 2**20, transcendentals=2**20
        ),
        name="attend",
    )(x, qkv, out_proj, permutation((16, 16), (1, 0)), heads)


def exchange(blocks, groups):
    return lax.all_to_all(blocks, ("row", "col"), 0, 0, axis_index_groups=groups, tiled=True)


def on_device(field, w_expand, dw_kernel, w_project, qkv_block, out_block, qkv_grid, out_grid):
    n_row, n_col = lax.axis_size("row"), lax.axis_size("col")
    down = [(i, i + 1) for i in range(n_row - 1)]
    up = [(i + 1, i) for i in range(n_row - 1)]
    top = lax.ppermute(field[31], "row", down)
    bottom = lax.ppermute(field[0], "row", up)
    fill = jnp.zeros((14, CHANS), BF16)

    def rim(column):
        return jnp.concatenate([top[column : column + 1], field[:, column], bottom[column : column + 1], fill], axis=0)

    left = lax.ppermute(rim(63), "col", [(i, i + 1) for i in range(n_col - 1)])
    right = lax.ppermute(rim(0), "col", [(i + 1, i) for i in range(n_col - 1)])
    rims = (top, bottom, left, right)
    parts = [expand(field, w_expand, part) for part in range(2)]
    dw = dw_kernel.reshape(9, WIDE)
    groups = [[32 * row + 4 * j + c for row in range(n_row) for j in range(8)] for c in range(4)]
    homes = []
    for part in range(2):
        xp, hid = parts[part]
        mixed = mix(part, hid, parts[1 - part][1], xp, rims, w_expand, dw, w_project)
        blocked = attend(False, mixed, qkv_block, out_block).reshape(32, 2, 16, CHANS)
        gathered = exchange(blocked, groups).reshape(64, 16, CHANS)
        attended = attend(True, gathered, qkv_grid, out_grid).reshape(32, 2, 16, CHANS)
        homes.append(exchange(attended, groups))
    home = jnp.stack(homes).reshape(2, 8, 4, 2, 16, CHANS)
    return home.transpose(3, 0, 1, 2, 4, 5).reshape(32, 64, CHANS)


def solution(mesh):
    placed = (P("row", "col", None), P(), P(), P(), P(), P(), P(), P())
    return jax.shard_map(
        on_device, mesh=mesh, in_specs=placed, out_specs=P("row", "col", None), check_vma=False
    )
```

```python
import functools

import jax
import jax.numpy as jnp
import numpy as np
from jax import lax
from jax.experimental import pallas as pl
from jax.experimental.pallas import tpu as pltpu
from jax.sharding import PartitionSpec as P

BF16 = jnp.bfloat16
F32 = jnp.float32
HEAD = 32
CHANS = 512
WIDE = 2048
CB = 512
VMEM_LIMIT = 56 * 2**20
SCALE_LOG2 = float(HEAD**-0.5 * np.log2(np.e))


def layer_norm(v):
    mean = jnp.mean(v, axis=-1, keepdims=True)
    cent = v - mean
    var = jnp.mean(cent * cent, axis=-1, keepdims=True)
    return (cent * lax.rsqrt(var + 1e-05)).astype(BF16)


def gelu(v):
    half = 0.5 * v
    return half + half * lax.erf(v * 0.7071067811865476)


def mm(a, b):
    return lax.dot_general(a, b, (((1,), (0,)), ((), ())), preferred_element_type=F32)


def mm_nt(a, b):
    return lax.dot_general(a, b, (((1,), (1,)), ((), ())), preferred_element_type=F32)


def permutation(dims, order):
    count = int(np.prod(dims))
    source = np.arange(count).reshape(dims).transpose(order).reshape(-1)
    matrix = np.zeros((count, count), np.float32)
    matrix[np.arange(count), source] = 1.0
    return jnp.asarray(matrix, BF16)


def whole(shape):
    zeros = (0,) * len(shape)
    return pl.BlockSpec(shape, lambda *_: zeros)


def params():
    return pltpu.CompilerParams(vmem_limit_bytes=VMEM_LIMIT)


def segment_max(scores):
    low = lax.broadcasted_iota(jnp.int32, (1, 128), 1) < 64
    found = []
    for at in range(0, scores.shape[1], 128):
        v = scores[:, at : at + 128]
        first = jnp.max(jnp.where(low, v, -jnp.inf), axis=-1, keepdims=True)
        second = jnp.max(jnp.where(low, -jnp.inf, v), axis=-1, keepdims=True)
        found.append(jnp.where(low, first, second))
    return jnp.concatenate(found, axis=1)


def attention(grouped, wqkv_ref, wo_ref, mask_ref, proj, context, emit):
    mask = mask_ref[...]
    for half in range(2):
        x = grouped[8 * half : 8 * half + 8].reshape(512, CHANS).astype(F32)
        proj[...] = mm(layer_norm(x), wqkv_ref[...]).astype(BF16)
        for g in range(8):
            rows = slice(64 * g, 64 * g + 64)
            for at in range(0, CHANS, 128):
                query = proj[rows, at : at + 128]
                keys = jnp.concatenate([proj[rows, CHANS + at : CHANS + at + 128]] * 4, axis=0) * mask
                values = jnp.concatenate([proj[rows, 2 * CHANS + at : 2 * CHANS + at + 128]] * 4, axis=0) * mask
                scores = mm_nt(query, keys)
                weights = jnp.exp2((scores - segment_max(scores)) * SCALE_LOG2).astype(BF16)
                both = mm(weights, jnp.concatenate([values, mask], axis=1))
                context[rows, at : at + 128] = (both[:, :128] / both[:, 128:]).astype(BF16)
        emit(half, x + mm(context[...], wo_ref[...]))


def grid_kernel(x_ref, wqkv_ref, wo_ref, turn_ref, mask_ref, out_ref, grouped, proj, context):
    for t in range(4):
        moved = mm(turn_ref[...], x_ref[16 * t : 16 * t + 16].reshape(256, CHANS))
        grouped[:, 16 * t : 16 * t + 16] = moved.astype(BF16).reshape(16, 16, CHANS)

    def emit(half, rows):
        grouped[8 * half : 8 * half + 8] = rows.astype(BF16).reshape(8, 64, CHANS)

    attention(grouped, wqkv_ref, wo_ref, mask_ref, proj, context, emit)
    for t in range(4):
        moved = mm(turn_ref[...], grouped[:, 16 * t : 16 * t + 16].reshape(256, CHANS))
        out_ref[16 * t : 16 * t + 16] = moved.astype(BF16).reshape(16, 16, CHANS)


def head_mask():
    return jnp.asarray(np.arange(256)[:, None] // 64 == np.arange(128)[None] // HEAD, BF16)


def attention_scratch():
    return [
        pltpu.VMEM((16, 64, CHANS), BF16),
        pltpu.VMEM((512, 3 * CHANS), BF16),
        pltpu.VMEM((512, CHANS), BF16),
    ]


def grid_attention(x, qkv, out_proj):
    return pl.pallas_call(
        grid_kernel,
        grid=(1,),
        in_specs=[
            whole((64, 16, CHANS)),
            whole((CHANS, 3 * CHANS)),
            whole((CHANS, CHANS)),
            whole((256, 256)),
            whole((256, 128)),
        ],
        out_specs=whole((64, 16, CHANS)),
        out_shape=jax.ShapeDtypeStruct((64, 16, CHANS), BF16),
        scratch_shapes=attention_scratch(),
        compiler_params=params(),
        cost_estimate=pl.CostEstimate(
            flops=8 * 1024 * CHANS * CHANS, bytes_accessed=4 * 2**20, transcendentals=2**20
        ),
        name="grid_attention",
    )(x, qkv, out_proj, permutation((16, 16), (1, 0)), head_mask())


def local_kernel(
    part, x_ref, prev_ref, next_ref, top_ref, bot_ref, left_ref, right_ref, we_ref, dw_ref, wp_ref, wqkv_ref, wo_ref,
    spread_ref, turn_ref, mask_ref, out_ref, normed, pad, rim, spatial, acc, grouped, proj, context,
):
    step = pl.program_id(0)

    @pl.when(step == 0)
    def _():
        for pair in range(4):
            moved = mm(spread_ref[...], x_ref[:, 2 * pair : 2 * pair + 2].reshape(256, CHANS))
            acc[256 * pair : 256 * pair + 256] = moved
            normed[128 + 256 * pair : 384 + 256 * pair] = layer_norm(moved)
        if part == 0:
            before, after = (top_ref[...], prev_ref[0, 0]), (next_ref[0, 0], next_ref[1, 0])
        else:
            before, after = (prev_ref[0, 0], prev_ref[1, 0]), (next_ref[1, 0], bot_ref[...])
        edges = jnp.concatenate([before[0], after[0], before[1], after[1]], axis=0)
        moved = layer_norm(mm(spread_ref[...], edges))
        normed[0:128] = moved[0:128]
        normed[1152:1280] = moved[128:256]
        normed[1280:1328] = layer_norm(left_ref[...].astype(F32))
        normed[1328:1376] = layer_norm(right_ref[...].astype(F32))

    for at in range(0, CB, 256):
        hidden = gelu(mm(normed[...], we_ref[:, at : at + 256])).astype(BF16)
        pad[:, 1:9, :, at : at + 256] = hidden[:1280].reshape(10, 8, 16, 256)
        rim[:, at : at + 256] = hidden[1280:].astype(F32)
    sub = lax.broadcasted_iota(jnp.int32, (8, CB), 0)
    for row in range(10):
        at = 8 * part + row
        last = pad[row, 8].astype(F32)
        first = pad[row, 1].astype(F32)
        west, east = [], []
        for b in range(2):
            turned = pltpu.roll(last[8 * b : 8 * b + 8], 1, 0)
            west.append(jnp.where(sub == 0, rim[at + 16 * b : at + 16 * b + 1], turned))
            turned = pltpu.roll(first[8 * b : 8 * b + 8], 7, 0)
            east.append(jnp.where(sub == 7, rim[at + 48 + 16 * b : at + 48 + 16 * b + 1], turned))
        pad[row, 0] = jnp.concatenate(west, axis=0).astype(BF16)
        pad[row, 9] = jnp.concatenate(east, axis=0).astype(BF16)

    for pair in range(4):
        for lane in range(0, CB, 128):
            lanes = slice(lane, lane + 128)
            taps = [dw_ref[t : t + 1, lanes].astype(BF16) for t in range(9)]
            for i in (2 * pair, 2 * pair + 1):
                tiles = [[pad[i + da, jj, :, lanes] for jj in range(10)] for da in range(3)]
                for j in range(8):
                    sums = [
                        tiles[da][j] * taps[3 * da]
                        + tiles[da][j + 1] * taps[3 * da + 1]
                        + tiles[da][j + 2] * taps[3 * da + 2]
                        for da in range(3)
                    ]
                    total = sums[0] + sums[1] + sums[2]
                    spatial[i, j, :, lanes] = gelu(total.astype(F32)).astype(BF16)
        rows = slice(256 * pair, 256 * pair + 256)
        acc[rows] += mm(spatial[2 * pair : 2 * pair + 2].reshape(256, CB), wp_ref[...])

    @pl.when(step == WIDE // CB - 1)
    def _():
        for pair in range(4):
            mixed = acc[256 * pair : 256 * pair + 256].astype(BF16)
            grouped[:, 16 * pair : 16 * pair + 16] = mm(turn_ref[...], mixed).astype(BF16).reshape(16, 16, CHANS)

        def emit(half, rows):
            rows = rows.reshape(4, 2, 8, 8, CHANS)
            for i in range(8):
                out_ref[i, :, half] = rows[:, :, i].reshape(4, 16, CHANS).astype(BF16)

        attention(grouped, wqkv_ref, wo_ref, mask_ref, proj, context, emit)


def local_part(part, field, rims, w_expand, dw, w_project, qkv, out_proj):
    rows = field.reshape(2, 16, 64, CHANS)

    def edge(at):
        return pl.BlockSpec((2, 1, 64, CHANS), lambda s: (0, at, 0, 0))

    return pl.pallas_call(
        functools.partial(local_kernel, part),
        grid=(WIDE // CB,),
        in_specs=[
            pl.BlockSpec((2, 8, 64, CHANS), lambda s: (0, part, 0, 0)),
            edge((15, 7)[part]),
            edge((8, 0)[part]),
            whole((64, CHANS)),
            whole((64, CHANS)),
            whole((48, CHANS)),
            whole((48, CHANS)),
            pl.BlockSpec((CHANS, CB), lambda s: (0, s)),
            pl.BlockSpec((9, CB), lambda s: (0, s)),
            pl.BlockSpec((CB, CHANS), lambda s: (s, 0)),
            whole((CHANS, 3 * CHANS)),
            whole((CHANS, CHANS)),
            whole((256, 256)),
            whole((256, 256)),
            whole((256, 128)),
        ],
        out_specs=whole((8, 4, 2, 16, CHANS)),
        out_shape=jax.ShapeDtypeStruct((8, 4, 2, 16, CHANS), BF16),
        scratch_shapes=[
            pltpu.VMEM((1376, CHANS), BF16),
            pltpu.VMEM((10, 10, 16, CB), BF16),
            pltpu.VMEM((96, CB), F32),
            pltpu.VMEM((8, 8, 16, CB), BF16),
            pltpu.VMEM((1024, CHANS), F32),
            *attention_scratch(),
        ],
        compiler_params=params(),
        cost_estimate=pl.CostEstimate(
            flops=4 * 1024 * CHANS * WIDE, bytes_accessed=8 * 2**20, transcendentals=2048 * WIDE
        ),
        name="local_part",
    )(
        rows, rows, rows, *rims, w_expand, dw, w_project, qkv, out_proj,
        permutation((2, 2, 8, 8), (1, 3, 0, 2)), permutation((16, 16), (1, 0)), head_mask(),
    )


def exchange(blocks, groups):
    return lax.all_to_all(blocks, ("row", "col"), 0, 0, axis_index_groups=groups, tiled=True)


def on_device(field, w_expand, dw_kernel, w_project, qkv_block, out_block, qkv_grid, out_grid):
    n_row, n_col = lax.axis_size("row"), lax.axis_size("col")
    down = [(i, i + 1) for i in range(n_row - 1)]
    up = [(i + 1, i) for i in range(n_row - 1)]
    top = lax.ppermute(field[31], "row", down)
    bottom = lax.ppermute(field[0], "row", up)
    fill = jnp.zeros((14, CHANS), BF16)

    def rim(column):
        return jnp.concatenate([top[column : column + 1], field[:, column], bottom[column : column + 1], fill], axis=0)

    left = lax.ppermute(rim(63), "col", [(i, i + 1) for i in range(n_col - 1)])
    right = lax.ppermute(rim(0), "col", [(i + 1, i) for i in range(n_col - 1)])
    rims = (top, bottom, left, right)
    dw = dw_kernel.reshape(9, WIDE)
    groups = [[32 * row + 4 * j + c for row in range(n_row) for j in range(8)] for c in range(4)]
    homes = []
    for part in range(2):
        blocked = local_part(part, field, rims, w_expand, dw, w_project, qkv_block, out_block)
        gathered = exchange(blocked.reshape(32, 2, 16, CHANS), groups).reshape(64, 16, CHANS)
        attended = grid_attention(gathered, qkv_grid, out_grid)
        homes.append(exchange(attended.reshape(32, 2, 16, CHANS), groups))
    home = jnp.stack(homes).reshape(2, 8, 4, 2, 16, CHANS)
    return home.transpose(3, 0, 1, 2, 4, 5).reshape(32, 64, CHANS)


def solution(mesh):
    placed = (P("row", "col", None), P(), P(), P(), P(), P(), P(), P())
    return jax.shard_map(
        on_device, mesh=mesh, in_specs=placed, out_specs=P("row", "col", None), check_vma=False
    )
```

```python
import functools

import jax
import jax.numpy as jnp
import numpy as np
from jax import lax
from jax.experimental import pallas as pl
from jax.experimental.pallas import tpu as pltpu
from jax.sharding import PartitionSpec as P

BF16 = jnp.bfloat16
F32 = jnp.float32
HEAD = 32
CHANS = 512
WIDE = 2048
CB = 1024
VMEM_LIMIT = 56 * 2**20
SCALE_LOG2 = float(HEAD**-0.5 * np.log2(np.e))


def layer_norm(v):
    mean = jnp.mean(v, axis=-1, keepdims=True)
    cent = v - mean
    var = jnp.mean(cent * cent, axis=-1, keepdims=True)
    return (cent * lax.rsqrt(var + 1e-05)).astype(BF16)


def gelu(v):
    half = 0.5 * v
    return half + half * lax.erf(v * 0.7071067811865476)


def mm(a, b):
    return lax.dot_general(a, b, (((1,), (0,)), ((), ())), preferred_element_type=F32)


def mm_nt(a, b):
    return lax.dot_general(a, b, (((1,), (1,)), ((), ())), preferred_element_type=F32)


def permutation(dims, order):
    count = int(np.prod(dims))
    source = np.arange(count).reshape(dims).transpose(order).reshape(-1)
    matrix = np.zeros((count, count), np.float32)
    matrix[np.arange(count), source] = 1.0
    return jnp.asarray(matrix, BF16)


def whole(shape):
    zeros = (0,) * len(shape)
    return pl.BlockSpec(shape, lambda *_: zeros)


def params():
    return pltpu.CompilerParams(vmem_limit_bytes=VMEM_LIMIT)


def segment_max(scores):
    low = lax.broadcasted_iota(jnp.int32, (1, 128), 1) < 64
    found = []
    for at in range(0, scores.shape[1], 128):
        v = scores[:, at : at + 128]
        first = jnp.max(jnp.where(low, v, -jnp.inf), axis=-1, keepdims=True)
        second = jnp.max(jnp.where(low, -jnp.inf, v), axis=-1, keepdims=True)
        found.append(jnp.where(low, first, second))
    return jnp.concatenate(found, axis=1)


def attention(grouped, wqkv_ref, wo_ref, mask_ref, proj, context, emit):
    mask = mask_ref[...]
    for half in range(2):
        x = grouped[8 * half : 8 * half + 8].reshape(512, CHANS).astype(F32)
        proj[...] = mm(layer_norm(x), wqkv_ref[...]).astype(BF16)
        for g in range(8):
            rows = slice(64 * g, 64 * g + 64)
            for at in range(0, CHANS, 128):
                query = proj[rows, at : at + 128]
                keys = jnp.concatenate([proj[rows, CHANS + at : CHANS + at + 128]] * 4, axis=0) * mask
                values = jnp.concatenate([proj[rows, 2 * CHANS + at : 2 * CHANS + at + 128]] * 4, axis=0) * mask
                scores = mm_nt(query, keys)
                weights = jnp.exp2((scores - segment_max(scores)) * SCALE_LOG2).astype(BF16)
                both = mm(weights, jnp.concatenate([values, mask], axis=1))
                context[rows, at : at + 128] = (both[:, :128] / both[:, 128:]).astype(BF16)
        emit(half, x + mm(context[...], wo_ref[...]))


def grid_kernel(x_ref, wqkv_ref, wo_ref, turn_ref, mask_ref, *rest):
    out_ref, grouped, proj, context = rest[-4:]
    for t in range(4):
        moved = mm(turn_ref[...], x_ref[16 * t : 16 * t + 16].reshape(256, CHANS))
        grouped[:, 16 * t : 16 * t + 16] = moved.astype(BF16).reshape(16, 16, CHANS)

    def emit(half, rows):
        grouped[8 * half : 8 * half + 8] = rows.astype(BF16).reshape(8, 64, CHANS)

    attention(grouped, wqkv_ref, wo_ref, mask_ref, proj, context, emit)
    for t in range(4):
        moved = mm(turn_ref[...], grouped[:, 16 * t : 16 * t + 16].reshape(256, CHANS))
        out_ref[8 * t : 8 * t + 8, 0] = moved.astype(BF16).reshape(8, 2, 16, CHANS)


def head_mask():
    return jnp.asarray(np.arange(256)[:, None] // 64 == np.arange(128)[None] // HEAD, BF16)


def attention_scratch():
    return [
        pltpu.VMEM((16, 64, CHANS), BF16),
        pltpu.VMEM((512, 3 * CHANS), BF16),
        pltpu.VMEM((512, CHANS), BF16),
    ]


def grid_attention(part, x, qkv, out_proj, earlier):
    shape = (32, 2, 2, 16, CHANS)
    kept = [] if earlier is None else [earlier]
    return pl.pallas_call(
        grid_kernel,
        grid=(1,),
        in_specs=[
            whole((64, 16, CHANS)),
            whole((CHANS, 3 * CHANS)),
            whole((CHANS, CHANS)),
            whole((256, 256)),
            whole((256, 128)),
            *[pl.BlockSpec(memory_space=pl.ANY) for _ in kept],
        ],
        out_specs=pl.BlockSpec((32, 1, 2, 16, CHANS), lambda s: (0, part, 0, 0, 0)),
        out_shape=jax.ShapeDtypeStruct(shape, BF16),
        scratch_shapes=attention_scratch(),
        input_output_aliases={5: 0} if kept else {},
        compiler_params=params(),
        cost_estimate=pl.CostEstimate(
            flops=8 * 1024 * CHANS * CHANS, bytes_accessed=4 * 2**20, transcendentals=2**20
        ),
        name="grid_attention",
    )(x, qkv, out_proj, permutation((16, 16), (1, 0)), head_mask(), *kept)


def local_kernel(
    part, x_ref, prev_ref, next_ref, top_ref, bot_ref, left_ref, right_ref, we_ref, dw_ref, wp_ref, wqkv_ref, wo_ref,
    spread_ref, turn_ref, mask_ref, out_ref, normed, pad, rim, spatial, acc, grouped, proj, context,
):
    step = pl.program_id(0)

    @pl.when(step == 0)
    def _():
        for pair in range(4):
            moved = mm(spread_ref[...], x_ref[:, 2 * pair : 2 * pair + 2].reshape(256, CHANS))
            acc[256 * pair : 256 * pair + 256] = moved
            normed[128 + 256 * pair : 384 + 256 * pair] = layer_norm(moved)
        if part == 0:
            before, after = (top_ref[...], prev_ref[0, 0]), (next_ref[0, 0], next_ref[1, 0])
        else:
            before, after = (prev_ref[0, 0], prev_ref[1, 0]), (next_ref[1, 0], bot_ref[...])
        edges = jnp.concatenate([before[0], after[0], before[1], after[1]], axis=0)
        moved = layer_norm(mm(spread_ref[...], edges))
        normed[0:128] = moved[0:128]
        normed[1152:1280] = moved[128:256]
        normed[1280:1328] = layer_norm(left_ref[...].astype(F32))
        normed[1328:1376] = layer_norm(right_ref[...].astype(F32))

    for at in range(0, CB, 256):
        hidden = gelu(mm(normed[...], we_ref[:, at : at + 256])).astype(BF16)
        pad[:, 1:9, :, at : at + 256] = hidden[:1280].reshape(10, 8, 16, 256)
        rim[:, at : at + 256] = hidden[1280:].astype(F32)
    sub = lax.broadcasted_iota(jnp.int32, (8, CB), 0)
    for row in range(10):
        at = 8 * part + row
        last = pad[row, 8].astype(F32)
        first = pad[row, 1].astype(F32)
        west, east = [], []
        for b in range(2):
            turned = pltpu.roll(last[8 * b : 8 * b + 8], 1, 0)
            west.append(jnp.where(sub == 0, rim[at + 16 * b : at + 16 * b + 1], turned))
            turned = pltpu.roll(first[8 * b : 8 * b + 8], 7, 0)
            east.append(jnp.where(sub == 7, rim[at + 48 + 16 * b : at + 48 + 16 * b + 1], turned))
        pad[row, 0] = jnp.concatenate(west, axis=0).astype(BF16)
        pad[row, 9] = jnp.concatenate(east, axis=0).astype(BF16)

    taps = [[jnp.broadcast_to(dw_ref[a, b : b + 1].astype(BF16), (16, CB)) for b in range(3)] for a in range(3)]
    for pair in range(4):
        for i in (2 * pair, 2 * pair + 1):
            for j in range(8):
                sums = [
                    pad[i + a, j] * taps[a][0] + pad[i + a, j + 1] * taps[a][1] + pad[i + a, j + 2] * taps[a][2]
                    for a in range(3)
                ]
                total = sums[0] + sums[1] + sums[2]
                spatial[i, j] = gelu(total.astype(F32)).astype(BF16)
        rows = slice(256 * pair, 256 * pair + 256)
        acc[rows] += mm(spatial[2 * pair : 2 * pair + 2].reshape(256, CB), wp_ref[...])

    @pl.when(step == WIDE // CB - 1)
    def _():
        for pair in range(4):
            mixed = acc[256 * pair : 256 * pair + 256].astype(BF16)
            grouped[:, 16 * pair : 16 * pair + 16] = mm(turn_ref[...], mixed).astype(BF16).reshape(16, 16, CHANS)

        def emit(half, rows):
            rows = rows.reshape(4, 2, 8, 8, CHANS)
            for i in range(8):
                out_ref[i, :, half] = rows[:, :, i].reshape(4, 16, CHANS).astype(BF16)

        attention(grouped, wqkv_ref, wo_ref, mask_ref, proj, context, emit)


def local_part(part, field, rims, w_expand, dw_kernel, w_project, qkv, out_proj):
    rows = field.reshape(2, 16, 64, CHANS)

    def edge(at):
        return pl.BlockSpec((2, 1, 64, CHANS), lambda s: (0, at, 0, 0))

    return pl.pallas_call(
        functools.partial(local_kernel, part),
        grid=(WIDE // CB,),
        in_specs=[
            pl.BlockSpec((2, 8, 64, CHANS), lambda s: (0, part, 0, 0)),
            edge((15, 7)[part]),
            edge((8, 0)[part]),
            whole((64, CHANS)),
            whole((64, CHANS)),
            whole((48, CHANS)),
            whole((48, CHANS)),
            pl.BlockSpec((CHANS, CB), lambda s: (0, s)),
            pl.BlockSpec((3, 3, CB), lambda s: (0, 0, s)),
            pl.BlockSpec((CB, CHANS), lambda s: (s, 0)),
            whole((CHANS, 3 * CHANS)),
            whole((CHANS, CHANS)),
            whole((256, 256)),
            whole((256, 256)),
            whole((256, 128)),
        ],
        out_specs=whole((8, 4, 2, 16, CHANS)),
        out_shape=jax.ShapeDtypeStruct((8, 4, 2, 16, CHANS), BF16),
        scratch_shapes=[
            pltpu.VMEM((1376, CHANS), BF16),
            pltpu.VMEM((10, 10, 16, CB), BF16),
            pltpu.VMEM((96, CB), F32),
            pltpu.VMEM((8, 8, 16, CB), BF16),
            pltpu.VMEM((1024, CHANS), F32),
            *attention_scratch(),
        ],
        compiler_params=params(),
        cost_estimate=pl.CostEstimate(
            flops=4 * 1024 * CHANS * WIDE, bytes_accessed=8 * 2**20, transcendentals=2048 * WIDE
        ),
        name="local_part",
    )(
        rows, rows, rows, *rims, w_expand, dw_kernel, w_project, qkv, out_proj,
        permutation((2, 2, 8, 8), (1, 3, 0, 2)), permutation((16, 16), (1, 0)), head_mask(),
    )


def exchange(blocks, groups):
    return lax.all_to_all(blocks, ("row", "col"), 0, 0, axis_index_groups=groups, tiled=True)


def on_device(field, w_expand, dw_kernel, w_project, qkv_block, out_block, qkv_grid, out_grid):
    n_row, n_col = lax.axis_size("row"), lax.axis_size("col")
    down = [(i, i + 1) for i in range(n_row - 1)]
    up = [(i + 1, i) for i in range(n_row - 1)]
    top = lax.ppermute(field[31], "row", down)
    bottom = lax.ppermute(field[0], "row", up)
    fill = jnp.zeros((14, CHANS), BF16)

    def rim(column):
        return jnp.concatenate([top[column : column + 1], field[:, column], bottom[column : column + 1], fill], axis=0)

    left = lax.ppermute(rim(63), "col", [(i, i + 1) for i in range(n_col - 1)])
    right = lax.ppermute(rim(0), "col", [(i + 1, i) for i in range(n_col - 1)])
    rims = (top, bottom, left, right)
    groups = [[32 * row + 4 * j + c for row in range(n_row) for j in range(8)] for c in range(4)]
    gathered = []
    for part in range(2):
        blocked = local_part(part, field, rims, w_expand, dw_kernel, w_project, qkv_block, out_block)
        gathered.append(exchange(blocked.reshape(32, 2, 16, CHANS), groups).reshape(64, 16, CHANS))
    attended = None
    for part in range(2):
        attended = grid_attention(part, gathered[part], qkv_grid, out_grid, attended)
    home = exchange(attended, groups).reshape(8, 4, 2, 2, 16, CHANS)
    return home.transpose(3, 2, 0, 1, 4, 5).reshape(32, 64, CHANS)


def solution(mesh):
    placed = (P("row", "col", None), P(), P(), P(), P(), P(), P(), P())
    return jax.shard_map(
        on_device, mesh=mesh, in_specs=placed, out_specs=P("row", "col", None), check_vma=False
    )
```

```python
import functools

import jax
import jax.numpy as jnp
import numpy as np
from jax import lax
from jax.experimental import pallas as pl
from jax.experimental.pallas import tpu as pltpu
from jax.sharding import PartitionSpec as P

BF16 = jnp.bfloat16
F32 = jnp.float32
HEAD = 32
CHANS = 512
WIDE = 2048
CB = 1024
VMEM_LIMIT = 56 * 2**20
SCALE_LOG2 = float(HEAD**-0.5 * np.log2(np.e))


def layer_norm(v):
    mean = jnp.mean(v, axis=-1, keepdims=True)
    cent = v - mean
    var = jnp.mean(cent * cent, axis=-1, keepdims=True)
    return (cent * lax.rsqrt(var + 1e-05)).astype(BF16)


def gelu(v):
    half = 0.5 * v
    return half + half * lax.erf(v * 0.7071067811865476)


def mm(a, b):
    return lax.dot_general(a, b, (((1,), (0,)), ((), ())), preferred_element_type=F32)


def mm_nt(a, b):
    return lax.dot_general(a, b, (((1,), (1,)), ((), ())), preferred_element_type=F32)


def permutation(dims, order):
    count = int(np.prod(dims))
    source = np.arange(count).reshape(dims).transpose(order).reshape(-1)
    matrix = np.zeros((count, count), np.float32)
    matrix[np.arange(count), source] = 1.0
    return jnp.asarray(matrix, BF16)


def whole(shape):
    zeros = (0,) * len(shape)
    return pl.BlockSpec(shape, lambda *_: zeros)


def params():
    return pltpu.CompilerParams(vmem_limit_bytes=VMEM_LIMIT)


def segment_max(scores):
    low = lax.broadcasted_iota(jnp.int32, (1, 128), 1) < 64
    found = []
    for at in range(0, scores.shape[1], 128):
        v = scores[:, at : at + 128]
        first = jnp.max(jnp.where(low, v, -jnp.inf), axis=-1, keepdims=True)
        second = jnp.max(jnp.where(low, -jnp.inf, v), axis=-1, keepdims=True)
        found.append(jnp.where(low, first, second))
    return jnp.concatenate(found, axis=1)


def attention(grouped, wqkv_ref, wo_ref, mask_ref, proj, context, emit):
    mask = mask_ref[...]
    for half in range(2):
        x = grouped[8 * half : 8 * half + 8].reshape(512, CHANS).astype(F32)
        proj[...] = mm(layer_norm(x), wqkv_ref[...]).astype(BF16)
        for g in range(8):
            rows = slice(64 * g, 64 * g + 64)
            for at in range(0, CHANS, 128):
                query = proj[rows, at : at + 128]
                keys = jnp.concatenate([proj[rows, CHANS + at : CHANS + at + 128]] * 4, axis=0) * mask
                values = jnp.concatenate([proj[rows, 2 * CHANS + at : 2 * CHANS + at + 128]] * 4, axis=0) * mask
                scores = mm_nt(query, keys)
                weights = jnp.exp2((scores - segment_max(scores)) * SCALE_LOG2).astype(BF16)
                both = mm(weights, jnp.concatenate([values, mask], axis=1))
                context[rows, at : at + 128] = (both[:, :128] / both[:, 128:]).astype(BF16)
        emit(half, x + mm(context[...], wo_ref[...]))


def weight_copies(wqkv_hbm, wo_hbm, wqkv_ref, wo_ref, sems):
    return [
        pltpu.make_async_copy(wqkv_hbm, wqkv_ref, sems.at[0]),
        pltpu.make_async_copy(wo_hbm, wo_ref, sems.at[1]),
    ]


def grid_kernel(x_ref, turn_ref, mask_ref, wqkv_hbm, wo_hbm, *rest):
    out_ref, grouped, proj, context, wqkv_ref, wo_ref, sems = rest[-7:]
    copies = weight_copies(wqkv_hbm, wo_hbm, wqkv_ref, wo_ref, sems)
    for copy in copies:
        copy.start()
    for t in range(4):
        moved = mm(turn_ref[...], x_ref[16 * t : 16 * t + 16].reshape(256, CHANS))
        grouped[:, 16 * t : 16 * t + 16] = moved.astype(BF16).reshape(16, 16, CHANS)

    for copy in copies:
        copy.wait()

    def emit(half, rows):
        grouped[8 * half : 8 * half + 8] = rows.astype(BF16).reshape(8, 64, CHANS)

    attention(grouped, wqkv_ref, wo_ref, mask_ref, proj, context, emit)
    for t in range(4):
        moved = mm(turn_ref[...], grouped[:, 16 * t : 16 * t + 16].reshape(256, CHANS))
        out_ref[8 * t : 8 * t + 8, 0] = moved.astype(BF16).reshape(8, 2, 16, CHANS)


def head_mask():
    return jnp.asarray(np.arange(256)[:, None] // 64 == np.arange(128)[None] // HEAD, BF16)


def attention_scratch():
    return [
        pltpu.VMEM((16, 64, CHANS), BF16),
        pltpu.VMEM((512, 3 * CHANS), BF16),
        pltpu.VMEM((512, CHANS), BF16),
        pltpu.VMEM((CHANS, 3 * CHANS), BF16),
        pltpu.VMEM((CHANS, CHANS), BF16),
        pltpu.SemaphoreType.DMA((2,)),
    ]


def grid_attention(part, x, qkv, out_proj, earlier):
    shape = (32, 2, 2, 16, CHANS)
    kept = [] if earlier is None else [earlier]
    return pl.pallas_call(
        grid_kernel,
        grid=(1,),
        in_specs=[
            whole((64, 16, CHANS)),
            whole((256, 256)),
            whole((256, 128)),
            pl.BlockSpec(memory_space=pl.ANY),
            pl.BlockSpec(memory_space=pl.ANY),
            *[pl.BlockSpec(memory_space=pl.ANY) for _ in kept],
        ],
        out_specs=pl.BlockSpec((32, 1, 2, 16, CHANS), lambda s: (0, part, 0, 0, 0)),
        out_shape=jax.ShapeDtypeStruct(shape, BF16),
        scratch_shapes=attention_scratch(),
        input_output_aliases={5: 0} if kept else {},
        compiler_params=params(),
        cost_estimate=pl.CostEstimate(
            flops=8 * 1024 * CHANS * CHANS, bytes_accessed=4 * 2**20, transcendentals=2**20
        ),
        name="grid_attention",
    )(x, permutation((16, 16), (1, 0)), head_mask(), qkv, out_proj, *kept)


def expand_kernel(x_ref, w_ref, spread_ref, xp_ref, hid_ref, normed):
    for pair in range(2):
        moved = mm(spread_ref[...], x_ref[:, 2 * pair : 2 * pair + 2].reshape(256, CHANS))
        xp_ref[2 * pair : 2 * pair + 2] = moved.astype(BF16).reshape(2, 8, 16, CHANS)
        normed[256 * pair : 256 * pair + 256] = layer_norm(moved)
    for at in range(0, WIDE, 256):
        made = gelu(mm(normed[...], w_ref[:, at : at + 256])).astype(BF16)
        hid_ref[:, :, :, at : at + 256] = made.reshape(4, 8, 16, 256)


def expand(field, w_expand, after):
    return pl.pallas_call(
        lambda x, w, spread, _, *rest: expand_kernel(x, w, spread, *rest),
        grid=(4,),
        in_specs=[
            pl.BlockSpec((2, 4, 64, CHANS), lambda s: (0, s, 0, 0)),
            whole((CHANS, WIDE)),
            whole((256, 256)),
            pl.BlockSpec(memory_space=pl.ANY),
        ],
        out_specs=[
            pl.BlockSpec((4, 8, 16, CHANS), lambda s: (s, 0, 0, 0)),
            pl.BlockSpec((4, 8, 16, WIDE), lambda s: (s, 0, 0, 0)),
        ],
        out_shape=[
            jax.ShapeDtypeStruct((16, 8, 16, CHANS), BF16),
            jax.ShapeDtypeStruct((16, 8, 16, WIDE), BF16),
        ],
        scratch_shapes=[pltpu.VMEM((512, CHANS), BF16)],
        compiler_params=params(),
        cost_estimate=pl.CostEstimate(
            flops=4 * 1024 * CHANS * WIDE, bytes_accessed=16 * 2**20, transcendentals=2048 * WIDE
        ),
        name="expand",
    )(field.reshape(2, 16, 64, CHANS), w_expand, permutation((2, 2, 8, 8), (1, 3, 0, 2)), after)


def local_kernel(
    part, hid_ref, prev_ref, next_ref, xp_ref, rim_ref, left_ref, right_ref, we_ref, dw_ref, wp_ref,
    spread_ref, turn_ref, mask_ref, wqkv_hbm, wo_hbm, out_ref, pad, normed, rim, spatial, acc, grouped, proj, context,
    wqkv_ref, wo_ref, sems,
):
    step = pl.program_id(0)
    copies = weight_copies(wqkv_hbm, wo_hbm, wqkv_ref, wo_ref, sems)

    @pl.when(step == 0)
    def _():
        for copy in copies:
            copy.start()
        normed[0:64] = mm(spread_ref[...], layer_norm(rim_ref[...].astype(F32))).astype(BF16)
        normed[64:112] = layer_norm(left_ref[...].astype(F32))
        normed[112:160] = layer_norm(right_ref[...].astype(F32))
        acc[...] = xp_ref[...].reshape(1024, CHANS).astype(F32)

    for at in range(0, CB, 256):
        rim[:, at : at + 256] = gelu(mm(normed[...], we_ref[:, at : at + 256])).astype(BF16).astype(F32)
    pad[1:9, 1:9] = hid_ref[...]
    for j in range(8):
        before = prev_ref[0, j]
        after = next_ref[0, j]
        if part == 0:
            before = jnp.concatenate([rim[8 * j : 8 * j + 8], before.astype(F32)[0:8]], axis=0).astype(BF16)
        else:
            after = jnp.concatenate([after.astype(F32)[8:16], rim[8 * j : 8 * j + 8]], axis=0).astype(BF16)
        pad[0, 1 + j] = before
        pad[9, 1 + j] = after
    sub = lax.broadcasted_iota(jnp.int32, (8, CB), 0)
    for row in range(10):
        at = 64 + 8 * part + row
        last = pad[row, 8].astype(F32)
        first = pad[row, 1].astype(F32)
        west, east = [], []
        for b in range(2):
            turned = pltpu.roll(last[8 * b : 8 * b + 8], 1, 0)
            west.append(jnp.where(sub == 0, rim[at + 16 * b : at + 16 * b + 1], turned))
            turned = pltpu.roll(first[8 * b : 8 * b + 8], 7, 0)
            east.append(jnp.where(sub == 7, rim[at + 48 + 16 * b : at + 48 + 16 * b + 1], turned))
        pad[row, 0] = jnp.concatenate(west, axis=0).astype(BF16)
        pad[row, 9] = jnp.concatenate(east, axis=0).astype(BF16)

    taps = [[jnp.broadcast_to(dw_ref[a, b : b + 1].astype(BF16), (16, CB)) for b in range(3)] for a in range(3)]
    for pair in range(4):
        for i in (2 * pair, 2 * pair + 1):
            for j in range(8):
                sums = [
                    pad[i + a, j] * taps[a][0] + pad[i + a, j + 1] * taps[a][1] + pad[i + a, j + 2] * taps[a][2]
                    for a in range(3)
                ]
                total = sums[0] + sums[1] + sums[2]
                spatial[i, j] = gelu(total.astype(F32)).astype(BF16)
        rows = slice(256 * pair, 256 * pair + 256)
        acc[rows] += mm(spatial[2 * pair : 2 * pair + 2].reshape(256, CB), wp_ref[...])

    @pl.when(step == WIDE // CB - 1)
    def _():
        for pair in range(4):
            mixed = acc[256 * pair : 256 * pair + 256].astype(BF16)
            grouped[:, 16 * pair : 16 * pair + 16] = mm(turn_ref[...], mixed).astype(BF16).reshape(16, 16, CHANS)
        for copy in copies:
            copy.wait()

        def emit(half, rows):
            rows = rows.reshape(4, 2, 8, 8, CHANS)
            for i in range(8):
                out_ref[i, :, half] = rows[:, :, i].reshape(4, 16, CHANS).astype(BF16)

        attention(grouped, wqkv_ref, wo_ref, mask_ref, proj, context, emit)


def local_part(part, xp, hid, rims, w_expand, dw_kernel, w_project, qkv, out_proj):
    top, bottom, left, right = rims

    def edge(at):
        return pl.BlockSpec((1, 8, 16, CB), lambda s: (at, 0, 0, s))

    return pl.pallas_call(
        functools.partial(local_kernel, part),
        grid=(WIDE // CB,),
        in_specs=[
            pl.BlockSpec((8, 8, 16, CB), lambda s: (part, 0, 0, s)),
            edge((15, 7)[part]),
            edge((8, 0)[part]),
            pl.BlockSpec((8, 8, 16, CHANS), lambda s: (part, 0, 0, 0)),
            whole((64, CHANS)),
            whole((48, CHANS)),
            whole((48, CHANS)),
            pl.BlockSpec((CHANS, CB), lambda s: (0, s)),
            pl.BlockSpec((3, 3, CB), lambda s: (0, 0, s)),
            pl.BlockSpec((CB, CHANS), lambda s: (s, 0)),
            whole((64, 64)),
            whole((256, 256)),
            whole((256, 128)),
            pl.BlockSpec(memory_space=pl.ANY),
            pl.BlockSpec(memory_space=pl.ANY),
        ],
        out_specs=whole((8, 4, 2, 16, CHANS)),
        out_shape=jax.ShapeDtypeStruct((8, 4, 2, 16, CHANS), BF16),
        scratch_shapes=[
            pltpu.VMEM((10, 10, 16, CB), BF16),
            pltpu.VMEM((160, CHANS), BF16),
            pltpu.VMEM((160, CB), F32),
            pltpu.VMEM((8, 8, 16, CB), BF16),
            pltpu.VMEM((1024, CHANS), F32),
            *attention_scratch(),
        ],
        compiler_params=params(),
        cost_estimate=pl.CostEstimate(
            flops=4 * 1024 * CHANS * WIDE, bytes_accessed=8 * 2**20, transcendentals=2048 * WIDE
        ),
        name="local_part",
    )(
        hid, hid, hid, xp, (top, bottom)[part], left, right, w_expand, dw_kernel, w_project,
        permutation((8, 8), (1, 0)), permutation((16, 16), (1, 0)), head_mask(), qkv, out_proj,
    )


def exchange(blocks, groups):
    return lax.all_to_all(blocks, ("row", "col"), 0, 0, axis_index_groups=groups, tiled=True)


def on_device(field, w_expand, dw_kernel, w_project, qkv_block, out_block, qkv_grid, out_grid):
    n_row, n_col = lax.axis_size("row"), lax.axis_size("col")
    down = [(i, i + 1) for i in range(n_row - 1)]
    up = [(i + 1, i) for i in range(n_row - 1)]
    top = lax.ppermute(field[31], "row", down)
    bottom = lax.ppermute(field[0], "row", up)
    fill = jnp.zeros((14, CHANS), BF16)

    def rim(column):
        return jnp.concatenate([top[column : column + 1], field[:, column], bottom[column : column + 1], fill], axis=0)

    east, west = rim(63), rim(0)
    left = lax.ppermute(east, "col", [(i, i + 1) for i in range(n_col - 1)])
    right = lax.ppermute(west, "col", [(i + 1, i) for i in range(n_col - 1)])
    rims = (top, bottom, left, right)
    xp, hid = expand(field, w_expand, east)
    groups = [[32 * row + 4 * j + c for row in range(n_row) for j in range(8)] for c in range(4)]
    gathered = []
    for part in range(2):
        blocked = local_part(part, xp, hid, rims, w_expand, dw_kernel, w_project, qkv_block, out_block)
        gathered.append(exchange(blocked.reshape(32, 2, 16, CHANS), groups).reshape(64, 16, CHANS))
    attended = None
    for part in range(2):
        attended = grid_attention(part, gathered[part], qkv_grid, out_grid, attended)
    home = exchange(attended, groups).reshape(8, 4, 2, 2, 16, CHANS)
    return home.transpose(3, 2, 0, 1, 4, 5).reshape(32, 64, CHANS)


def solution(mesh):
    placed = (P("row", "col", None), P(), P(), P(), P(), P(), P(), P())
    return jax.shard_map(
        on_device, mesh=mesh, in_specs=placed, out_specs=P("row", "col", None), check_vma=False
    )
```

```python
import functools

import jax
import jax.numpy as jnp
import numpy as np
from jax import lax
from jax.experimental import pallas as pl
from jax.experimental.pallas import tpu as pltpu
from jax.sharding import PartitionSpec as P

BF16 = jnp.bfloat16
F32 = jnp.float32
HEAD = 32
CHANS = 512
WIDE = 2048
CB = 1024
VMEM_LIMIT = 24 * 2**20
SCALE_LOG2 = float(HEAD**-0.5 * np.log2(np.e))


def layer_norm(v):
    mean = jnp.mean(v, axis=-1, keepdims=True)
    cent = v - mean
    var = jnp.mean(cent * cent, axis=-1, keepdims=True)
    return (cent * lax.rsqrt(var + 1e-05)).astype(BF16)


def gelu(v):
    half = 0.5 * v
    return half + half * lax.erf(v * 0.7071067811865476)


def mm(a, b):
    return lax.dot_general(a, b, (((1,), (0,)), ((), ())), preferred_element_type=F32)


def mm_nt(a, b):
    return lax.dot_general(a, b, (((1,), (1,)), ((), ())), preferred_element_type=F32)


def permutation(dims, order):
    count = int(np.prod(dims))
    source = np.arange(count).reshape(dims).transpose(order).reshape(-1)
    matrix = np.zeros((count, count), np.float32)
    matrix[np.arange(count), source] = 1.0
    return jnp.asarray(matrix, BF16)


def whole(shape):
    zeros = (0,) * len(shape)
    return pl.BlockSpec(shape, lambda *_: zeros)


def params():
    return pltpu.CompilerParams(vmem_limit_bytes=VMEM_LIMIT)


def segment_max(scores):
    low = lax.broadcasted_iota(jnp.int32, (1, 128), 1) < 64
    found = []
    for at in range(0, scores.shape[1], 128):
        v = scores[:, at : at + 128]
        first = jnp.max(jnp.where(low, v, -jnp.inf), axis=-1, keepdims=True)
        second = jnp.max(jnp.where(low, -jnp.inf, v), axis=-1, keepdims=True)
        found.append(jnp.where(low, first, second))
    return jnp.concatenate(found, axis=1)


def attention(grouped, wqkv_ref, wo_ref, mask_ref, proj, context, emit):
    mask = mask_ref[...]
    for half in range(2):
        x = grouped[8 * half : 8 * half + 8].reshape(512, CHANS).astype(F32)
        proj[...] = mm(layer_norm(x), wqkv_ref[...]).astype(BF16)
        for g in range(8):
            rows = slice(64 * g, 64 * g + 64)
            for at in range(0, CHANS, 128):
                query = proj[rows, at : at + 128]
                keys = jnp.concatenate([proj[rows, CHANS + at : CHANS + at + 128]] * 4, axis=0) * mask
                values = jnp.concatenate([proj[rows, 2 * CHANS + at : 2 * CHANS + at + 128]] * 4, axis=0) * mask
                scores = mm_nt(query, keys)
                weights = jnp.exp2((scores - segment_max(scores)) * SCALE_LOG2).astype(BF16)
                both = mm(weights, jnp.concatenate([values, mask], axis=1))
                context[rows, at : at + 128] = (both[:, :128] / both[:, 128:]).astype(BF16)
        emit(half, x + mm(context[...], wo_ref[...]))


def grid_kernel(x_ref, wqkv_ref, wo_ref, turn_ref, mask_ref, *rest):
    out_ref, grouped, proj, context = rest[-4:]
    for t in range(4):
        moved = mm(turn_ref[...], x_ref[16 * t : 16 * t + 16].reshape(256, CHANS))
        grouped[:, 16 * t : 16 * t + 16] = moved.astype(BF16).reshape(16, 16, CHANS)

    def emit(half, rows):
        grouped[8 * half : 8 * half + 8] = rows.astype(BF16).reshape(8, 64, CHANS)

    attention(grouped, wqkv_ref, wo_ref, mask_ref, proj, context, emit)
    for t in range(4):
        moved = mm(turn_ref[...], grouped[:, 16 * t : 16 * t + 16].reshape(256, CHANS))
        out_ref[8 * t : 8 * t + 8, 0] = moved.astype(BF16).reshape(8, 2, 16, CHANS)


def head_mask():
    return jnp.asarray(np.arange(256)[:, None] // 64 == np.arange(128)[None] // HEAD, BF16)


def attention_scratch():
    return [
        pltpu.VMEM((16, 64, CHANS), BF16),
        pltpu.VMEM((512, 3 * CHANS), BF16),
        pltpu.VMEM((512, CHANS), BF16),
    ]


def grid_attention(part, x, qkv, out_proj, earlier):
    shape = (32, 2, 2, 16, CHANS)
    kept = [] if earlier is None else [earlier]
    return pl.pallas_call(
        grid_kernel,
        grid=(1,),
        in_specs=[
            whole((64, 16, CHANS)),
            whole((CHANS, 3 * CHANS)),
            whole((CHANS, CHANS)),
            whole((256, 256)),
            whole((256, 128)),
            *[pl.BlockSpec(memory_space=pl.ANY) for _ in kept],
        ],
        out_specs=pl.BlockSpec((32, 1, 2, 16, CHANS), lambda s: (0, part, 0, 0, 0)),
        out_shape=jax.ShapeDtypeStruct(shape, BF16),
        scratch_shapes=attention_scratch(),
        input_output_aliases={5: 0} if kept else {},
        compiler_params=params(),
        cost_estimate=pl.CostEstimate(
            flops=8 * 1024 * CHANS * CHANS, bytes_accessed=4 * 2**20, transcendentals=2**20
        ),
        name="grid_attention",
    )(x, qkv, out_proj, permutation((16, 16), (1, 0)), head_mask(), *kept)


def local_kernel(
    part, x_ref, prev_ref, next_ref, top_ref, bot_ref, left_ref, right_ref, we_ref, dw_ref, wp_ref, wqkv_ref, wo_ref,
    spread_ref, turn_ref, mask_ref, out_ref, normed, pad, rim, spatial, acc, grouped, proj, context,
):
    step = pl.program_id(0)

    @pl.when(step == 0)
    def _():
        for pair in range(4):
            moved = mm(spread_ref[...], x_ref[:, 2 * pair : 2 * pair + 2].reshape(256, CHANS))
            acc[256 * pair : 256 * pair + 256] = moved
            normed[128 + 256 * pair : 384 + 256 * pair] = layer_norm(moved)
        if part == 0:
            before, after = (top_ref[...], prev_ref[0, 0]), (next_ref[0, 0], next_ref[1, 0])
        else:
            before, after = (prev_ref[0, 0], prev_ref[1, 0]), (next_ref[1, 0], bot_ref[...])
        edges = jnp.concatenate([before[0], after[0], before[1], after[1]], axis=0)
        moved = layer_norm(mm(spread_ref[...], edges))
        normed[0:128] = moved[0:128]
        normed[1152:1280] = moved[128:256]
        normed[1280:1328] = layer_norm(left_ref[...].astype(F32))
        normed[1328:1376] = layer_norm(right_ref[...].astype(F32))

    for at in range(0, CB, 256):
        hidden = gelu(mm(normed[...], we_ref[:, at : at + 256])).astype(BF16)
        pad[:, 1:9, :, at : at + 256] = hidden[:1280].reshape(10, 8, 16, 256)
        rim[:, at : at + 256] = hidden[1280:].astype(F32)
    sub = lax.broadcasted_iota(jnp.int32, (8, CB), 0)
    for row in range(10):
        at = 8 * part + row
        last = pad[row, 8].astype(F32)
        first = pad[row, 1].astype(F32)
        west, east = [], []
        for b in range(2):
            turned = pltpu.roll(last[8 * b : 8 * b + 8], 1, 0)
            west.append(jnp.where(sub == 0, rim[at + 16 * b : at + 16 * b + 1], turned))
            turned = pltpu.roll(first[8 * b : 8 * b + 8], 7, 0)
            east.append(jnp.where(sub == 7, rim[at + 48 + 16 * b : at + 48 + 16 * b + 1], turned))
        pad[row, 0] = jnp.concatenate(west, axis=0).astype(BF16)
        pad[row, 9] = jnp.concatenate(east, axis=0).astype(BF16)

    taps = [[jnp.broadcast_to(dw_ref[a, b : b + 1].astype(BF16), (16, CB)) for b in range(3)] for a in range(3)]
    for pair in range(4):
        for i in (2 * pair, 2 * pair + 1):
            for j in range(8):
                sums = [
                    pad[i + a, j] * taps[a][0] + pad[i + a, j + 1] * taps[a][1] + pad[i + a, j + 2] * taps[a][2]
                    for a in range(3)
                ]
                total = sums[0] + sums[1] + sums[2]
                spatial[i, j] = gelu(total.astype(F32)).astype(BF16)
        rows = slice(256 * pair, 256 * pair + 256)
        acc[rows] += mm(spatial[2 * pair : 2 * pair + 2].reshape(256, CB), wp_ref[...])

    @pl.when(step == WIDE // CB - 1)
    def _():
        for pair in range(4):
            mixed = acc[256 * pair : 256 * pair + 256].astype(BF16)
            grouped[:, 16 * pair : 16 * pair + 16] = mm(turn_ref[...], mixed).astype(BF16).reshape(16, 16, CHANS)

        def emit(half, rows):
            rows = rows.reshape(4, 2, 8, 8, CHANS)
            for i in range(8):
                out_ref[i, :, half] = rows[:, :, i].reshape(4, 16, CHANS).astype(BF16)

        attention(grouped, wqkv_ref, wo_ref, mask_ref, proj, context, emit)


def local_part(part, field, rims, w_expand, dw_kernel, w_project, qkv, out_proj):
    rows = field.reshape(2, 16, 64, CHANS)

    def edge(at):
        return pl.BlockSpec((2, 1, 64, CHANS), lambda s: (0, at, 0, 0))

    return pl.pallas_call(
        functools.partial(local_kernel, part),
        grid=(WIDE // CB,),
        in_specs=[
            pl.BlockSpec((2, 8, 64, CHANS), lambda s: (0, part, 0, 0)),
            edge((15, 7)[part]),
            edge((8, 0)[part]),
            whole((64, CHANS)),
            whole((64, CHANS)),
            whole((48, CHANS)),
            whole((48, CHANS)),
            pl.BlockSpec((CHANS, CB), lambda s: (0, s)),
            pl.BlockSpec((3, 3, CB), lambda s: (0, 0, s)),
            pl.BlockSpec((CB, CHANS), lambda s: (s, 0)),
            whole((CHANS, 3 * CHANS)),
            whole((CHANS, CHANS)),
            whole((256, 256)),
            whole((256, 256)),
            whole((256, 128)),
        ],
        out_specs=whole((8, 4, 2, 16, CHANS)),
        out_shape=jax.ShapeDtypeStruct((8, 4, 2, 16, CHANS), BF16),
        scratch_shapes=[
            pltpu.VMEM((1376, CHANS), BF16),
            pltpu.VMEM((10, 10, 16, CB), BF16),
            pltpu.VMEM((96, CB), F32),
            pltpu.VMEM((8, 8, 16, CB), BF16),
            pltpu.VMEM((1024, CHANS), F32),
            *attention_scratch(),
        ],
        compiler_params=params(),
        cost_estimate=pl.CostEstimate(
            flops=4 * 1024 * CHANS * WIDE, bytes_accessed=8 * 2**20, transcendentals=2048 * WIDE
        ),
        name="local_part",
    )(
        rows, rows, rows, *rims, w_expand, dw_kernel, w_project, qkv, out_proj,
        permutation((2, 2, 8, 8), (1, 3, 0, 2)), permutation((16, 16), (1, 0)), head_mask(),
    )


def exchange(blocks, groups):
    return lax.all_to_all(blocks, ("row", "col"), 0, 0, axis_index_groups=groups, tiled=True)


def on_device(field, w_expand, dw_kernel, w_project, qkv_block, out_block, qkv_grid, out_grid):
    n_row, n_col = lax.axis_size("row"), lax.axis_size("col")
    down = [(i, i + 1) for i in range(n_row - 1)]
    up = [(i + 1, i) for i in range(n_row - 1)]
    top = lax.ppermute(field[31], "row", down)
    bottom = lax.ppermute(field[0], "row", up)
    fill = jnp.zeros((14, CHANS), BF16)

    def rim(column):
        return jnp.concatenate([top[column : column + 1], field[:, column], bottom[column : column + 1], fill], axis=0)

    left = lax.ppermute(rim(63), "col", [(i, i + 1) for i in range(n_col - 1)])
    right = lax.ppermute(rim(0), "col", [(i + 1, i) for i in range(n_col - 1)])
    rims = (top, bottom, left, right)
    groups = [[32 * row + 4 * j + c for row in range(n_row) for j in range(8)] for c in range(4)]
    gathered = []
    for part in range(2):
        blocked = local_part(part, field, rims, w_expand, dw_kernel, w_project, qkv_block, out_block)
        gathered.append(exchange(blocked.reshape(32, 2, 16, CHANS), groups).reshape(64, 16, CHANS))
    attended = None
    for part in range(2):
        attended = grid_attention(part, gathered[part], qkv_grid, out_grid, attended)
    home = exchange(attended, groups).reshape(8, 4, 2, 2, 16, CHANS)
    return home.transpose(3, 2, 0, 1, 4, 5).reshape(32, 64, CHANS)


def solution(mesh):
    placed = (P("row", "col", None), P(), P(), P(), P(), P(), P(), P())
    return jax.shard_map(
        on_device, mesh=mesh, in_specs=placed, out_specs=P("row", "col", None), check_vma=False
    )
```

```python
import functools

import jax
import jax.numpy as jnp
import numpy as np
from jax import lax
from jax.experimental import pallas as pl
from jax.experimental.pallas import tpu as pltpu
from jax.sharding import PartitionSpec as P

BF16 = jnp.bfloat16
F32 = jnp.float32
HEAD = 32
CHANS = 512
WIDE = 2048
CB = 1024
BLOCKS = WIDE // CB
VMEM_LIMIT = 36 * 2**20
SCALE_LOG2 = float(HEAD**-0.5 * np.log2(np.e))


def layer_norm(v):
    mean = jnp.mean(v, axis=-1, keepdims=True)
    cent = v - mean
    var = jnp.mean(cent * cent, axis=-1, keepdims=True)
    return (cent * lax.rsqrt(var + 1e-05)).astype(BF16)


def gelu(v):
    half = 0.5 * v
    return half + half * lax.erf(v * 0.7071067811865476)


def mm(a, b):
    return lax.dot_general(a, b, (((1,), (0,)), ((), ())), preferred_element_type=F32)


def mm_nt(a, b):
    return lax.dot_general(a, b, (((1,), (1,)), ((), ())), preferred_element_type=F32)


def ones_where(shape, holds):
    row = lax.broadcasted_iota(jnp.int32, shape, 0)
    column = lax.broadcasted_iota(jnp.int32, shape, 1)
    return jnp.where(holds(row, column), 1.0, 0.0).astype(BF16)


def spread_matrix():
    return ones_where(
        (256, 256),
        lambda r, c: c == ((r >> 3) & 1) * 128 + (r >> 7) * 64 + (r & 7) * 8 + ((r >> 4) & 7),
    )


def turn_matrix():
    return ones_where((256, 256), lambda r, c: c == (r & 15) * 16 + (r >> 4))


def head_mask():
    return ones_where((256, 128), lambda r, c: (r >> 6) == (c >> 5))


def in_vmem():
    return pl.BlockSpec(memory_space=pltpu.VMEM)


def in_hbm(count):
    return [pl.BlockSpec(memory_space=pltpu.HBM)] * count


def kept_in_hbm(*arrays):
    return [pltpu.with_memory_space_constraint(a, pltpu.HBM) for a in arrays]


def fetch(sems, *pairs):
    copies = [pltpu.make_async_copy(source, to, sems.at[at]) for at, (source, to) in enumerate(pairs)]
    for copy in copies:
        copy.start()
    return copies


def params():
    return pltpu.CompilerParams(vmem_limit_bytes=VMEM_LIMIT)


def segment_max(scores):
    low = lax.broadcasted_iota(jnp.int32, (1, 128), 1) < 64
    found = []
    for at in range(0, scores.shape[1], 128):
        v = scores[:, at : at + 128]
        first = jnp.max(jnp.where(low, v, -jnp.inf), axis=-1, keepdims=True)
        second = jnp.max(jnp.where(low, -jnp.inf, v), axis=-1, keepdims=True)
        found.append(jnp.where(low, first, second))
    return jnp.concatenate(found, axis=1)


def attention(grouped, wqkv_ref, wo_ref, mask_ref, proj, context, emit):
    mask = mask_ref[...]
    for half in range(2):
        x = grouped[8 * half : 8 * half + 8].reshape(512, CHANS).astype(F32)
        proj[...] = mm(layer_norm(x), wqkv_ref[...]).astype(BF16)
        for g in range(8):
            rows = slice(64 * g, 64 * g + 64)
            for at in range(0, CHANS, 128):
                query = proj[rows, at : at + 128]
                keys = jnp.concatenate([proj[rows, CHANS + at : CHANS + at + 128]] * 4, axis=0) * mask
                values = jnp.concatenate([proj[rows, 2 * CHANS + at : 2 * CHANS + at + 128]] * 4, axis=0) * mask
                scores = mm_nt(query, keys)
                weights = jnp.exp2((scores - segment_max(scores)) * SCALE_LOG2).astype(BF16)
                both = mm(weights, jnp.concatenate([values, mask], axis=1))
                context[rows, at : at + 128] = (both[:, :128] / both[:, 128:]).astype(BF16)
        emit(half, x + mm(context[...], wo_ref[...]))


def grid_kernel(part, x_ref, wqkv_hbm, wo_hbm, *rest):
    out_ref, grouped, proj, context, turn_ref, mask_ref, wqkv_ref, wo_ref, sems = rest[-9:]
    copies = fetch(sems, (wqkv_hbm, wqkv_ref), (wo_hbm, wo_ref))
    turn_ref[...] = turn_matrix()
    mask_ref[...] = head_mask()
    for t in range(4):
        moved = mm(turn_ref[...], x_ref[16 * t : 16 * t + 16].reshape(256, CHANS))
        grouped[:, 16 * t : 16 * t + 16] = moved.astype(BF16).reshape(16, 16, CHANS)
    for copy in copies:
        copy.wait()

    def emit(half, rows):
        grouped[8 * half : 8 * half + 8] = rows.astype(BF16).reshape(8, 64, CHANS)

    attention(grouped, wqkv_ref, wo_ref, mask_ref, proj, context, emit)
    for t in range(4):
        moved = mm(turn_ref[...], grouped[:, 16 * t : 16 * t + 16].reshape(256, CHANS))
        out_ref[8 * t : 8 * t + 8, part] = moved.astype(BF16).reshape(8, 2, 16, CHANS)


def attention_scratch():
    return [
        pltpu.VMEM((16, 64, CHANS), BF16),
        pltpu.VMEM((512, 3 * CHANS), BF16),
        pltpu.VMEM((512, CHANS), BF16),
        pltpu.VMEM((256, 256), BF16),
        pltpu.VMEM((256, 128), BF16),
        pltpu.VMEM((CHANS, 3 * CHANS), BF16),
        pltpu.VMEM((CHANS, CHANS), BF16),
    ]


def grid_attention(part, x, qkv, out_proj, earlier):
    shape = (32, 2, 2, 16, CHANS)
    kept = [] if earlier is None else [earlier]
    return pl.pallas_call(
        functools.partial(grid_kernel, part),
        in_specs=[in_vmem(), *in_hbm(2), *[in_vmem() for _ in kept]],
        out_specs=in_vmem(),
        out_shape=jax.ShapeDtypeStruct(shape, BF16),
        scratch_shapes=[*attention_scratch(), pltpu.SemaphoreType.DMA((2,))],
        input_output_aliases={3: 0} if kept else {},
        compiler_params=params(),
        cost_estimate=pl.CostEstimate(
            flops=8 * 1024 * CHANS * CHANS, bytes_accessed=4 * 2**20, transcendentals=2**20
        ),
        name="grid_attention",
    )(x, *kept_in_hbm(qkv, out_proj), *kept)


def local_kernel(
    part, top_ref, bot_ref, left_ref, right_ref, x_hbm, we_hbm, dw_hbm, wp_hbm, wqkv_hbm, wo_hbm, out_ref, x_ref, edge_ref, spread_ref, we_ref, dw_ref, wp_ref, normed, pad, rim, spatial, acc,
    grouped, proj, context, turn_ref, mask_ref, wqkv_ref, wo_ref, sems,
):
    if part == 0:
        edges = [(x_hbm.at[0, 15], edge_ref.at[2]), (x_hbm.at[0, 8], edge_ref.at[1]), (x_hbm.at[1, 8], edge_ref.at[3])]
    else:
        edges = [(x_hbm.at[0, 7], edge_ref.at[0]), (x_hbm.at[1, 7], edge_ref.at[2]), (x_hbm.at[1, 0], edge_ref.at[1])]
    blocks = [slice(CB * s, CB * s + CB) for s in range(BLOCKS)]
    copies = fetch(
        sems,
        (x_hbm.at[:, 8 * part : 8 * part + 8], x_ref),
        *edges,
        *[(we_hbm.at[:, lanes], we_ref.at[s]) for s, lanes in enumerate(blocks)],
        (dw_hbm, dw_ref),
        *[(wp_hbm.at[lanes], wp_ref.at[s]) for s, lanes in enumerate(blocks)],
        (wqkv_hbm, wqkv_ref),
        (wo_hbm, wo_ref),
    )
    if part == 0:
        edge_ref[0] = top_ref[...]
    else:
        edge_ref[3] = bot_ref[...]
    normed[1280:1328] = layer_norm(left_ref[...].astype(F32))
    normed[1328:1376] = layer_norm(right_ref[...].astype(F32))
    spread_ref[...] = spread_matrix()
    turn_ref[...] = turn_matrix()
    mask_ref[...] = head_mask()
    for copy in copies[:4]:
        copy.wait()
    for pair in range(4):
        moved = mm(spread_ref[...], x_ref[:, 2 * pair : 2 * pair + 2].reshape(256, CHANS))
        acc[256 * pair : 256 * pair + 256] = moved
        normed[128 + 256 * pair : 384 + 256 * pair] = layer_norm(moved)
    moved = layer_norm(mm(spread_ref[...], edge_ref[...].reshape(256, CHANS)))
    normed[0:128] = moved[0:128]
    normed[1152:1280] = moved[128:256]

    sub = lax.broadcasted_iota(jnp.int32, (8, CB), 0)
    for s, lanes in enumerate(blocks):
        copies[4 + s].wait()
        for at in range(0, CB, 256):
            hidden = gelu(mm(normed[...], we_ref[s, :, at : at + 256])).astype(BF16)
            pad[:, 1:9, :, at : at + 256] = hidden[:1280].reshape(10, 8, 16, 256)
            rim[:, at : at + 256] = hidden[1280:].astype(F32)
        for row in range(10):
            at = 8 * part + row
            last = pad[row, 8].astype(F32)
            first = pad[row, 1].astype(F32)
            west, east = [], []
            for b in range(2):
                turned = pltpu.roll(last[8 * b : 8 * b + 8], 1, 0)
                west.append(jnp.where(sub == 0, rim[at + 16 * b : at + 16 * b + 1], turned))
                turned = pltpu.roll(first[8 * b : 8 * b + 8], 7, 0)
                east.append(jnp.where(sub == 7, rim[at + 48 + 16 * b : at + 48 + 16 * b + 1], turned))
            pad[row, 0] = jnp.concatenate(west, axis=0).astype(BF16)
            pad[row, 9] = jnp.concatenate(east, axis=0).astype(BF16)

        if s == 0:
            copies[4 + BLOCKS].wait()
        copies[5 + BLOCKS + s].wait()
        taps = [[jnp.broadcast_to(dw_ref[a, b : b + 1, lanes].astype(BF16), (16, CB)) for b in range(3)] for a in range(3)]
        for pair in range(4):
            for i in (2 * pair, 2 * pair + 1):
                for j in range(8):
                    sums = [
                        pad[i + a, j] * taps[a][0] + pad[i + a, j + 1] * taps[a][1] + pad[i + a, j + 2] * taps[a][2]
                        for a in range(3)
                    ]
                    total = sums[0] + sums[1] + sums[2]
                    spatial[i, j] = gelu(total.astype(F32)).astype(BF16)
            rows = slice(256 * pair, 256 * pair + 256)
            acc[rows] += mm(spatial[2 * pair : 2 * pair + 2].reshape(256, CB), wp_ref[s])

    for copy in copies[5 + 2 * BLOCKS :]:
        copy.wait()
    for pair in range(4):
        mixed = acc[256 * pair : 256 * pair + 256].astype(BF16)
        grouped[:, 16 * pair : 16 * pair + 16] = mm(turn_ref[...], mixed).astype(BF16).reshape(16, 16, CHANS)

    def emit(half, rows):
        rows = rows.reshape(4, 2, 8, 8, CHANS)
        for i in range(8):
            out_ref[i, :, half] = rows[:, :, i].reshape(4, 16, CHANS).astype(BF16)

    attention(grouped, wqkv_ref, wo_ref, mask_ref, proj, context, emit)


def local_part(part, field, rims, w_expand, dw_kernel, w_project, qkv, out_proj):
    return pl.pallas_call(
        functools.partial(local_kernel, part),
        in_specs=[*[in_vmem() for _ in rims], *in_hbm(6)],
        out_specs=in_vmem(),
        out_shape=jax.ShapeDtypeStruct((8, 4, 2, 16, CHANS), BF16),
        scratch_shapes=[
            pltpu.VMEM((2, 8, 64, CHANS), BF16),
            pltpu.VMEM((4, 64, CHANS), BF16),
            pltpu.VMEM((256, 256), BF16),
            pltpu.VMEM((BLOCKS, CHANS, CB), BF16),
            pltpu.VMEM((3, 3, WIDE), F32),
            pltpu.VMEM((BLOCKS, CB, CHANS), BF16),
            pltpu.VMEM((1376, CHANS), BF16),
            pltpu.VMEM((10, 10, 16, CB), BF16),
            pltpu.VMEM((96, CB), F32),
            pltpu.VMEM((8, 8, 16, CB), BF16),
            pltpu.VMEM((1024, CHANS), F32),
            *attention_scratch(),
            pltpu.SemaphoreType.DMA((7 + 2 * BLOCKS,)),
        ],
        compiler_params=params(),
        cost_estimate=pl.CostEstimate(
            flops=4 * 1024 * CHANS * WIDE, bytes_accessed=8 * 2**20, transcendentals=2048 * WIDE
        ),
        name="local_part",
    )(
        *rims,
        *kept_in_hbm(field.reshape(2, 16, 64, CHANS), w_expand, dw_kernel, w_project, qkv, out_proj),
    )


def exchange(blocks, groups):
    return lax.all_to_all(blocks, ("row", "col"), 0, 0, axis_index_groups=groups, tiled=True)


def on_device(field, w_expand, dw_kernel, w_project, qkv_block, out_block, qkv_grid, out_grid):
    n_row, n_col = lax.axis_size("row"), lax.axis_size("col")
    down = [(i, i + 1) for i in range(n_row - 1)]
    up = [(i + 1, i) for i in range(n_row - 1)]
    top = lax.ppermute(field[31], "row", down)
    bottom = lax.ppermute(field[0], "row", up)
    fill = jnp.zeros((14, CHANS), BF16)

    def rim(column):
        return jnp.concatenate([top[column : column + 1], field[:, column], bottom[column : column + 1], fill], axis=0)

    left = lax.ppermute(rim(63), "col", [(i, i + 1) for i in range(n_col - 1)])
    right = lax.ppermute(rim(0), "col", [(i + 1, i) for i in range(n_col - 1)])
    rims = (top, bottom, left, right)
    groups = [[32 * row + 4 * j + c for row in range(n_row) for j in range(8)] for c in range(4)]
    gathered = []
    for part in range(2):
        blocked = local_part(part, field, rims, w_expand, dw_kernel, w_project, qkv_block, out_block)
        gathered.append(exchange(blocked.reshape(32, 2, 16, CHANS), groups).reshape(64, 16, CHANS))
    attended = None
    for part in range(2):
        attended = grid_attention(part, gathered[part], qkv_grid, out_grid, attended)
    home = exchange(attended, groups).reshape(8, 4, 2, 2, 16, CHANS)
    return home.transpose(3, 2, 0, 1, 4, 5).reshape(32, 64, CHANS)


def solution(mesh):
    placed = (P("row", "col", None), P(), P(), P(), P(), P(), P(), P())
    return jax.shard_map(
        on_device, mesh=mesh, in_specs=placed, out_specs=P("row", "col", None), check_vma=False
    )
```

```python
import functools

import jax
import jax.numpy as jnp
import numpy as np
from jax import lax
from jax.experimental import pallas as pl
from jax.experimental.pallas import tpu as pltpu
from jax.sharding import PartitionSpec as P

BF16 = jnp.bfloat16
F32 = jnp.float32
HEAD = 32
CHANS = 512
WIDE = 2048
CB = 1024
BLOCKS = WIDE // CB
PAIRS = 4
VMEM_LIMIT = 28 * 2**20
SCALE_LOG2 = float(HEAD**-0.5 * np.log2(np.e))


def layer_norm(v):
    mean = jnp.mean(v, axis=-1, keepdims=True)
    cent = v - mean
    var = jnp.mean(cent * cent, axis=-1, keepdims=True)
    return (cent * lax.rsqrt(var + 1e-05)).astype(BF16)


def gelu(v):
    half = 0.5 * v
    return half + half * lax.erf(v * 0.7071067811865476)


def mm(a, b):
    return lax.dot_general(a, b, (((1,), (0,)), ((), ())), preferred_element_type=F32)


def mm_nt(a, b):
    return lax.dot_general(a, b, (((1,), (1,)), ((), ())), preferred_element_type=F32)


def ones_where(shape, holds):
    row = lax.broadcasted_iota(jnp.int32, shape, 0)
    column = lax.broadcasted_iota(jnp.int32, shape, 1)
    return jnp.where(holds(row, column), 1.0, 0.0).astype(BF16)


def spread_matrix():
    return ones_where(
        (256, 256),
        lambda r, c: c == ((r >> 3) & 1) * 128 + (r >> 7) * 64 + (r & 7) * 8 + ((r >> 4) & 7),
    )


def turn_matrix():
    return ones_where((256, 256), lambda r, c: c == (r & 15) * 16 + (r >> 4))


def edge_matrix(part):
    def holds(r, c):
        j, b, q = r >> 4, (r >> 3) & 1, r & 7
        own = c == j * 16 + 8 * part + q
        rim = c == 128 + q * 8 + j
        return (own & (b == 1 - part)) | (rim & (b == part))

    return ones_where((128, 192), holds)


def head_mask():
    return ones_where((256, 128), lambda r, c: (r >> 6) == (c >> 5))


def in_vmem():
    return pl.BlockSpec(memory_space=pltpu.VMEM)


def in_hbm(count):
    return [pl.BlockSpec(memory_space=pltpu.HBM)] * count


def kept_in_hbm(*arrays):
    return [pltpu.with_memory_space_constraint(a, pltpu.HBM) for a in arrays]


def fetch(sems, *pairs):
    copies = [pltpu.make_async_copy(source, to, sems.at[at]) for at, (source, to) in enumerate(pairs)]
    for copy in copies:
        copy.start()
    return copies


def params():
    return pltpu.CompilerParams(vmem_limit_bytes=VMEM_LIMIT)


def segment_max(scores):
    low = lax.broadcasted_iota(jnp.int32, (1, 128), 1) < 64
    found = []
    for at in range(0, scores.shape[1], 128):
        v = scores[:, at : at + 128]
        first = jnp.max(jnp.where(low, v, -jnp.inf), axis=-1, keepdims=True)
        second = jnp.max(jnp.where(low, -jnp.inf, v), axis=-1, keepdims=True)
        found.append(jnp.where(low, first, second))
    return jnp.concatenate(found, axis=1)


def attention(grouped, wqkv_ref, wo_ref, mask_ref, proj, context, emit):
    mask = mask_ref[...]

    def one(half, carry):
        x = grouped[pl.ds(8 * half, 8)].reshape(512, CHANS).astype(F32)
        proj[...] = mm(layer_norm(x), wqkv_ref[...]).astype(BF16)
        for g in range(8):
            rows = slice(64 * g, 64 * g + 64)
            for at in range(0, CHANS, 128):
                query = proj[rows, at : at + 128]
                keys = jnp.concatenate([proj[rows, CHANS + at : CHANS + at + 128]] * 4, axis=0) * mask
                values = jnp.concatenate([proj[rows, 2 * CHANS + at : 2 * CHANS + at + 128]] * 4, axis=0) * mask
                scores = mm_nt(query, keys)
                weights = jnp.exp2((scores - segment_max(scores)) * SCALE_LOG2).astype(BF16)
                both = mm(weights, jnp.concatenate([values, mask], axis=1))
                context[rows, at : at + 128] = (both[:, :128] / both[:, 128:]).astype(BF16)
        emit(half, x + mm(context[...], wo_ref[...]))
        return carry

    lax.fori_loop(0, 2, one, 0, unroll=2)


def grid_kernel(x_ref, wqkv_ref, wo_ref, *rest):
    out_ref, grouped, proj, context, turn_ref, mask_ref = rest[-6:]
    turn_ref[...] = turn_matrix()
    mask_ref[...] = head_mask()
    for t in range(4):
        moved = mm(turn_ref[...], x_ref[16 * t : 16 * t + 16].reshape(256, CHANS))
        grouped[:, 16 * t : 16 * t + 16] = moved.astype(BF16).reshape(16, 16, CHANS)

    def emit(half, rows):
        grouped[pl.ds(8 * half, 8)] = rows.astype(BF16).reshape(8, 64, CHANS)

    attention(grouped, wqkv_ref, wo_ref, mask_ref, proj, context, emit)
    for t in range(4):
        moved = mm(turn_ref[...], grouped[:, 16 * t : 16 * t + 16].reshape(256, CHANS))
        moved = moved.astype(BF16).reshape(8, 2, 16, CHANS)
        if len(rest) == 6:
            out_ref[8 * t : 8 * t + 8] = moved
        else:
            out_ref[8 * t : 8 * t + 8, 1] = moved
    if len(rest) > 6:
        out_ref[:, 0] = rest[0][...]


def attention_scratch():
    return [
        pltpu.VMEM((16, 64, CHANS), BF16),
        pltpu.VMEM((512, 3 * CHANS), BF16),
        pltpu.VMEM((512, CHANS), BF16),
        pltpu.VMEM((256, 256), BF16),
        pltpu.VMEM((256, 128), BF16),
    ]


def grid_attention(x, qkv, out_proj, *earlier):
    shape = (32, 2, 2, 16, CHANS) if earlier else (32, 2, 16, CHANS)
    return pl.pallas_call(
        grid_kernel,
        in_specs=[in_vmem() for _ in range(3 + len(earlier))],
        out_specs=in_vmem(),
        out_shape=jax.ShapeDtypeStruct(shape, BF16),
        scratch_shapes=attention_scratch(),
        compiler_params=params(),
        cost_estimate=pl.CostEstimate(
            flops=8 * 1024 * CHANS * CHANS, bytes_accessed=4 * 2**20, transcendentals=2**20
        ),
        name="grid_attention",
    )(x, qkv, out_proj, *earlier)


def prepare_kernel(x_hbm, we_hbm, dw_hbm, wp_hbm, *rest):
    small_hbm, (_, normed_ref, xp_ref, we_ref, dw_ref, wp_ref), small, (x_ref, spread_ref, sems) = (
        rest[0:4], rest[4:10], rest[10:14], rest[14:],
    )
    rows = [
        fetch(sems.at[0, pl.ds(k, 1)], (x_hbm.at[:, 8 * k : 8 * k + 8], x_ref.at[:, 8 * k : 8 * k + 8]))[0]
        for k in range(2)
    ]
    copies = fetch(
        sems.at[1],
        *[(we_hbm.at[:, CB * s : CB * s + CB], we_ref.at[s]) for s in range(BLOCKS)],
        *[(dw_hbm.at[:, :, CB * s : CB * s + CB], dw_ref.at[s]) for s in range(BLOCKS)],
        *[(wp_hbm.at[CB * s : CB * s + CB], wp_ref.at[s]) for s in range(BLOCKS)],
        *zip(small_hbm, small),
    )
    spread_ref[...] = spread_matrix()
    for pair in range(8):
        if pair % 4 == 0:
            rows[pair // 4].wait()
        moved = mm(spread_ref[...], x_ref[:, 2 * pair : 2 * pair + 2].reshape(256, CHANS))
        xp_ref[256 * pair : 256 * pair + 256] = moved.astype(BF16)
        normed_ref[256 * pair : 256 * pair + 256] = layer_norm(moved)
    for copy in copies:
        copy.wait()


def prepare(after, field, w_expand, dw_kernel, w_project, *small):
    out_shape = [
        jax.ShapeDtypeStruct((2048, CHANS), BF16),
        jax.ShapeDtypeStruct((2048, CHANS), BF16),
        jax.ShapeDtypeStruct((BLOCKS, CHANS, CB), BF16),
        jax.ShapeDtypeStruct((BLOCKS, 3, 3, CB), F32),
        jax.ShapeDtypeStruct((BLOCKS, CB, CHANS), BF16),
        *[jax.ShapeDtypeStruct(a.shape, BF16) for a in small],
    ]
    return pl.pallas_call(
        prepare_kernel,
        in_specs=[*in_hbm(8), pl.BlockSpec(memory_space=pl.ANY)],
        out_specs=[in_vmem() for _ in out_shape],
        out_shape=out_shape,
        scratch_shapes=[
            pltpu.VMEM((2, 16, 64, CHANS), BF16),
            pltpu.VMEM((256, 256), BF16),
            pltpu.SemaphoreType.DMA((2, 4 + 3 * BLOCKS)),
        ],
        compiler_params=params(),
        cost_estimate=pl.CostEstimate(flops=10**10, bytes_accessed=16 * 2**20, transcendentals=0),
        name="prepare",
    )(*kept_in_hbm(field.reshape(2, 16, 64, CHANS), w_expand, dw_kernel, w_project, *small), after)


def local_kernel(
    part, rim_ref, left_ref, right_ref, normed_ref, xp_ref, we_ref, dw_ref, wp_ref, wqkv_ref, wo_ref, out_ref,
    outer, pad, rim, spatial, acc, grouped, proj, context, turn_ref, mask_ref,
):
    turn_ref[...] = turn_matrix()
    mask_ref[...] = head_mask()
    own = slice(1024 * part, 1024 * part + 1024)
    acc[...] = xp_ref[own].astype(F32)
    before, after = ((15, 8), (7, 0))[part]
    special = (before, after)[part]
    source = jnp.concatenate(
        [normed_ref[128 * special : 128 * special + 128], layer_norm(rim_ref[...].astype(F32))], axis=0
    )
    mixed_edge = mm(edge_matrix(part), source).astype(BF16)
    if part == 0:
        outer[0:128] = mixed_edge
        outer[128:256] = normed_ref[128 * after : 128 * after + 128]
    else:
        outer[0:128] = normed_ref[128 * before : 128 * before + 128]
        outer[128:256] = mixed_edge
    outer[256:304] = layer_norm(left_ref[...].astype(F32))
    outer[304:352] = layer_norm(right_ref[...].astype(F32))

    sub = lax.broadcasted_iota(jnp.int32, (8, CB), 0)

    def block(s, carry):
        for at in range(0, CB, 256):
            made = gelu(mm(normed_ref[own], we_ref[s, :, at : at + 256])).astype(BF16)
            pad[1:9, 1:9, :, at : at + 256] = made.reshape(8, 8, 16, 256)
            made = gelu(mm(outer[...], we_ref[s, :, at : at + 256])).astype(BF16)
            pad[0, 1:9, :, at : at + 256] = made[0:128].reshape(8, 16, 256)
            pad[9, 1:9, :, at : at + 256] = made[128:256].reshape(8, 16, 256)
            rim[:, at : at + 256] = made[256:352].astype(F32)
        for row in range(10):
            at = 8 * part + row
            last = pad[row, 8].astype(F32)
            first = pad[row, 1].astype(F32)
            west, east = [], []
            for b in range(2):
                turned = pltpu.roll(last[8 * b : 8 * b + 8], 1, 0)
                west.append(jnp.where(sub == 0, rim[at + 16 * b : at + 16 * b + 1], turned))
                turned = pltpu.roll(first[8 * b : 8 * b + 8], 7, 0)
                east.append(jnp.where(sub == 7, rim[at + 48 + 16 * b : at + 48 + 16 * b + 1], turned))
            pad[row, 0] = jnp.concatenate(west, axis=0).astype(BF16)
            pad[row, 9] = jnp.concatenate(east, axis=0).astype(BF16)

        taps = [[jnp.broadcast_to(dw_ref[s, a, b : b + 1].astype(BF16), (16, CB)) for b in range(3)] for a in range(3)]

        def pair_of_rows(pair, carry):
            for i in range(2):
                for j in range(8):
                    sums = [
                        pad[2 * pair + i + a, j] * taps[a][0]
                        + pad[2 * pair + i + a, j + 1] * taps[a][1]
                        + pad[2 * pair + i + a, j + 2] * taps[a][2]
                        for a in range(3)
                    ]
                    total = sums[0] + sums[1] + sums[2]
                    spatial[2 * pair + i, j] = gelu(total.astype(F32)).astype(BF16)
            rows = pl.ds(pl.multiple_of(256 * pair, 256), 256)
            acc[rows] += mm(spatial[pl.ds(2 * pair, 2)].reshape(256, CB), wp_ref[s])
            return carry

        lax.fori_loop(0, 4, pair_of_rows, 0, unroll=PAIRS)
        return carry

    lax.fori_loop(0, BLOCKS, block, 0)
    for pair in range(4):
        mixed = acc[256 * pair : 256 * pair + 256].astype(BF16)
        grouped[:, 16 * pair : 16 * pair + 16] = mm(turn_ref[...], mixed).astype(BF16).reshape(16, 16, CHANS)

    def emit(half, rows):
        rows = rows.reshape(4, 2, 8, 8, CHANS)
        for i in range(8):
            out_ref[i, :, half] = rows[:, :, i].reshape(4, 16, CHANS).astype(BF16)

    attention(grouped, wqkv_ref, wo_ref, mask_ref, proj, context, emit)


def local_part(part, rims, prepared):
    top, bottom, left, right = rims
    operands = ((top, bottom)[part], left, right, *prepared)
    return pl.pallas_call(
        functools.partial(local_kernel, part),
        in_specs=[in_vmem() for _ in operands],
        out_specs=in_vmem(),
        out_shape=jax.ShapeDtypeStruct((8, 4, 2, 16, CHANS), BF16),
        scratch_shapes=[
            pltpu.VMEM((352, CHANS), BF16),
            pltpu.VMEM((10, 10, 16, CB), BF16),
            pltpu.VMEM((96, CB), F32),
            pltpu.VMEM((8, 8, 16, CB), BF16),
            pltpu.VMEM((1024, CHANS), F32),
            *attention_scratch(),
        ],
        compiler_params=params(),
        cost_estimate=pl.CostEstimate(
            flops=4 * 1024 * CHANS * WIDE, bytes_accessed=8 * 2**20, transcendentals=2048 * WIDE
        ),
        name="local_part",
    )(*operands)


def exchange(blocks, groups):
    return lax.all_to_all(blocks, ("row", "col"), 0, 0, axis_index_groups=groups, tiled=True)


def on_device(field, w_expand, dw_kernel, w_project, qkv_block, out_block, qkv_grid, out_grid):
    n_row, n_col = lax.axis_size("row"), lax.axis_size("col")
    down = [(i, i + 1) for i in range(n_row - 1)]
    up = [(i + 1, i) for i in range(n_row - 1)]
    top = lax.ppermute(field[31], "row", down)
    bottom = lax.ppermute(field[0], "row", up)
    fill = jnp.zeros((14, CHANS), BF16)

    def rim(column):
        return jnp.concatenate([top[column : column + 1], field[:, column], bottom[column : column + 1], fill], axis=0)

    east, west = rim(63), rim(0)
    left = lax.ppermute(east, "col", [(i, i + 1) for i in range(n_col - 1)])
    right = lax.ppermute(west, "col", [(i + 1, i) for i in range(n_col - 1)])
    *prepared, qkv_block, out_block, qkv_grid, out_grid = prepare(
        east, field, w_expand, dw_kernel, w_project, qkv_block, out_block, qkv_grid, out_grid
    )
    groups = [[32 * row + 4 * j + c for row in range(n_row) for j in range(8)] for c in range(4)]
    gathered = []
    for part in range(2):
        blocked = local_part(part, (top, bottom, left, right), (*prepared, qkv_block, out_block))
        gathered.append(exchange(blocked.reshape(32, 2, 16, CHANS), groups).reshape(64, 16, CHANS))
    attended = grid_attention(gathered[0], qkv_grid, out_grid)
    attended = grid_attention(gathered[1], qkv_grid, out_grid, attended)
    home = exchange(attended, groups).reshape(8, 4, 2, 2, 16, CHANS)
    return home.transpose(3, 2, 0, 1, 4, 5).reshape(32, 64, CHANS)


def solution(mesh):
    placed = (P("row", "col", None), P(), P(), P(), P(), P(), P(), P())
    return jax.shard_map(
        on_device, mesh=mesh, in_specs=placed, out_specs=P("row", "col", None), check_vma=False
    )
```

```python
import functools

import jax
import jax.numpy as jnp
import numpy as np
from jax import lax
from jax.experimental import pallas as pl
from jax.experimental.pallas import tpu as pltpu
from jax.sharding import PartitionSpec as P

BF16 = jnp.bfloat16
F32 = jnp.float32
HEAD = 32
CHANS = 512
WIDE = 2048
CB = 1024
BLOCKS = WIDE // CB
PAIRS = 4
PIECES = CB // 256
VMEM_LIMIT = 36 * 2**20
SCALE_LOG2 = float(HEAD**-0.5 * np.log2(np.e))


def layer_norm(v):
    mean = jnp.mean(v, axis=-1, keepdims=True)
    cent = v - mean
    var = jnp.mean(cent * cent, axis=-1, keepdims=True)
    return (cent * lax.rsqrt(var + 1e-05)).astype(BF16)


def gelu(v):
    half = 0.5 * v
    return half + half * lax.erf(v * 0.7071067811865476)


def mm(a, b):
    return lax.dot_general(a, b, (((1,), (0,)), ((), ())), preferred_element_type=F32)


def mm_nt(a, b):
    return lax.dot_general(a, b, (((1,), (1,)), ((), ())), preferred_element_type=F32)


def ones_where(shape, holds):
    row = lax.broadcasted_iota(jnp.int32, shape, 0)
    column = lax.broadcasted_iota(jnp.int32, shape, 1)
    return jnp.where(holds(row, column), 1.0, 0.0).astype(BF16)


def spread_matrix():
    return ones_where(
        (256, 256),
        lambda r, c: c == ((r >> 3) & 1) * 128 + (r >> 7) * 64 + (r & 7) * 8 + ((r >> 4) & 7),
    )


def turn_matrix():
    return ones_where((256, 256), lambda r, c: c == (r & 15) * 16 + (r >> 4))


def edge_matrix(part):
    def holds(r, c):
        j, b, q = r >> 4, (r >> 3) & 1, r & 7
        own = c == j * 16 + 8 * part + q
        rim = c == 128 + q * 8 + j
        return (own & (b == 1 - part)) | (rim & (b == part))

    return ones_where((128, 192), holds)


def head_mask():
    return ones_where((256, 128), lambda r, c: (r >> 6) == (c >> 5))


def in_vmem():
    return pl.BlockSpec(memory_space=pltpu.VMEM)


def in_hbm(count):
    return [pl.BlockSpec(memory_space=pltpu.HBM)] * count


def kept_in_hbm(*arrays):
    return [pltpu.with_memory_space_constraint(a, pltpu.HBM) for a in arrays]


def fetch(sems, *pairs):
    copies = [pltpu.make_async_copy(source, to, sems.at[at]) for at, (source, to) in enumerate(pairs)]
    for copy in copies:
        copy.start()
    return copies


def params():
    return pltpu.CompilerParams(vmem_limit_bytes=VMEM_LIMIT)


def segment_max(scores):
    low = lax.broadcasted_iota(jnp.int32, (1, 128), 1) < 64
    found = []
    for at in range(0, scores.shape[1], 128):
        v = scores[:, at : at + 128]
        first = jnp.max(jnp.where(low, v, -jnp.inf), axis=-1, keepdims=True)
        second = jnp.max(jnp.where(low, -jnp.inf, v), axis=-1, keepdims=True)
        found.append(jnp.where(low, first, second))
    return jnp.concatenate(found, axis=1)


def attention(grouped, wqkv_ref, wo_ref, mask_ref, proj, context, emit):
    mask = mask_ref[...]

    def one(half, carry):
        x = grouped[pl.ds(8 * half, 8)].reshape(512, CHANS).astype(F32)
        proj[...] = mm(layer_norm(x), wqkv_ref[...]).astype(BF16)
        for g in range(8):
            rows = slice(64 * g, 64 * g + 64)
            for at in range(0, CHANS, 128):
                query = proj[rows, at : at + 128]
                keys = jnp.concatenate([proj[rows, CHANS + at : CHANS + at + 128]] * 4, axis=0) * mask
                values = jnp.concatenate([proj[rows, 2 * CHANS + at : 2 * CHANS + at + 128]] * 4, axis=0) * mask
                scores = mm_nt(query, keys)
                weights = jnp.exp2((scores - segment_max(scores)) * SCALE_LOG2).astype(BF16)
                both = mm(weights, jnp.concatenate([values, mask], axis=1))
                context[rows, at : at + 128] = (both[:, :128] / both[:, 128:]).astype(BF16)
        emit(half, x + mm(context[...], wo_ref[...]))
        return carry

    lax.fori_loop(0, 2, one, 0, unroll=2)


def grid_kernel(x_ref, wqkv_hbm, wo_hbm, *rest):
    out_ref, grouped, proj, context, turn_ref, mask_ref, wqkv_ref, wo_ref, sems = rest[-9:]
    copies = fetch(sems, (wqkv_hbm, wqkv_ref), (wo_hbm, wo_ref))
    turn_ref[...] = turn_matrix()
    mask_ref[...] = head_mask()
    for t in range(4):
        moved = mm(turn_ref[...], x_ref[16 * t : 16 * t + 16].reshape(256, CHANS))
        grouped[:, 16 * t : 16 * t + 16] = moved.astype(BF16).reshape(16, 16, CHANS)

    def emit(half, rows):
        grouped[pl.ds(8 * half, 8)] = rows.astype(BF16).reshape(8, 64, CHANS)

    for copy in copies:
        copy.wait()
    attention(grouped, wqkv_ref, wo_ref, mask_ref, proj, context, emit)
    for t in range(4):
        moved = mm(turn_ref[...], grouped[:, 16 * t : 16 * t + 16].reshape(256, CHANS))
        moved = moved.astype(BF16).reshape(8, 2, 16, CHANS)
        if len(rest) == 9:
            out_ref[8 * t : 8 * t + 8] = moved
        else:
            out_ref[8 * t : 8 * t + 8, 1] = moved
    if len(rest) > 9:
        out_ref[:, 0] = rest[0][...]


def attention_scratch():
    return [
        pltpu.VMEM((16, 64, CHANS), BF16),
        pltpu.VMEM((512, 3 * CHANS), BF16),
        pltpu.VMEM((512, CHANS), BF16),
        pltpu.VMEM((256, 256), BF16),
        pltpu.VMEM((256, 128), BF16),
        pltpu.VMEM((CHANS, 3 * CHANS), BF16),
        pltpu.VMEM((CHANS, CHANS), BF16),
    ]


def grid_attention(x, qkv, out_proj, *earlier):
    shape = (32, 2, 2, 16, CHANS) if earlier else (32, 2, 16, CHANS)
    return pl.pallas_call(
        grid_kernel,
        in_specs=[in_vmem(), *in_hbm(2), *[in_vmem() for _ in earlier]],
        out_specs=in_vmem(),
        out_shape=jax.ShapeDtypeStruct(shape, BF16),
        scratch_shapes=[*attention_scratch(), pltpu.SemaphoreType.DMA((2,))],
        compiler_params=params(),
        cost_estimate=pl.CostEstimate(
            flops=8 * 1024 * CHANS * CHANS, bytes_accessed=4 * 2**20, transcendentals=2**20
        ),
        name="grid_attention",
    )(x, *kept_in_hbm(qkv, out_proj), *earlier)


def prepare_kernel(x_ref, _, normed_ref, xp_ref):
    spread = spread_matrix()
    for pair in range(4):
        moved = mm(spread, x_ref[:, 2 * pair : 2 * pair + 2].reshape(256, CHANS))
        xp_ref[256 * pair : 256 * pair + 256] = moved.astype(BF16)
        normed_ref[256 * pair : 256 * pair + 256] = layer_norm(moved)


def prepare(field, after):
    return pl.pallas_call(
        prepare_kernel,
        grid=(2,),
        in_specs=[
            pl.BlockSpec((2, 8, 64, CHANS), lambda k: (0, k, 0, 0)),
            pl.BlockSpec(memory_space=pl.ANY),
        ],
        out_specs=[pl.BlockSpec((1024, CHANS), lambda k: (k, 0))] * 2,
        out_shape=[pltpu.HBM((2048, CHANS), BF16)] * 2,
        compiler_params=params(),
        cost_estimate=pl.CostEstimate(flops=10**10, bytes_accessed=16 * 2**20, transcendentals=0),
        name="prepare",
    )(kept_in_hbm(field.reshape(2, 16, 64, CHANS))[0], after)


def local_kernel(
    part, rim_ref, left_ref, right_ref, normed_hbm, xp_hbm, we_hbm, dw_hbm, wp_hbm, wqkv_hbm, wo_hbm, out_ref,
    normed_ref, outer, special_ref, xp_ref, we_ref, dw_ref, wp_ref, pad, rim, spatial, acc,
    grouped, proj, context, turn_ref, mask_ref, wqkv_ref, wo_ref, sems,
):
    before, after = ((15, 8), (7, 0))[part]
    special, plain = ((before, after), (after, before))[part]
    plain_at = (128, 0)[part]
    first = fetch(
        sems.at[0],
        (normed_hbm.at[128 * special : 128 * special + 128], special_ref),
        (normed_hbm.at[1024 * part : 1024 * part + 1024], normed_ref),
        (normed_hbm.at[128 * plain : 128 * plain + 128], outer.at[plain_at : plain_at + 128]),
    )

    def expansion(s, piece):
        lanes = pl.ds(pl.multiple_of(CB * s + 256 * piece, 256), 256)
        return pltpu.make_async_copy(we_hbm.at[:, lanes], we_ref.at[s, piece], sems.at[1 + s, piece])

    def others(s):
        lanes = pl.ds(pl.multiple_of(CB * s, CB), CB)
        return [
            pltpu.make_async_copy(dw_hbm.at[:, :, lanes], dw_ref.at[s], sems.at[1 + s, PIECES]),
            pltpu.make_async_copy(wp_hbm.at[lanes], wp_ref.at[s], sems.at[1 + s, PIECES + 1]),
        ]

    for s in range(BLOCKS):
        for piece in range(PIECES):
            expansion(s, piece).start()
        for copy in others(s):
            copy.start()
    last = fetch(sems.at[1 + BLOCKS], (xp_hbm.at[1024 * part : 1024 * part + 1024], xp_ref), (wqkv_hbm, wqkv_ref), (wo_hbm, wo_ref))
    turn_ref[...] = turn_matrix()
    mask_ref[...] = head_mask()
    outer[256:304] = layer_norm(left_ref[...].astype(F32))
    outer[304:352] = layer_norm(right_ref[...].astype(F32))
    acc[...] = jnp.zeros_like(acc)
    first[0].wait()
    source = jnp.concatenate([special_ref[...], layer_norm(rim_ref[...].astype(F32))], axis=0)
    outer[128 - plain_at : 256 - plain_at] = mm(edge_matrix(part), source).astype(BF16)
    for copy in first[1:]:
        copy.wait()

    sub = lax.broadcasted_iota(jnp.int32, (8, CB), 0)

    def block(s, carry):
        for piece in range(PIECES):
            at = 256 * piece
            expansion(s, piece).wait()
            made = gelu(mm(normed_ref[...], we_ref[s, piece])).astype(BF16)
            pad[1:9, 1:9, :, at : at + 256] = made.reshape(8, 8, 16, 256)
            made = gelu(mm(outer[...], we_ref[s, piece])).astype(BF16)
            pad[0, 1:9, :, at : at + 256] = made[0:128].reshape(8, 16, 256)
            pad[9, 1:9, :, at : at + 256] = made[128:256].reshape(8, 16, 256)
            rim[:, at : at + 256] = made[256:352].astype(F32)
        for row in range(10):
            at = 8 * part + row
            last = pad[row, 8].astype(F32)
            first = pad[row, 1].astype(F32)
            west, east = [], []
            for b in range(2):
                turned = pltpu.roll(last[8 * b : 8 * b + 8], 1, 0)
                west.append(jnp.where(sub == 0, rim[at + 16 * b : at + 16 * b + 1], turned))
                turned = pltpu.roll(first[8 * b : 8 * b + 8], 7, 0)
                east.append(jnp.where(sub == 7, rim[at + 48 + 16 * b : at + 48 + 16 * b + 1], turned))
            pad[row, 0] = jnp.concatenate(west, axis=0).astype(BF16)
            pad[row, 9] = jnp.concatenate(east, axis=0).astype(BF16)

        for copy in others(s):
            copy.wait()
        taps = [[jnp.broadcast_to(dw_ref[s, a, b : b + 1].astype(BF16), (16, CB)) for b in range(3)] for a in range(3)]

        def pair_of_rows(pair, carry):
            for i in range(2):
                for j in range(8):
                    sums = [
                        pad[2 * pair + i + a, j] * taps[a][0]
                        + pad[2 * pair + i + a, j + 1] * taps[a][1]
                        + pad[2 * pair + i + a, j + 2] * taps[a][2]
                        for a in range(3)
                    ]
                    total = sums[0] + sums[1] + sums[2]
                    spatial[2 * pair + i, j] = gelu(total.astype(F32)).astype(BF16)
            rows = pl.ds(pl.multiple_of(256 * pair, 256), 256)
            acc[rows] += mm(spatial[pl.ds(2 * pair, 2)].reshape(256, CB), wp_ref[s])
            return carry

        lax.fori_loop(0, 4, pair_of_rows, 0, unroll=PAIRS)
        return carry

    lax.fori_loop(0, BLOCKS, block, 0)
    for copy in last:
        copy.wait()
    for pair in range(4):
        rows = slice(256 * pair, 256 * pair + 256)
        mixed = (xp_ref[rows].astype(F32) + acc[rows]).astype(BF16)
        grouped[:, 16 * pair : 16 * pair + 16] = mm(turn_ref[...], mixed).astype(BF16).reshape(16, 16, CHANS)

    def emit(half, rows):
        rows = rows.reshape(4, 2, 8, 8, CHANS)
        for i in range(8):
            out_ref[i, :, half] = rows[:, :, i].reshape(4, 16, CHANS).astype(BF16)

    attention(grouped, wqkv_ref, wo_ref, mask_ref, proj, context, emit)


def local_part(part, rims, *arrays):
    top, bottom, left, right = rims
    return pl.pallas_call(
        functools.partial(local_kernel, part),
        in_specs=[*[in_vmem() for _ in range(3)], *in_hbm(len(arrays))],
        out_specs=in_vmem(),
        out_shape=jax.ShapeDtypeStruct((8, 4, 2, 16, CHANS), BF16),
        scratch_shapes=[
            pltpu.VMEM((1024, CHANS), BF16),
            pltpu.VMEM((352, CHANS), BF16),
            pltpu.VMEM((128, CHANS), BF16),
            pltpu.VMEM((1024, CHANS), BF16),
            pltpu.VMEM((BLOCKS, PIECES, CHANS, 256), BF16),
            pltpu.VMEM((BLOCKS, 3, 3, CB), F32),
            pltpu.VMEM((BLOCKS, CB, CHANS), BF16),
            pltpu.VMEM((10, 10, 16, CB), BF16),
            pltpu.VMEM((96, CB), F32),
            pltpu.VMEM((8, 8, 16, CB), BF16),
            pltpu.VMEM((1024, CHANS), F32),
            *attention_scratch(),
            pltpu.SemaphoreType.DMA((2 + BLOCKS, PIECES + 2)),
        ],
        compiler_params=params(),
        cost_estimate=pl.CostEstimate(
            flops=4 * 1024 * CHANS * WIDE, bytes_accessed=8 * 2**20, transcendentals=2048 * WIDE
        ),
        name="local_part",
    )((top, bottom)[part], left, right, *kept_in_hbm(*arrays))


def exchange(blocks, groups):
    return lax.all_to_all(blocks, ("row", "col"), 0, 0, axis_index_groups=groups, tiled=True)


def on_device(field, w_expand, dw_kernel, w_project, qkv_block, out_block, qkv_grid, out_grid):
    n_row, n_col = lax.axis_size("row"), lax.axis_size("col")
    down = [(i, i + 1) for i in range(n_row - 1)]
    up = [(i + 1, i) for i in range(n_row - 1)]
    top = lax.ppermute(field[31], "row", down)
    bottom = lax.ppermute(field[0], "row", up)
    fill = jnp.zeros((14, CHANS), BF16)

    def rim(column):
        return jnp.concatenate([top[column : column + 1], field[:, column], bottom[column : column + 1], fill], axis=0)

    east, west = rim(63), rim(0)
    left = lax.ppermute(east, "col", [(i, i + 1) for i in range(n_col - 1)])
    right = lax.ppermute(west, "col", [(i + 1, i) for i in range(n_col - 1)])
    normed, xp = prepare(field, east)
    groups = [[32 * row + 4 * j + c for row in range(n_row) for j in range(8)] for c in range(4)]
    gathered = []
    for part in range(2):
        blocked = local_part(
            part, (top, bottom, left, right), normed, xp, w_expand, dw_kernel, w_project, qkv_block, out_block
        )
        gathered.append(exchange(blocked.reshape(32, 2, 16, CHANS), groups).reshape(64, 16, CHANS))
    attended = grid_attention(gathered[0], qkv_grid, out_grid)
    attended = grid_attention(gathered[1], qkv_grid, out_grid, attended)
    home = exchange(attended, groups).reshape(8, 4, 2, 2, 16, CHANS)
    return home.transpose(3, 2, 0, 1, 4, 5).reshape(32, 64, CHANS)


def solution(mesh):
    placed = (P("row", "col", None), P(), P(), P(), P(), P(), P(), P())
    return jax.shard_map(
        on_device, mesh=mesh, in_specs=placed, out_specs=P("row", "col", None), check_vma=False
    )
```

```python
import functools

import jax
import jax.numpy as jnp
import numpy as np
from jax import lax
from jax.experimental import pallas as pl
from jax.experimental.pallas import tpu as pltpu
from jax.sharding import PartitionSpec as P

BF16 = jnp.bfloat16
F32 = jnp.float32
HEAD = 32
CHANS = 512
WIDE = 2048
CB = 1024
BLOCKS = WIDE // CB
PAIRS = 4
PIECES = CB // 256
VMEM_LIMIT = 36 * 2**20
SCALE_LOG2 = float(HEAD**-0.5 * np.log2(np.e))


def layer_norm(v):
    mean = jnp.mean(v, axis=-1, keepdims=True)
    cent = v - mean
    var = jnp.mean(cent * cent, axis=-1, keepdims=True)
    return (cent * lax.rsqrt(var + 1e-05)).astype(BF16)


def gelu(v):
    half = 0.5 * v
    return half + half * lax.erf(v * 0.7071067811865476)


def mm(a, b):
    return lax.dot_general(a, b, (((1,), (0,)), ((), ())), preferred_element_type=F32)


def mm_nt(a, b):
    return lax.dot_general(a, b, (((1,), (1,)), ((), ())), preferred_element_type=F32)


def ones_where(shape, holds):
    row = lax.broadcasted_iota(jnp.int32, shape, 0)
    column = lax.broadcasted_iota(jnp.int32, shape, 1)
    return jnp.where(holds(row, column), 1.0, 0.0).astype(BF16)


def spread_matrix():
    return ones_where(
        (256, 256),
        lambda r, c: c == ((r >> 3) & 1) * 128 + (r >> 7) * 64 + (r & 7) * 8 + ((r >> 4) & 7),
    )


def turn_matrix():
    return ones_where((256, 256), lambda r, c: c == (r & 15) * 16 + (r >> 4))


def edge_matrix(part):
    def holds(r, c):
        j, b, q = r >> 4, (r >> 3) & 1, r & 7
        own = c == j * 16 + 8 * part + q
        rim = c == 128 + q * 8 + j
        return (own & (b == 1 - part)) | (rim & (b == part))

    return ones_where((128, 192), holds)


def head_mask():
    return ones_where((256, 128), lambda r, c: (r >> 6) == (c >> 5))


def in_vmem():
    return pl.BlockSpec(memory_space=pltpu.VMEM)


def in_hbm(count):
    return [pl.BlockSpec(memory_space=pltpu.HBM)] * count


def kept_in_hbm(*arrays):
    return [pltpu.with_memory_space_constraint(a, pltpu.HBM) for a in arrays]


def fetch(sems, *pairs):
    copies = [pltpu.make_async_copy(source, to, sems.at[at]) for at, (source, to) in enumerate(pairs)]
    for copy in copies:
        copy.start()
    return copies


def params():
    return pltpu.CompilerParams(vmem_limit_bytes=VMEM_LIMIT)


def segment_max(scores):
    low = lax.broadcasted_iota(jnp.int32, (1, 128), 1) < 64
    found = []
    for at in range(0, scores.shape[1], 128):
        v = scores[:, at : at + 128]
        first = jnp.max(jnp.where(low, v, -jnp.inf), axis=-1, keepdims=True)
        second = jnp.max(jnp.where(low, -jnp.inf, v), axis=-1, keepdims=True)
        found.append(jnp.where(low, first, second))
    return jnp.concatenate(found, axis=1)


def weight_fetches(wqkv_hbm, wo_hbm, wqkv_ref, wo_ref, sems):
    copies = [
        pltpu.make_async_copy(wqkv_hbm.at[:, CHANS * k : CHANS * k + CHANS], wqkv_ref.at[k], sems.at[k]) for k in range(3)
    ]
    return [*copies, pltpu.make_async_copy(wo_hbm, wo_ref, sems.at[3])]


def attention(grouped, wqkv_ref, wo_ref, mask_ref, proj, context, copies, emit):
    mask = mask_ref[...]
    for half in range(2):
        x = grouped[8 * half : 8 * half + 8].reshape(512, CHANS).astype(F32)
        normed = layer_norm(x)
        for k in range(3):
            if half == 0:
                copies[k].wait()
            proj[:, CHANS * k : CHANS * k + CHANS] = mm(normed, wqkv_ref[k]).astype(BF16)
        for g in range(8):
            rows = slice(64 * g, 64 * g + 64)
            for at in range(0, CHANS, 128):
                query = proj[rows, at : at + 128]
                keys = jnp.concatenate([proj[rows, CHANS + at : CHANS + at + 128]] * 4, axis=0) * mask
                values = jnp.concatenate([proj[rows, 2 * CHANS + at : 2 * CHANS + at + 128]] * 4, axis=0) * mask
                scores = mm_nt(query, keys)
                weights = jnp.exp2((scores - segment_max(scores)) * SCALE_LOG2).astype(BF16)
                both = mm(weights, jnp.concatenate([values, mask], axis=1))
                context[rows, at : at + 128] = (both[:, :128] / both[:, 128:]).astype(BF16)
        if half == 0:
            copies[3].wait()
        emit(half, x + mm(context[...], wo_ref[...]))


def grid_kernel(x_ref, wqkv_hbm, wo_hbm, *rest):
    out_ref, grouped, proj, context, turn_ref, mask_ref, wqkv_ref, wo_ref, sems = rest[-9:]
    copies = weight_fetches(wqkv_hbm, wo_hbm, wqkv_ref, wo_ref, sems)
    for copy in copies:
        copy.start()
    turn_ref[...] = turn_matrix()
    mask_ref[...] = head_mask()
    for t in range(4):
        moved = mm(turn_ref[...], x_ref[16 * t : 16 * t + 16].reshape(256, CHANS))
        grouped[:, 16 * t : 16 * t + 16] = moved.astype(BF16).reshape(16, 16, CHANS)

    def emit(half, rows):
        grouped[pl.ds(8 * half, 8)] = rows.astype(BF16).reshape(8, 64, CHANS)

    attention(grouped, wqkv_ref, wo_ref, mask_ref, proj, context, copies, emit)
    for t in range(4):
        moved = mm(turn_ref[...], grouped[:, 16 * t : 16 * t + 16].reshape(256, CHANS))
        moved = moved.astype(BF16).reshape(8, 2, 16, CHANS)
        if len(rest) == 9:
            out_ref[8 * t : 8 * t + 8] = moved
        else:
            out_ref[8 * t : 8 * t + 8, 1] = moved
    if len(rest) > 9:
        out_ref[:, 0] = rest[0][...]


def attention_scratch():
    return [
        pltpu.VMEM((16, 64, CHANS), BF16),
        pltpu.VMEM((512, 3 * CHANS), BF16),
        pltpu.VMEM((512, CHANS), BF16),
        pltpu.VMEM((256, 256), BF16),
        pltpu.VMEM((256, 128), BF16),
        pltpu.VMEM((3, CHANS, CHANS), BF16),
        pltpu.VMEM((CHANS, CHANS), BF16),
    ]


def grid_attention(x, qkv, out_proj, *earlier):
    shape = (32, 2, 2, 16, CHANS) if earlier else (32, 2, 16, CHANS)
    return pl.pallas_call(
        grid_kernel,
        in_specs=[in_vmem(), *in_hbm(2), *[in_vmem() for _ in earlier]],
        out_specs=in_vmem(),
        out_shape=jax.ShapeDtypeStruct(shape, BF16),
        scratch_shapes=[*attention_scratch(), pltpu.SemaphoreType.DMA((4,))],
        compiler_params=params(),
        cost_estimate=pl.CostEstimate(
            flops=8 * 1024 * CHANS * CHANS, bytes_accessed=4 * 2**20, transcendentals=2**20
        ),
        name="grid_attention",
    )(x, *kept_in_hbm(qkv, out_proj), *earlier)


def prepare_kernel(x_ref, _, normed_ref, xp_ref):
    spread = spread_matrix()
    for pair in range(4):
        moved = mm(spread, x_ref[:, 2 * pair : 2 * pair + 2].reshape(256, CHANS))
        xp_ref[256 * pair : 256 * pair + 256] = moved.astype(BF16)
        normed_ref[256 * pair : 256 * pair + 256] = layer_norm(moved)


def prepare(field, after):
    return pl.pallas_call(
        prepare_kernel,
        grid=(2,),
        in_specs=[
            pl.BlockSpec((2, 8, 64, CHANS), lambda k: (0, k, 0, 0)),
            pl.BlockSpec(memory_space=pl.ANY),
        ],
        out_specs=[pl.BlockSpec((1024, CHANS), lambda k: (k, 0))] * 2,
        out_shape=[pltpu.HBM((2048, CHANS), BF16)] * 2,
        compiler_params=params(),
        cost_estimate=pl.CostEstimate(flops=10**10, bytes_accessed=16 * 2**20, transcendentals=0),
        name="prepare",
    )(kept_in_hbm(field.reshape(2, 16, 64, CHANS))[0], after)


def local_kernel(
    part, rim_ref, left_ref, right_ref, normed_hbm, xp_hbm, we_hbm, dw_hbm, wp_hbm, wqkv_hbm, wo_hbm, out_ref,
    normed_ref, outer, special_ref, xp_ref, we_ref, dw_ref, wp_ref, pad, rim, spatial, acc,
    grouped, proj, context, turn_ref, mask_ref, wqkv_ref, wo_ref, sems,
):
    before, after = ((15, 8), (7, 0))[part]
    special, plain = ((before, after), (after, before))[part]
    plain_at = (128, 0)[part]
    first = fetch(
        sems.at[0],
        (normed_hbm.at[128 * special : 128 * special + 128], special_ref),
        (normed_hbm.at[1024 * part : 1024 * part + 1024], normed_ref),
        (normed_hbm.at[128 * plain : 128 * plain + 128], outer.at[plain_at : plain_at + 128]),
    )

    def expansion(s, piece):
        lanes = pl.ds(pl.multiple_of(CB * s + 256 * piece, 256), 256)
        return pltpu.make_async_copy(we_hbm.at[:, lanes], we_ref.at[s, piece], sems.at[1 + s, piece])

    def others(s):
        lanes = pl.ds(pl.multiple_of(CB * s, CB), CB)
        return [
            pltpu.make_async_copy(dw_hbm.at[:, :, lanes], dw_ref.at[s], sems.at[1 + s, PIECES]),
            pltpu.make_async_copy(wp_hbm.at[lanes], wp_ref.at[s], sems.at[1 + s, PIECES + 1]),
        ]

    for piece in range(PIECES):
        expansion(0, piece).start()
    tokens = pltpu.make_async_copy(xp_hbm.at[1024 * part : 1024 * part + 1024], xp_ref, sems.at[0, 3])
    last = weight_fetches(wqkv_hbm, wo_hbm, wqkv_ref, wo_ref, sems.at[1 + BLOCKS])
    turn_ref[...] = turn_matrix()
    mask_ref[...] = head_mask()
    outer[256:304] = layer_norm(left_ref[...].astype(F32))
    outer[304:352] = layer_norm(right_ref[...].astype(F32))
    acc[...] = jnp.zeros_like(acc)
    first[0].wait()
    source = jnp.concatenate([special_ref[...], layer_norm(rim_ref[...].astype(F32))], axis=0)
    outer[128 - plain_at : 256 - plain_at] = mm(edge_matrix(part), source).astype(BF16)
    for copy in first[1:]:
        copy.wait()
    for copy in others(0):
        copy.start()

    sub = lax.broadcasted_iota(jnp.int32, (8, CB), 0)

    def block(s, carry):
        for piece in range(PIECES):
            at = 256 * piece
            expansion(s, piece).wait()
            made = gelu(mm(normed_ref[...], we_ref[s, piece])).astype(BF16)
            pad[1:9, 1:9, :, at : at + 256] = made.reshape(8, 8, 16, 256)
            made = gelu(mm(outer[...], we_ref[s, piece])).astype(BF16)
            pad[0, 1:9, :, at : at + 256] = made[0:128].reshape(8, 16, 256)
            pad[9, 1:9, :, at : at + 256] = made[128:256].reshape(8, 16, 256)
            rim[:, at : at + 256] = made[256:352].astype(F32)
        for row in range(10):
            at = 8 * part + row
            far = pad[row, 8].astype(F32)
            near = pad[row, 1].astype(F32)
            west, east = [], []
            for b in range(2):
                turned = pltpu.roll(far[8 * b : 8 * b + 8], 1, 0)
                west.append(jnp.where(sub == 0, rim[at + 16 * b : at + 16 * b + 1], turned))
                turned = pltpu.roll(near[8 * b : 8 * b + 8], 7, 0)
                east.append(jnp.where(sub == 7, rim[at + 48 + 16 * b : at + 48 + 16 * b + 1], turned))
            pad[row, 0] = jnp.concatenate(west, axis=0).astype(BF16)
            pad[row, 9] = jnp.concatenate(east, axis=0).astype(BF16)

        for copy in others(s):
            copy.wait()

        @pl.when(s + 1 < BLOCKS)
        def _():
            for piece in range(PIECES):
                expansion(s + 1, piece).start()
            for copy in others(s + 1):
                copy.start()

        @pl.when(s == BLOCKS - 1)
        def _():
            tokens.start()
            for copy in last:
                copy.start()

        taps = [[jnp.broadcast_to(dw_ref[s, a, b : b + 1].astype(BF16), (16, CB)) for b in range(3)] for a in range(3)]

        def pair_of_rows(pair, carry):
            for i in range(2):
                for j in range(8):
                    sums = [
                        pad[2 * pair + i + a, j] * taps[a][0]
                        + pad[2 * pair + i + a, j + 1] * taps[a][1]
                        + pad[2 * pair + i + a, j + 2] * taps[a][2]
                        for a in range(3)
                    ]
                    total = sums[0] + sums[1] + sums[2]
                    spatial[2 * pair + i, j] = gelu(total.astype(F32)).astype(BF16)
            rows = pl.ds(pl.multiple_of(256 * pair, 256), 256)
            acc[rows] += mm(spatial[pl.ds(2 * pair, 2)].reshape(256, CB), wp_ref[s])
            return carry

        lax.fori_loop(0, 4, pair_of_rows, 0, unroll=PAIRS)
        return carry

    lax.fori_loop(0, BLOCKS, block, 0)
    tokens.wait()
    for pair in range(4):
        rows = slice(256 * pair, 256 * pair + 256)
        mixed = (xp_ref[rows].astype(F32) + acc[rows]).astype(BF16)
        grouped[:, 16 * pair : 16 * pair + 16] = mm(turn_ref[...], mixed).astype(BF16).reshape(16, 16, CHANS)

    def emit(half, rows):
        rows = rows.reshape(4, 2, 8, 8, CHANS)
        for i in range(8):
            out_ref[i, :, half] = rows[:, :, i].reshape(4, 16, CHANS).astype(BF16)

    attention(grouped, wqkv_ref, wo_ref, mask_ref, proj, context, last, emit)


def local_part(part, rims, *arrays):
    top, bottom, left, right = rims
    return pl.pallas_call(
        functools.partial(local_kernel, part),
        in_specs=[*[in_vmem() for _ in range(3)], *in_hbm(len(arrays))],
        out_specs=in_vmem(),
        out_shape=jax.ShapeDtypeStruct((8, 4, 2, 16, CHANS), BF16),
        scratch_shapes=[
            pltpu.VMEM((1024, CHANS), BF16),
            pltpu.VMEM((352, CHANS), BF16),
            pltpu.VMEM((128, CHANS), BF16),
            pltpu.VMEM((1024, CHANS), BF16),
            pltpu.VMEM((BLOCKS, PIECES, CHANS, 256), BF16),
            pltpu.VMEM((BLOCKS, 3, 3, CB), F32),
            pltpu.VMEM((BLOCKS, CB, CHANS), BF16),
            pltpu.VMEM((10, 10, 16, CB), BF16),
            pltpu.VMEM((96, CB), F32),
            pltpu.VMEM((8, 8, 16, CB), BF16),
            pltpu.VMEM((1024, CHANS), F32),
            *attention_scratch(),
            pltpu.SemaphoreType.DMA((2 + BLOCKS, PIECES + 2)),
        ],
        compiler_params=params(),
        cost_estimate=pl.CostEstimate(
            flops=4 * 1024 * CHANS * WIDE, bytes_accessed=8 * 2**20, transcendentals=2048 * WIDE
        ),
        name="local_part",
    )((top, bottom)[part], left, right, *kept_in_hbm(*arrays))


def exchange(blocks, groups):
    return lax.all_to_all(blocks, ("row", "col"), 0, 0, axis_index_groups=groups, tiled=True)


def on_device(field, w_expand, dw_kernel, w_project, qkv_block, out_block, qkv_grid, out_grid):
    n_row, n_col = lax.axis_size("row"), lax.axis_size("col")
    down = [(i, i + 1) for i in range(n_row - 1)]
    up = [(i + 1, i) for i in range(n_row - 1)]
    top = lax.ppermute(field[31], "row", down)
    bottom = lax.ppermute(field[0], "row", up)
    fill = jnp.zeros((14, CHANS), BF16)

    def rim(column):
        return jnp.concatenate([top[column : column + 1], field[:, column], bottom[column : column + 1], fill], axis=0)

    east, west = rim(63), rim(0)
    left = lax.ppermute(east, "col", [(i, i + 1) for i in range(n_col - 1)])
    right = lax.ppermute(west, "col", [(i + 1, i) for i in range(n_col - 1)])
    normed, xp = prepare(field, east)
    groups = [[32 * row + 4 * j + c for row in range(n_row) for j in range(8)] for c in range(4)]
    gathered = []
    for part in range(2):
        blocked = local_part(
            part, (top, bottom, left, right), normed, xp, w_expand, dw_kernel, w_project, qkv_block, out_block
        )
        gathered.append(exchange(blocked.reshape(32, 2, 16, CHANS), groups).reshape(64, 16, CHANS))
    attended = grid_attention(gathered[0], qkv_grid, out_grid)
    attended = grid_attention(gathered[1], qkv_grid, out_grid, attended)
    home = exchange(attended, groups).reshape(8, 4, 2, 2, 16, CHANS)
    return home.transpose(3, 2, 0, 1, 4, 5).reshape(32, 64, CHANS)


def solution(mesh):
    placed = (P("row", "col", None), P(), P(), P(), P(), P(), P(), P())
    return jax.shard_map(
        on_device, mesh=mesh, in_specs=placed, out_specs=P("row", "col", None), check_vma=False
    )
```

```python
import functools

import jax
import jax.numpy as jnp
import numpy as np
from jax import lax
from jax.experimental import pallas as pl
from jax.experimental.pallas import tpu as pltpu
from jax.sharding import PartitionSpec as P

BF16 = jnp.bfloat16
F32 = jnp.float32
HEAD = 32
CHANS = 512
WIDE = 2048
CB = 1024
BLOCKS = WIDE // CB
PAIRS = 4
VMEM_LIMIT = 36 * 2**20
SCALE_LOG2 = float(HEAD**-0.5 * np.log2(np.e))


def layer_norm(v):
    mean = jnp.mean(v, axis=-1, keepdims=True)
    cent = v - mean
    var = jnp.mean(cent * cent, axis=-1, keepdims=True)
    return (cent * lax.rsqrt(var + 1e-05)).astype(BF16)


def gelu(v):
    half = 0.5 * v
    return half + half * lax.erf(v * 0.7071067811865476)


def mm(a, b):
    return lax.dot_general(a, b, (((1,), (0,)), ((), ())), preferred_element_type=F32)


def mm_nt(a, b):
    return lax.dot_general(a, b, (((1,), (1,)), ((), ())), preferred_element_type=F32)


def ones_where(shape, holds):
    row = lax.broadcasted_iota(jnp.int32, shape, 0)
    column = lax.broadcasted_iota(jnp.int32, shape, 1)
    return jnp.where(holds(row, column), 1.0, 0.0).astype(BF16)


def spread_matrix():
    return ones_where(
        (256, 256),
        lambda r, c: c == ((r >> 3) & 1) * 128 + (r >> 7) * 64 + (r & 7) * 8 + ((r >> 4) & 7),
    )


def turn_matrix():
    return ones_where((256, 256), lambda r, c: c == (r & 15) * 16 + (r >> 4))


def edge_matrix(part):
    def holds(r, c):
        j, b, q = r >> 4, (r >> 3) & 1, r & 7
        own = c == j * 16 + 8 * part + q
        rim = c == 128 + q * 8 + j
        return (own & (b == 1 - part)) | (rim & (b == part))

    return ones_where((128, 192), holds)


def head_mask():
    return ones_where((256, 128), lambda r, c: (r >> 6) == (c >> 5))


def in_vmem():
    return pl.BlockSpec(memory_space=pltpu.VMEM)


def in_hbm(count):
    return [pl.BlockSpec(memory_space=pltpu.HBM)] * count


def kept_in_hbm(*arrays):
    return [pltpu.with_memory_space_constraint(a, pltpu.HBM) for a in arrays]


def fetch(sems, *pairs):
    copies = [pltpu.make_async_copy(source, to, sems.at[at]) for at, (source, to) in enumerate(pairs)]
    for copy in copies:
        copy.start()
    return copies


def params():
    return pltpu.CompilerParams(vmem_limit_bytes=VMEM_LIMIT)


def segment_max(scores):
    low = lax.broadcasted_iota(jnp.int32, (1, 128), 1) < 64
    found = []
    for at in range(0, scores.shape[1], 128):
        v = scores[:, at : at + 128]
        first = jnp.max(jnp.where(low, v, -jnp.inf), axis=-1, keepdims=True)
        second = jnp.max(jnp.where(low, -jnp.inf, v), axis=-1, keepdims=True)
        found.append(jnp.where(low, first, second))
    return jnp.concatenate(found, axis=1)


def attention(grouped, wqkv_ref, wo_ref, mask_ref, proj, context, emit):
    mask = mask_ref[...]

    def one(half, carry):
        x = grouped[pl.ds(8 * half, 8)].reshape(512, CHANS).astype(F32)
        proj[...] = mm(layer_norm(x), wqkv_ref[...]).astype(BF16)
        for g in range(8):
            rows = slice(64 * g, 64 * g + 64)
            for at in range(0, CHANS, 128):
                query = proj[rows, at : at + 128]
                keys = jnp.concatenate([proj[rows, CHANS + at : CHANS + at + 128]] * 4, axis=0) * mask
                values = jnp.concatenate([proj[rows, 2 * CHANS + at : 2 * CHANS + at + 128]] * 4, axis=0) * mask
                scores = mm_nt(query, keys)
                weights = jnp.exp2((scores - segment_max(scores)) * SCALE_LOG2).astype(BF16)
                both = mm(weights, jnp.concatenate([values, mask], axis=1))
                context[rows, at : at + 128] = (both[:, :128] / both[:, 128:]).astype(BF16)
        emit(half, x + mm(context[...], wo_ref[...]))
        return carry

    lax.fori_loop(0, 2, one, 0, unroll=2)


def grid_kernel(x_ref, wqkv_hbm, wo_hbm, *rest):
    out_ref, grouped, proj, context, turn_ref, mask_ref, wqkv_ref, wo_ref, sems = rest[-9:]
    copies = fetch(sems, (wqkv_hbm, wqkv_ref), (wo_hbm, wo_ref))
    turn_ref[...] = turn_matrix()
    mask_ref[...] = head_mask()
    for t in range(4):
        moved = mm(turn_ref[...], x_ref[16 * t : 16 * t + 16].reshape(256, CHANS))
        grouped[:, 16 * t : 16 * t + 16] = moved.astype(BF16).reshape(16, 16, CHANS)

    def emit(half, rows):
        grouped[pl.ds(8 * half, 8)] = rows.astype(BF16).reshape(8, 64, CHANS)

    for copy in copies:
        copy.wait()
    attention(grouped, wqkv_ref, wo_ref, mask_ref, proj, context, emit)
    for t in range(4):
        moved = mm(turn_ref[...], grouped[:, 16 * t : 16 * t + 16].reshape(256, CHANS))
        moved = moved.astype(BF16).reshape(8, 2, 16, CHANS)
        if len(rest) == 9:
            out_ref[8 * t : 8 * t + 8] = moved
        else:
            out_ref[8 * t : 8 * t + 8, 1] = moved
    if len(rest) > 9:
        out_ref[:, 0] = rest[0][...]


def attention_scratch():
    return [
        pltpu.VMEM((16, 64, CHANS), BF16),
        pltpu.VMEM((512, 3 * CHANS), BF16),
        pltpu.VMEM((512, CHANS), BF16),
        pltpu.VMEM((256, 256), BF16),
        pltpu.VMEM((256, 128), BF16),
        pltpu.VMEM((CHANS, 3 * CHANS), BF16),
        pltpu.VMEM((CHANS, CHANS), BF16),
    ]


def grid_attention(x, qkv, out_proj, *earlier):
    shape = (32, 2, 2, 16, CHANS) if earlier else (32, 2, 16, CHANS)
    return pl.pallas_call(
        grid_kernel,
        in_specs=[in_vmem(), *in_hbm(2), *[in_vmem() for _ in earlier]],
        out_specs=in_vmem(),
        out_shape=jax.ShapeDtypeStruct(shape, BF16),
        scratch_shapes=[*attention_scratch(), pltpu.SemaphoreType.DMA((2,))],
        compiler_params=params(),
        cost_estimate=pl.CostEstimate(
            flops=8 * 1024 * CHANS * CHANS, bytes_accessed=4 * 2**20, transcendentals=2**20
        ),
        name="grid_attention",
    )(x, *kept_in_hbm(qkv, out_proj), *earlier)


def prepare_kernel(x_ref, _, normed_ref, xp_ref):
    spread = spread_matrix()
    for pair in range(4):
        moved = mm(spread, x_ref[:, 2 * pair : 2 * pair + 2].reshape(256, CHANS))
        xp_ref[256 * pair : 256 * pair + 256] = moved.astype(BF16)
        normed_ref[256 * pair : 256 * pair + 256] = layer_norm(moved)


def prepare(field, after):
    return pl.pallas_call(
        prepare_kernel,
        grid=(2,),
        in_specs=[
            pl.BlockSpec((2, 8, 64, CHANS), lambda k: (0, k, 0, 0)),
            pl.BlockSpec(memory_space=pl.ANY),
        ],
        out_specs=[pl.BlockSpec((1024, CHANS), lambda k: (k, 0))] * 2,
        out_shape=[pltpu.HBM((2048, CHANS), BF16)] * 2,
        compiler_params=params(),
        cost_estimate=pl.CostEstimate(flops=10**10, bytes_accessed=16 * 2**20, transcendentals=0),
        name="prepare",
    )(kept_in_hbm(field.reshape(2, 16, 64, CHANS))[0], after)


def local_kernel(
    part, rim_ref, left_ref, right_ref, normed_hbm, xp_hbm, we_hbm, dw_hbm, wp_hbm, wqkv_hbm, wo_hbm, out_ref,
    normed_ref, outer, special_ref, xp_ref, we_ref, dw_ref, wp_ref, pad, rim, spatial, acc,
    grouped, proj, context, turn_ref, mask_ref, wqkv_ref, wo_ref, sems,
):
    before, after = ((15, 8), (7, 0))[part]
    special, plain = ((before, after), (after, before))[part]
    plain_at = (128, 0)[part]
    first = fetch(
        sems.at[0],
        (normed_hbm.at[128 * special : 128 * special + 128], special_ref),
        (normed_hbm.at[1024 * part : 1024 * part + 1024], normed_ref),
        (normed_hbm.at[128 * plain : 128 * plain + 128], outer.at[plain_at : plain_at + 128]),
    )

    blocks = []
    for s in range(BLOCKS):
        lanes = slice(CB * s, CB * s + CB)
        blocks += fetch(
            sems.at[1 + s],
            (we_hbm.at[:, lanes], we_ref.at[s]),
            (dw_hbm.at[:, :, lanes], dw_ref.at[s]),
            (wp_hbm.at[lanes], wp_ref.at[s]),
        )
    last = fetch(sems.at[1 + BLOCKS], (xp_hbm.at[1024 * part : 1024 * part + 1024], xp_ref), (wqkv_hbm, wqkv_ref), (wo_hbm, wo_ref))
    turn_ref[...] = turn_matrix()
    mask_ref[...] = head_mask()
    outer[256:304] = layer_norm(left_ref[...].astype(F32))
    outer[304:352] = layer_norm(right_ref[...].astype(F32))
    acc[...] = jnp.zeros_like(acc)
    first[0].wait()
    source = jnp.concatenate([special_ref[...], layer_norm(rim_ref[...].astype(F32))], axis=0)
    outer[128 - plain_at : 256 - plain_at] = mm(edge_matrix(part), source).astype(BF16)
    for copy in (*first[1:], *blocks):
        copy.wait()

    sub = lax.broadcasted_iota(jnp.int32, (8, CB), 0)

    def block(s, carry):
        for at in range(0, CB, 256):
            made = gelu(mm(normed_ref[...], we_ref[s, :, at : at + 256])).astype(BF16)
            pad[1:9, 1:9, :, at : at + 256] = made.reshape(8, 8, 16, 256)
            made = gelu(mm(outer[...], we_ref[s, :, at : at + 256])).astype(BF16)
            pad[0, 1:9, :, at : at + 256] = made[0:128].reshape(8, 16, 256)
            pad[9, 1:9, :, at : at + 256] = made[128:256].reshape(8, 16, 256)
            rim[:, at : at + 256] = made[256:352].astype(F32)
        for row in range(10):
            at = 8 * part + row
            last = pad[row, 8].astype(F32)
            first = pad[row, 1].astype(F32)
            west, east = [], []
            for b in range(2):
                turned = pltpu.roll(last[8 * b : 8 * b + 8], 1, 0)
                west.append(jnp.where(sub == 0, rim[at + 16 * b : at + 16 * b + 1], turned))
                turned = pltpu.roll(first[8 * b : 8 * b + 8], 7, 0)
                east.append(jnp.where(sub == 7, rim[at + 48 + 16 * b : at + 48 + 16 * b + 1], turned))
            pad[row, 0] = jnp.concatenate(west, axis=0).astype(BF16)
            pad[row, 9] = jnp.concatenate(east, axis=0).astype(BF16)

        taps = [[jnp.broadcast_to(dw_ref[s, a, b : b + 1].astype(BF16), (16, CB)) for b in range(3)] for a in range(3)]

        def pair_of_rows(pair, carry):
            for i in range(2):
                for j in range(8):
                    sums = [
                        pad[2 * pair + i + a, j] * taps[a][0]
                        + pad[2 * pair + i + a, j + 1] * taps[a][1]
                        + pad[2 * pair + i + a, j + 2] * taps[a][2]
                        for a in range(3)
                    ]
                    total = sums[0] + sums[1] + sums[2]
                    spatial[2 * pair + i, j] = gelu(total.astype(F32)).astype(BF16)
            rows = pl.ds(pl.multiple_of(256 * pair, 256), 256)
            acc[rows] += mm(spatial[pl.ds(2 * pair, 2)].reshape(256, CB), wp_ref[s])
            return carry

        lax.fori_loop(0, 4, pair_of_rows, 0, unroll=PAIRS)
        return carry

    lax.fori_loop(0, BLOCKS, block, 0)
    for copy in last:
        copy.wait()
    for pair in range(4):
        rows = slice(256 * pair, 256 * pair + 256)
        mixed = (xp_ref[rows].astype(F32) + acc[rows]).astype(BF16)
        grouped[:, 16 * pair : 16 * pair + 16] = mm(turn_ref[...], mixed).astype(BF16).reshape(16, 16, CHANS)

    def emit(half, rows):
        rows = rows.reshape(4, 2, 8, 8, CHANS)
        for i in range(8):
            out_ref[i, :, half] = rows[:, :, i].reshape(4, 16, CHANS).astype(BF16)

    attention(grouped, wqkv_ref, wo_ref, mask_ref, proj, context, emit)


def local_part(part, rims, *arrays):
    top, bottom, left, right = rims
    return pl.pallas_call(
        functools.partial(local_kernel, part),
        in_specs=[*[in_vmem() for _ in range(3)], *in_hbm(len(arrays))],
        out_specs=in_vmem(),
        out_shape=jax.ShapeDtypeStruct((8, 4, 2, 16, CHANS), BF16),
        scratch_shapes=[
            pltpu.VMEM((1024, CHANS), BF16),
            pltpu.VMEM((352, CHANS), BF16),
            pltpu.VMEM((128, CHANS), BF16),
            pltpu.VMEM((1024, CHANS), BF16),
            pltpu.VMEM((BLOCKS, CHANS, CB), BF16),
            pltpu.VMEM((BLOCKS, 3, 3, CB), F32),
            pltpu.VMEM((BLOCKS, CB, CHANS), BF16),
            pltpu.VMEM((10, 10, 16, CB), BF16),
            pltpu.VMEM((96, CB), F32),
            pltpu.VMEM((8, 8, 16, CB), BF16),
            pltpu.VMEM((1024, CHANS), F32),
            *attention_scratch(),
            pltpu.SemaphoreType.DMA((2 + BLOCKS, 3)),
        ],
        compiler_params=params(),
        cost_estimate=pl.CostEstimate(
            flops=4 * 1024 * CHANS * WIDE, bytes_accessed=8 * 2**20, transcendentals=2048 * WIDE
        ),
        name="local_part",
    )((top, bottom)[part], left, right, *kept_in_hbm(*arrays))


def exchange(blocks, groups):
    return lax.all_to_all(blocks, ("row", "col"), 0, 0, axis_index_groups=groups, tiled=True)


def on_device(field, w_expand, dw_kernel, w_project, qkv_block, out_block, qkv_grid, out_grid):
    n_row, n_col = lax.axis_size("row"), lax.axis_size("col")
    down = [(i, i + 1) for i in range(n_row - 1)]
    up = [(i + 1, i) for i in range(n_row - 1)]
    top = lax.ppermute(field[31], "row", down)
    bottom = lax.ppermute(field[0], "row", up)
    fill = jnp.zeros((14, CHANS), BF16)

    def rim(column):
        return jnp.concatenate([top[column : column + 1], field[:, column], bottom[column : column + 1], fill], axis=0)

    east, west = rim(63), rim(0)
    left = lax.ppermute(east, "col", [(i, i + 1) for i in range(n_col - 1)])
    right = lax.ppermute(west, "col", [(i + 1, i) for i in range(n_col - 1)])
    normed, xp = prepare(field, east)
    groups = [[32 * row + 4 * j + c for row in range(n_row) for j in range(8)] for c in range(4)]
    gathered = []
    for part in range(2):
        blocked = local_part(
            part, (top, bottom, left, right), normed, xp, w_expand, dw_kernel, w_project, qkv_block, out_block
        )
        gathered.append(exchange(blocked.reshape(32, 2, 16, CHANS), groups).reshape(64, 16, CHANS))
    attended = grid_attention(gathered[0], qkv_grid, out_grid)
    attended = grid_attention(gathered[1], qkv_grid, out_grid, attended)
    home = exchange(attended, groups).reshape(8, 4, 2, 2, 16, CHANS)
    return home.transpose(3, 2, 0, 1, 4, 5).reshape(32, 64, CHANS)


def solution(mesh):
    placed = (P("row", "col", None), P(), P(), P(), P(), P(), P(), P())
    return jax.shard_map(
        on_device, mesh=mesh, in_specs=placed, out_specs=P("row", "col", None), check_vma=False
    )
```

```python
import functools

import jax
import jax.numpy as jnp
import numpy as np
from jax import lax
from jax.experimental import pallas as pl
from jax.experimental.pallas import tpu as pltpu
from jax.sharding import PartitionSpec as P

BF16 = jnp.bfloat16
F32 = jnp.float32
HEAD = 32
CHANS = 512
WIDE = 2048
CB = 1024
BLOCKS = WIDE // CB
PAIRS = 4
VMEM_LIMIT = 36 * 2**20
SCALE_LOG2 = float(HEAD**-0.5 * np.log2(np.e))


def layer_norm(v):
    mean = jnp.mean(v, axis=-1, keepdims=True)
    cent = v - mean
    var = jnp.mean(cent * cent, axis=-1, keepdims=True)
    return (cent * lax.rsqrt(var + 1e-05)).astype(BF16)


def gelu(v):
    half = 0.5 * v
    return half + half * lax.erf(v * 0.7071067811865476)


def mm(a, b):
    return lax.dot_general(a, b, (((1,), (0,)), ((), ())), preferred_element_type=F32)


def mm_nt(a, b):
    return lax.dot_general(a, b, (((1,), (1,)), ((), ())), preferred_element_type=F32)


def ones_where(shape, holds):
    row = lax.broadcasted_iota(jnp.int32, shape, 0)
    column = lax.broadcasted_iota(jnp.int32, shape, 1)
    return jnp.where(holds(row, column), 1.0, 0.0).astype(BF16)


def spread_matrix():
    return ones_where(
        (256, 256),
        lambda r, c: c == ((r >> 3) & 1) * 128 + (r >> 7) * 64 + (r & 7) * 8 + ((r >> 4) & 7),
    )


def turn_matrix():
    return ones_where((256, 256), lambda r, c: c == (r & 15) * 16 + (r >> 4))


def edge_matrix(part):
    def holds(r, c):
        j, b, q = r >> 4, (r >> 3) & 1, r & 7
        own = c == j * 16 + 8 * part + q
        rim = c == 128 + q * 8 + j
        return (own & (b == 1 - part)) | (rim & (b == part))

    return ones_where((128, 192), holds)


def head_mask():
    return ones_where((256, 128), lambda r, c: (r >> 6) == (c >> 5))


def in_vmem():
    return pl.BlockSpec(memory_space=pltpu.VMEM)


def in_hbm(count):
    return [pl.BlockSpec(memory_space=pltpu.HBM)] * count


def kept_in_hbm(*arrays):
    return [pltpu.with_memory_space_constraint(a, pltpu.HBM) for a in arrays]


def fetch(sems, *pairs):
    copies = [pltpu.make_async_copy(source, to, sems.at[at]) for at, (source, to) in enumerate(pairs)]
    for copy in copies:
        copy.start()
    return copies


def params():
    return pltpu.CompilerParams(vmem_limit_bytes=VMEM_LIMIT)


def segment_max(scores):
    low = lax.broadcasted_iota(jnp.int32, (1, 128), 1) < 64
    found = []
    for at in range(0, scores.shape[1], 128):
        v = scores[:, at : at + 128]
        first = jnp.max(jnp.where(low, v, -jnp.inf), axis=-1, keepdims=True)
        second = jnp.max(jnp.where(low, -jnp.inf, v), axis=-1, keepdims=True)
        found.append(jnp.where(low, first, second))
    return jnp.concatenate(found, axis=1)


def attention(grouped, wqkv_ref, wo_ref, mask_ref, proj, context, emit):
    mask = mask_ref[...]

    def one(half, carry):
        x = grouped[pl.ds(8 * half, 8)].reshape(512, CHANS).astype(F32)
        proj[...] = mm(layer_norm(x), wqkv_ref[...]).astype(BF16)
        for g in range(8):
            rows = slice(64 * g, 64 * g + 64)
            for at in range(0, CHANS, 128):
                query = proj[rows, at : at + 128]
                keys = jnp.concatenate([proj[rows, CHANS + at : CHANS + at + 128]] * 4, axis=0) * mask
                values = jnp.concatenate([proj[rows, 2 * CHANS + at : 2 * CHANS + at + 128]] * 4, axis=0) * mask
                scores = mm_nt(query, keys)
                weights = jnp.exp2((scores - segment_max(scores)) * SCALE_LOG2).astype(BF16)
                both = mm(weights, jnp.concatenate([values, mask], axis=1))
                context[rows, at : at + 128] = (both[:, :128] / both[:, 128:]).astype(BF16)
        emit(half, x + mm(context[...], wo_ref[...]))
        return carry

    lax.fori_loop(0, 2, one, 0, unroll=2)


def grid_kernel(x_ref, wqkv_hbm, wo_hbm, *rest):
    out_ref, grouped, proj, context, turn_ref, mask_ref, wqkv_ref, wo_ref, sems = rest[-9:]
    copies = fetch(sems, (wqkv_hbm, wqkv_ref), (wo_hbm, wo_ref))
    turn_ref[...] = turn_matrix()
    mask_ref[...] = head_mask()
    for t in range(4):
        moved = mm(turn_ref[...], x_ref[16 * t : 16 * t + 16].reshape(256, CHANS))
        grouped[:, 16 * t : 16 * t + 16] = moved.astype(BF16).reshape(16, 16, CHANS)

    def emit(half, rows):
        grouped[pl.ds(8 * half, 8)] = rows.astype(BF16).reshape(8, 64, CHANS)

    for copy in copies:
        copy.wait()
    attention(grouped, wqkv_ref, wo_ref, mask_ref, proj, context, emit)
    for t in range(4):
        moved = mm(turn_ref[...], grouped[:, 16 * t : 16 * t + 16].reshape(256, CHANS))
        moved = moved.astype(BF16).reshape(8, 2, 16, CHANS)
        if len(rest) == 9:
            out_ref[8 * t : 8 * t + 8] = moved
        else:
            out_ref[8 * t : 8 * t + 8, 1] = moved
    if len(rest) > 9:
        out_ref[:, 0] = rest[0][...]


def attention_scratch():
    return [
        pltpu.VMEM((16, 64, CHANS), BF16),
        pltpu.VMEM((512, 3 * CHANS), BF16),
        pltpu.VMEM((512, CHANS), BF16),
        pltpu.VMEM((256, 256), BF16),
        pltpu.VMEM((256, 128), BF16),
        pltpu.VMEM((CHANS, 3 * CHANS), BF16),
        pltpu.VMEM((CHANS, CHANS), BF16),
    ]


def grid_attention(x, qkv, out_proj, *earlier):
    shape = (32, 2, 2, 16, CHANS) if earlier else (32, 2, 16, CHANS)
    return pl.pallas_call(
        grid_kernel,
        in_specs=[in_vmem(), *in_hbm(2), *[in_vmem() for _ in earlier]],
        out_specs=in_vmem(),
        out_shape=jax.ShapeDtypeStruct(shape, BF16),
        scratch_shapes=[*attention_scratch(), pltpu.SemaphoreType.DMA((2,))],
        compiler_params=params(),
        cost_estimate=pl.CostEstimate(
            flops=8 * 1024 * CHANS * CHANS, bytes_accessed=4 * 2**20, transcendentals=2**20
        ),
        name="grid_attention",
    )(x, *kept_in_hbm(qkv, out_proj), *earlier)


def prepare_kernel(x_ref, _, normed_ref, xp_ref):
    spread = spread_matrix()
    for pair in range(4):
        moved = mm(spread, x_ref[:, 2 * pair : 2 * pair + 2].reshape(256, CHANS))
        xp_ref[256 * pair : 256 * pair + 256] = moved.astype(BF16)
        normed_ref[256 * pair : 256 * pair + 256] = layer_norm(moved)


def prepare(field, after):
    return pl.pallas_call(
        prepare_kernel,
        grid=(2,),
        in_specs=[
            pl.BlockSpec((2, 8, 64, CHANS), lambda k: (0, k, 0, 0)),
            pl.BlockSpec(memory_space=pl.ANY),
        ],
        out_specs=[pl.BlockSpec((1024, CHANS), lambda k: (k, 0))] * 2,
        out_shape=[pltpu.HBM((2048, CHANS), BF16)] * 2,
        compiler_params=params(),
        cost_estimate=pl.CostEstimate(flops=10**10, bytes_accessed=16 * 2**20, transcendentals=0),
        name="prepare",
    )(kept_in_hbm(field.reshape(2, 16, 64, CHANS))[0], after)


def local_kernel(
    part, rim_ref, left_ref, right_ref, normed_hbm, xp_hbm, we_hbm, dw_hbm, wp_hbm, wqkv_hbm, wo_hbm, out_ref,
    normed_ref, outer, special_ref, xp_ref, we_ref, dw_ref, wp_ref, pad, rim, spatial, acc,
    grouped, proj, context, turn_ref, mask_ref, wqkv_ref, wo_ref, sems,
):
    before, after = ((15, 8), (7, 0))[part]
    special, plain = ((before, after), (after, before))[part]
    plain_at = (128, 0)[part]
    first = fetch(
        sems.at[0],
        (normed_hbm.at[128 * special : 128 * special + 128], special_ref),
        (normed_hbm.at[1024 * part : 1024 * part + 1024], normed_ref),
        (normed_hbm.at[128 * plain : 128 * plain + 128], outer.at[plain_at : plain_at + 128]),
    )

    blocks = []
    for s in range(BLOCKS):
        lanes = slice(CB * s, CB * s + CB)
        blocks += fetch(
            sems.at[1 + s],
            (we_hbm.at[:, lanes], we_ref.at[s]),
            (dw_hbm.at[:, :, lanes], dw_ref.at[s]),
            (wp_hbm.at[lanes], wp_ref.at[s]),
        )
    turn_ref[...] = turn_matrix()
    mask_ref[...] = head_mask()
    outer[256:304] = layer_norm(left_ref[...].astype(F32))
    outer[304:352] = layer_norm(right_ref[...].astype(F32))
    acc[...] = jnp.zeros_like(acc)
    first[0].wait()
    source = jnp.concatenate([special_ref[...], layer_norm(rim_ref[...].astype(F32))], axis=0)
    outer[128 - plain_at : 256 - plain_at] = mm(edge_matrix(part), source).astype(BF16)
    for copy in (*first[1:], *blocks):
        copy.wait()
    last = fetch(
        sems.at[1 + BLOCKS],
        (xp_hbm.at[1024 * part : 1024 * part + 1024], xp_ref),
        (wqkv_hbm, wqkv_ref),
        (wo_hbm, wo_ref),
    )

    sub = lax.broadcasted_iota(jnp.int32, (8, CB), 0)

    def block(s, carry):
        for at in range(0, CB, 256):
            made = gelu(mm(normed_ref[...], we_ref[s, :, at : at + 256])).astype(BF16)
            pad[1:9, 1:9, :, at : at + 256] = made.reshape(8, 8, 16, 256)
            made = gelu(mm(outer[...], we_ref[s, :, at : at + 256])).astype(BF16)
            pad[0, 1:9, :, at : at + 256] = made[0:128].reshape(8, 16, 256)
            pad[9, 1:9, :, at : at + 256] = made[128:256].reshape(8, 16, 256)
            rim[:, at : at + 256] = made[256:352].astype(F32)
        for row in range(10):
            at = 8 * part + row
            far = pad[row, 8].astype(F32)
            near = pad[row, 1].astype(F32)
            west, east = [], []
            for b in range(2):
                turned = pltpu.roll(far[8 * b : 8 * b + 8], 1, 0)
                west.append(jnp.where(sub == 0, rim[at + 16 * b : at + 16 * b + 1], turned))
                turned = pltpu.roll(near[8 * b : 8 * b + 8], 7, 0)
                east.append(jnp.where(sub == 7, rim[at + 48 + 16 * b : at + 48 + 16 * b + 1], turned))
            pad[row, 0] = jnp.concatenate(west, axis=0).astype(BF16)
            pad[row, 9] = jnp.concatenate(east, axis=0).astype(BF16)

        taps = [[jnp.broadcast_to(dw_ref[s, a, b : b + 1].astype(BF16), (16, CB)) for b in range(3)] for a in range(3)]

        def pair_of_rows(pair, carry):
            for i in range(2):
                for j in range(8):
                    sums = [
                        pad[2 * pair + i + a, j] * taps[a][0]
                        + pad[2 * pair + i + a, j + 1] * taps[a][1]
                        + pad[2 * pair + i + a, j + 2] * taps[a][2]
                        for a in range(3)
                    ]
                    total = sums[0] + sums[1] + sums[2]
                    spatial[2 * pair + i, j] = gelu(total)
            rows = pl.ds(pl.multiple_of(256 * pair, 256), 256)
            acc[rows] += mm(spatial[pl.ds(2 * pair, 2)].reshape(256, CB), wp_ref[s])
            return carry

        lax.fori_loop(0, 4, pair_of_rows, 0, unroll=PAIRS)
        return carry

    lax.fori_loop(0, BLOCKS, block, 0)
    for copy in last:
        copy.wait()
    for pair in range(4):
        rows = slice(256 * pair, 256 * pair + 256)
        mixed = (xp_ref[rows].astype(F32) + acc[rows]).astype(BF16)
        grouped[:, 16 * pair : 16 * pair + 16] = mm(turn_ref[...], mixed).astype(BF16).reshape(16, 16, CHANS)

    def emit(half, rows):
        rows = rows.reshape(4, 2, 8, 8, CHANS)
        for i in range(8):
            out_ref[i, :, half] = rows[:, :, i].reshape(4, 16, CHANS).astype(BF16)

    attention(grouped, wqkv_ref, wo_ref, mask_ref, proj, context, emit)


def local_part(part, rims, *arrays):
    top, bottom, left, right = rims
    return pl.pallas_call(
        functools.partial(local_kernel, part),
        in_specs=[*[in_vmem() for _ in range(3)], *in_hbm(len(arrays))],
        out_specs=in_vmem(),
        out_shape=jax.ShapeDtypeStruct((8, 4, 2, 16, CHANS), BF16),
        scratch_shapes=[
            pltpu.VMEM((1024, CHANS), BF16),
            pltpu.VMEM((352, CHANS), BF16),
            pltpu.VMEM((128, CHANS), BF16),
            pltpu.VMEM((1024, CHANS), BF16),
            pltpu.VMEM((BLOCKS, CHANS, CB), BF16),
            pltpu.VMEM((BLOCKS, 3, 3, CB), F32),
            pltpu.VMEM((BLOCKS, CB, CHANS), BF16),
            pltpu.VMEM((10, 10, 16, CB), BF16),
            pltpu.VMEM((96, CB), F32),
            pltpu.VMEM((8, 8, 16, CB), BF16),
            pltpu.VMEM((1024, CHANS), F32),
            *attention_scratch(),
            pltpu.SemaphoreType.DMA((2 + BLOCKS, 3)),
        ],
        compiler_params=params(),
        cost_estimate=pl.CostEstimate(
            flops=4 * 1024 * CHANS * WIDE, bytes_accessed=8 * 2**20, transcendentals=2048 * WIDE
        ),
        name="local_part",
    )((top, bottom)[part], left, right, *kept_in_hbm(*arrays))


def exchange(blocks, groups):
    return lax.all_to_all(blocks, ("row", "col"), 0, 0, axis_index_groups=groups, tiled=True)


def on_device(field, w_expand, dw_kernel, w_project, qkv_block, out_block, qkv_grid, out_grid):
    n_row, n_col = lax.axis_size("row"), lax.axis_size("col")
    down = [(i, i + 1) for i in range(n_row - 1)]
    up = [(i + 1, i) for i in range(n_row - 1)]
    top = lax.ppermute(field[31], "row", down)
    bottom = lax.ppermute(field[0], "row", up)
    fill = jnp.zeros((14, CHANS), BF16)

    def rim(column):
        return jnp.concatenate([top[column : column + 1], field[:, column], bottom[column : column + 1], fill], axis=0)

    east, west = rim(63), rim(0)
    left = lax.ppermute(east, "col", [(i, i + 1) for i in range(n_col - 1)])
    right = lax.ppermute(west, "col", [(i + 1, i) for i in range(n_col - 1)])
    normed, xp = prepare(field, east)
    groups = [[32 * row + 4 * j + c for row in range(n_row) for j in range(8)] for c in range(4)]
    gathered = []
    for part in range(2):
        blocked = local_part(
            part, (top, bottom, left, right), normed, xp, w_expand, dw_kernel, w_project, qkv_block, out_block
        )
        gathered.append(exchange(blocked.reshape(32, 2, 16, CHANS), groups).reshape(64, 16, CHANS))
    attended = grid_attention(gathered[0], qkv_grid, out_grid)
    attended = grid_attention(gathered[1], qkv_grid, out_grid, attended)
    home = exchange(attended, groups).reshape(8, 4, 2, 2, 16, CHANS)
    return home.transpose(3, 2, 0, 1, 4, 5).reshape(32, 64, CHANS)


def solution(mesh):
    placed = (P("row", "col", None), P(), P(), P(), P(), P(), P(), P())
    return jax.shard_map(
        on_device, mesh=mesh, in_specs=placed, out_specs=P("row", "col", None), check_vma=False
    )
```

```python
import functools

import jax
import jax.numpy as jnp
import numpy as np
from jax import lax
from jax.experimental import pallas as pl
from jax.experimental.pallas import tpu as pltpu
from jax.sharding import PartitionSpec as P

BF16 = jnp.bfloat16
F32 = jnp.float32
HEAD = 32
CHANS = 512
WIDE = 2048
CB = 1024
BLOCKS = WIDE // CB
PAIRS = 4
VMEM_LIMIT = 36 * 2**20
SCALE_LOG2 = float(HEAD**-0.5 * np.log2(np.e))


def layer_norm(v):
    mean = jnp.mean(v, axis=-1, keepdims=True)
    cent = v - mean
    var = jnp.mean(cent * cent, axis=-1, keepdims=True)
    return (cent * lax.rsqrt(var + 1e-05)).astype(BF16)


def gelu(v):
    half = 0.5 * v
    return half + half * lax.erf(v * 0.7071067811865476)


def mm(a, b):
    return lax.dot_general(a, b, (((1,), (0,)), ((), ())), preferred_element_type=F32)


def mm_nt(a, b):
    return lax.dot_general(a, b, (((1,), (1,)), ((), ())), preferred_element_type=F32)


def ones_where(shape, holds):
    row = lax.broadcasted_iota(jnp.int32, shape, 0)
    column = lax.broadcasted_iota(jnp.int32, shape, 1)
    return jnp.where(holds(row, column), 1.0, 0.0).astype(BF16)


def spread_matrix():
    return ones_where(
        (256, 256),
        lambda r, c: c == ((r >> 3) & 1) * 128 + (r >> 7) * 64 + (r & 7) * 8 + ((r >> 4) & 7),
    )


def turn_matrix():
    return ones_where((256, 256), lambda r, c: c == (r & 15) * 16 + (r >> 4))


def edge_matrix(part):
    def holds(r, c):
        j, b, q = r >> 4, (r >> 3) & 1, r & 7
        own = c == j * 16 + 8 * part + q
        rim = c == 128 + q * 8 + j
        return (own & (b == 1 - part)) | (rim & (b == part))

    return ones_where((128, 192), holds)


def head_mask():
    return ones_where((256, 128), lambda r, c: (r >> 6) == (c >> 5))


def in_vmem():
    return pl.BlockSpec(memory_space=pltpu.VMEM)


def in_hbm(count):
    return [pl.BlockSpec(memory_space=pltpu.HBM)] * count


def kept_in_hbm(*arrays):
    return [pltpu.with_memory_space_constraint(a, pltpu.HBM) for a in arrays]


def fetch(sems, *pairs):
    copies = [pltpu.make_async_copy(source, to, sems.at[at]) for at, (source, to) in enumerate(pairs)]
    for copy in copies:
        copy.start()
    return copies


def params():
    return pltpu.CompilerParams(vmem_limit_bytes=VMEM_LIMIT)


def segment_max(scores):
    low = lax.broadcasted_iota(jnp.int32, (1, 128), 1) < 64
    found = []
    for at in range(0, scores.shape[1], 128):
        v = scores[:, at : at + 128]
        first = jnp.max(jnp.where(low, v, -jnp.inf), axis=-1, keepdims=True)
        second = jnp.max(jnp.where(low, -jnp.inf, v), axis=-1, keepdims=True)
        found.append(jnp.where(low, first, second))
    return jnp.concatenate(found, axis=1)


def attention(grouped, wqkv_ref, wo_ref, mask_ref, proj, context, emit, unroll):
    mask = mask_ref[...]

    def one(half, carry):
        x = grouped[pl.ds(8 * half, 8)].reshape(512, CHANS).astype(F32)
        proj[...] = mm(layer_norm(x), wqkv_ref[...]).astype(BF16)
        for g in range(8):
            rows = slice(64 * g, 64 * g + 64)
            for at in range(0, CHANS, 128):
                query = proj[rows, at : at + 128]
                keys = jnp.concatenate([proj[rows, CHANS + at : CHANS + at + 128]] * 4, axis=0) * mask
                values = jnp.concatenate([proj[rows, 2 * CHANS + at : 2 * CHANS + at + 128]] * 4, axis=0) * mask
                scores = mm_nt(query, keys)
                weights = jnp.exp2((scores - segment_max(scores)) * SCALE_LOG2).astype(BF16)
                both = mm(weights, jnp.concatenate([values, mask], axis=1))
                context[rows, at : at + 128] = (both[:, :128] / both[:, 128:]).astype(BF16)
        emit(half, x + mm(context[...], wo_ref[...]))
        return carry

    lax.fori_loop(0, 2, one, 0, unroll=unroll)


def grid_kernel(x_ref, wqkv_hbm, wo_hbm, *rest):
    out_ref, grouped, proj, context, turn_ref, mask_ref, wqkv_ref, wo_ref, sems = rest[-9:]
    copies = fetch(sems, (wqkv_hbm, wqkv_ref), (wo_hbm, wo_ref))
    turn_ref[...] = turn_matrix()
    mask_ref[...] = head_mask()
    for t in range(4):
        moved = mm(turn_ref[...], x_ref[16 * t : 16 * t + 16].reshape(256, CHANS))
        grouped[:, 16 * t : 16 * t + 16] = moved.astype(BF16).reshape(16, 16, CHANS)

    def emit(half, rows):
        grouped[pl.ds(8 * half, 8)] = rows.astype(BF16).reshape(8, 64, CHANS)

    for copy in copies:
        copy.wait()
    attention(grouped, wqkv_ref, wo_ref, mask_ref, proj, context, emit, 2)
    for t in range(4):
        moved = mm(turn_ref[...], grouped[:, 16 * t : 16 * t + 16].reshape(256, CHANS))
        moved = moved.astype(BF16).reshape(8, 2, 16, CHANS)
        if len(rest) == 9:
            out_ref[8 * t : 8 * t + 8] = moved
        else:
            out_ref[8 * t : 8 * t + 8, 1] = moved
    if len(rest) > 9:
        out_ref[:, 0] = rest[0][...]


def attention_scratch():
    return [
        pltpu.VMEM((16, 64, CHANS), BF16),
        pltpu.VMEM((512, 3 * CHANS), BF16),
        pltpu.VMEM((512, CHANS), BF16),
        pltpu.VMEM((256, 256), BF16),
        pltpu.VMEM((256, 128), BF16),
        pltpu.VMEM((CHANS, 3 * CHANS), BF16),
        pltpu.VMEM((CHANS, CHANS), BF16),
    ]


def grid_attention(x, qkv, out_proj, *earlier):
    shape = (32, 2, 2, 16, CHANS) if earlier else (32, 2, 16, CHANS)
    return pl.pallas_call(
        grid_kernel,
        in_specs=[in_vmem(), *in_hbm(2), *[in_vmem() for _ in earlier]],
        out_specs=in_vmem(),
        out_shape=jax.ShapeDtypeStruct(shape, BF16),
        scratch_shapes=[*attention_scratch(), pltpu.SemaphoreType.DMA((2,))],
        compiler_params=params(),
        cost_estimate=pl.CostEstimate(
            flops=8 * 1024 * CHANS * CHANS, bytes_accessed=4 * 2**20, transcendentals=2**20
        ),
        name="grid_attention",
    )(x, *kept_in_hbm(qkv, out_proj), *earlier)


def prepare_kernel(x_ref, _, normed_ref, xp_ref):
    spread = spread_matrix()
    for pair in range(4):
        moved = mm(spread, x_ref[:, 2 * pair : 2 * pair + 2].reshape(256, CHANS))
        xp_ref[256 * pair : 256 * pair + 256] = moved.astype(BF16)
        normed_ref[256 * pair : 256 * pair + 256] = layer_norm(moved)


def prepare(field, after):
    return pl.pallas_call(
        prepare_kernel,
        grid=(2,),
        in_specs=[
            pl.BlockSpec((2, 8, 64, CHANS), lambda k: (0, k, 0, 0)),
            pl.BlockSpec(memory_space=pl.ANY),
        ],
        out_specs=[pl.BlockSpec((1024, CHANS), lambda k: (k, 0))] * 2,
        out_shape=[pltpu.HBM((2048, CHANS), BF16)] * 2,
        compiler_params=params(),
        cost_estimate=pl.CostEstimate(flops=10**10, bytes_accessed=16 * 2**20, transcendentals=0),
        name="prepare",
    )(kept_in_hbm(field.reshape(2, 16, 64, CHANS))[0], after)


def local_kernel(
    part, rim_ref, left_ref, right_ref, normed_hbm, xp_hbm, we_hbm, dw_hbm, wp_hbm, wqkv_hbm, wo_hbm, out_ref,
    normed_ref, outer, special_ref, xp_ref, we_ref, dw_ref, wp_ref, pad, rim, spatial, acc,
    grouped, proj, context, turn_ref, mask_ref, wqkv_ref, wo_ref, sems,
):
    before, after = ((15, 8), (7, 0))[part]
    special, plain = ((before, after), (after, before))[part]
    plain_at = (128, 0)[part]
    first = fetch(
        sems.at[0],
        (normed_hbm.at[128 * special : 128 * special + 128], special_ref),
        (normed_hbm.at[1024 * part : 1024 * part + 1024], normed_ref),
        (normed_hbm.at[128 * plain : 128 * plain + 128], outer.at[plain_at : plain_at + 128]),
    )


    def fetch_block(s):
        lanes = slice(CB * s, CB * s + CB)
        return fetch(
            sems.at[1 + s],
            (we_hbm.at[:, lanes], we_ref.at[s]),
            (dw_hbm.at[:, :, lanes], dw_ref.at[s]),
            (wp_hbm.at[lanes], wp_ref.at[s]),
        )

    blocks = [fetch_block(0)]
    turn_ref[...] = turn_matrix()
    mask_ref[...] = head_mask()
    outer[256:304] = layer_norm(left_ref[...].astype(F32))
    outer[304:352] = layer_norm(right_ref[...].astype(F32))
    acc[...] = jnp.zeros_like(acc)
    first[0].wait()
    source = jnp.concatenate([special_ref[...], layer_norm(rim_ref[...].astype(F32))], axis=0)
    outer[128 - plain_at : 256 - plain_at] = mm(edge_matrix(part), source).astype(BF16)
    for copy in first[1:]:
        copy.wait()

    sub = lax.broadcasted_iota(jnp.int32, (8, CB), 0)

    def block(s):
        blocks[s][0].wait()
        for at in range(0, CB, 256):
            made = gelu(mm(normed_ref[...], we_ref[s, :, at : at + 256]).astype(BF16))
            pad[1:9, 1:9, :, at : at + 256] = made.reshape(8, 8, 16, 256)
            made = gelu(mm(outer[...], we_ref[s, :, at : at + 256]).astype(BF16))
            pad[0, 1:9, :, at : at + 256] = made[0:128].reshape(8, 16, 256)
            pad[9, 1:9, :, at : at + 256] = made[128:256].reshape(8, 16, 256)
            rim[:, at : at + 256] = made[256:352].astype(F32)
        for row in range(10):
            at = 8 * part + row
            far = pad[row, 8].astype(F32)
            near = pad[row, 1].astype(F32)
            west, east = [], []
            for b in range(2):
                turned = pltpu.roll(far[8 * b : 8 * b + 8], 1, 0)
                west.append(jnp.where(sub == 0, rim[at + 16 * b : at + 16 * b + 1], turned))
                turned = pltpu.roll(near[8 * b : 8 * b + 8], 7, 0)
                east.append(jnp.where(sub == 7, rim[at + 48 + 16 * b : at + 48 + 16 * b + 1], turned))
            pad[row, 0] = jnp.concatenate(west, axis=0).astype(BF16)
            pad[row, 9] = jnp.concatenate(east, axis=0).astype(BF16)

        if s + 1 < BLOCKS:
            blocks.append(fetch_block(s + 1))
        for copy in blocks[s][1:]:
            copy.wait()
        taps = [[jnp.broadcast_to(dw_ref[s, a, b : b + 1].astype(BF16), (16, CB)) for b in range(3)] for a in range(3)]

        def pair_of_rows(pair, carry):
            for i in range(2):
                for j in range(8):
                    sums = [
                        pad[2 * pair + i + a, j] * taps[a][0]
                        + pad[2 * pair + i + a, j + 1] * taps[a][1]
                        + pad[2 * pair + i + a, j + 2] * taps[a][2]
                        for a in range(3)
                    ]
                    total = sums[0] + sums[1] + sums[2]
                    spatial[2 * pair + i, j] = gelu(total)
            rows = pl.ds(pl.multiple_of(256 * pair, 256), 256)
            acc[rows] += mm(spatial[pl.ds(2 * pair, 2)].reshape(256, CB), wp_ref[s])
            return carry

        lax.fori_loop(0, 4, pair_of_rows, 0, unroll=PAIRS)

    for s in range(BLOCKS):
        if s == BLOCKS - 1:
            last = fetch(
                sems.at[1 + BLOCKS],
                (xp_hbm.at[1024 * part : 1024 * part + 1024], xp_ref),
                (wqkv_hbm, wqkv_ref),
                (wo_hbm, wo_ref),
            )
        block(s)
    for copy in last:
        copy.wait()
    for pair in range(4):
        rows = slice(256 * pair, 256 * pair + 256)
        mixed = (xp_ref[rows].astype(F32) + acc[rows]).astype(BF16)
        grouped[:, 16 * pair : 16 * pair + 16] = mm(turn_ref[...], mixed).astype(BF16).reshape(16, 16, CHANS)

    def emit(half, rows):
        rows = rows.reshape(4, 2, 8, 8, CHANS)
        for i in range(8):
            out_ref[i, :, half] = rows[:, :, i].reshape(4, 16, CHANS).astype(BF16)

    attention(grouped, wqkv_ref, wo_ref, mask_ref, proj, context, emit, 1)


def local_part(part, rims, *arrays):
    top, bottom, left, right = rims
    return pl.pallas_call(
        functools.partial(local_kernel, part),
        in_specs=[*[in_vmem() for _ in range(3)], *in_hbm(len(arrays))],
        out_specs=in_vmem(),
        out_shape=jax.ShapeDtypeStruct((8, 4, 2, 16, CHANS), BF16),
        scratch_shapes=[
            pltpu.VMEM((1024, CHANS), BF16),
            pltpu.VMEM((352, CHANS), BF16),
            pltpu.VMEM((128, CHANS), BF16),
            pltpu.VMEM((1024, CHANS), BF16),
            pltpu.VMEM((BLOCKS, CHANS, CB), BF16),
            pltpu.VMEM((BLOCKS, 3, 3, CB), F32),
            pltpu.VMEM((BLOCKS, CB, CHANS), BF16),
            pltpu.VMEM((10, 10, 16, CB), BF16),
            pltpu.VMEM((96, CB), F32),
            pltpu.VMEM((8, 8, 16, CB), BF16),
            pltpu.VMEM((1024, CHANS), F32),
            *attention_scratch(),
            pltpu.SemaphoreType.DMA((2 + BLOCKS, 3)),
        ],
        compiler_params=params(),
        cost_estimate=pl.CostEstimate(
            flops=4 * 1024 * CHANS * WIDE, bytes_accessed=8 * 2**20, transcendentals=2048 * WIDE
        ),
        name="local_part",
    )((top, bottom)[part], left, right, *kept_in_hbm(*arrays))


def exchange(blocks, groups):
    return lax.all_to_all(blocks, ("row", "col"), 0, 0, axis_index_groups=groups, tiled=True)


def on_device(field, w_expand, dw_kernel, w_project, qkv_block, out_block, qkv_grid, out_grid):
    n_row, n_col = lax.axis_size("row"), lax.axis_size("col")
    down = [(i, i + 1) for i in range(n_row - 1)]
    up = [(i + 1, i) for i in range(n_row - 1)]
    top = lax.ppermute(field[31], "row", down)
    bottom = lax.ppermute(field[0], "row", up)
    fill = jnp.zeros((14, CHANS), BF16)

    def rim(column):
        return jnp.concatenate([top[column : column + 1], field[:, column], bottom[column : column + 1], fill], axis=0)

    east, west = rim(63), rim(0)
    left = lax.ppermute(east, "col", [(i, i + 1) for i in range(n_col - 1)])
    right = lax.ppermute(west, "col", [(i + 1, i) for i in range(n_col - 1)])
    normed, xp = prepare(field, east)
    groups = [[32 * row + 4 * j + c for row in range(n_row) for j in range(8)] for c in range(4)]
    gathered = []
    for part in range(2):
        blocked = local_part(
            part, (top, bottom, left, right), normed, xp, w_expand, dw_kernel, w_project, qkv_block, out_block
        )
        gathered.append(exchange(blocked.reshape(32, 2, 16, CHANS), groups).reshape(64, 16, CHANS))
    attended = grid_attention(gathered[0], qkv_grid, out_grid)
    attended = grid_attention(gathered[1], qkv_grid, out_grid, attended)
    home = exchange(attended, groups).reshape(8, 4, 2, 2, 16, CHANS)
    return home.transpose(3, 2, 0, 1, 4, 5).reshape(32, 64, CHANS)


def solution(mesh):
    placed = (P("row", "col", None), P(), P(), P(), P(), P(), P(), P())
    return jax.shard_map(
        on_device, mesh=mesh, in_specs=placed, out_specs=P("row", "col", None), check_vma=False
    )
```

```python
import functools

import jax
import jax.numpy as jnp
import numpy as np
from jax import lax
from jax.experimental import pallas as pl
from jax.experimental.pallas import tpu as pltpu
from jax.sharding import PartitionSpec as P

BF16 = jnp.bfloat16
F32 = jnp.float32
HEAD = 32
CHANS = 512
WIDE = 2048
CB = 1024
BLOCKS = WIDE // CB
PAIRS = 4
VMEM_LIMIT = 36 * 2**20
SCALE_LOG2 = float(HEAD**-0.5 * np.log2(np.e))


def layer_norm(v):
    mean = jnp.mean(v, axis=-1, keepdims=True)
    cent = v - mean
    var = jnp.mean(cent * cent, axis=-1, keepdims=True)
    return (cent * lax.rsqrt(var + 1e-05)).astype(BF16)


def gelu(v):
    half = 0.5 * v
    return half + half * lax.erf(v * 0.7071067811865476)


def mm(a, b):
    return lax.dot_general(a, b, (((1,), (0,)), ((), ())), preferred_element_type=F32)


def mm_nt(a, b):
    return lax.dot_general(a, b, (((1,), (1,)), ((), ())), preferred_element_type=F32)


def ones_where(shape, holds):
    row = lax.broadcasted_iota(jnp.int32, shape, 0)
    column = lax.broadcasted_iota(jnp.int32, shape, 1)
    return jnp.where(holds(row, column), 1.0, 0.0).astype(BF16)


def spread_matrix():
    return ones_where(
        (256, 256),
        lambda r, c: c == ((r >> 3) & 1) * 128 + (r >> 7) * 64 + (r & 7) * 8 + ((r >> 4) & 7),
    )


def turn_matrix():
    return ones_where((256, 256), lambda r, c: c == (r & 15) * 16 + (r >> 4))


def edge_matrix(part):
    def holds(r, c):
        j, b, q = r >> 4, (r >> 3) & 1, r & 7
        own = c == j * 16 + 8 * part + q
        rim = c == 128 + q * 8 + j
        return (own & (b == 1 - part)) | (rim & (b == part))

    return ones_where((128, 192), holds)


def head_mask():
    return ones_where((256, 128), lambda r, c: (r >> 6) == (c >> 5))


def in_vmem():
    return pl.BlockSpec(memory_space=pltpu.VMEM)


def in_hbm(count):
    return [pl.BlockSpec(memory_space=pltpu.HBM)] * count


def kept_in_hbm(*arrays):
    return [pltpu.with_memory_space_constraint(a, pltpu.HBM) for a in arrays]


def fetch(sems, *pairs):
    copies = [pltpu.make_async_copy(source, to, sems.at[at]) for at, (source, to) in enumerate(pairs)]
    for copy in copies:
        copy.start()
    return copies


def params():
    return pltpu.CompilerParams(vmem_limit_bytes=VMEM_LIMIT)


def segment_max(scores):
    low = lax.broadcasted_iota(jnp.int32, (1, 128), 1) < 64
    found = []
    for at in range(0, scores.shape[1], 128):
        v = scores[:, at : at + 128]
        first = jnp.max(jnp.where(low, v, -jnp.inf), axis=-1, keepdims=True)
        second = jnp.max(jnp.where(low, -jnp.inf, v), axis=-1, keepdims=True)
        found.append(jnp.where(low, first, second))
    return jnp.concatenate(found, axis=1)


def attention(grouped, wqkv_ref, wo_ref, mask_ref, proj, context, emit, unroll):
    mask = mask_ref[...]

    def one(half, carry):
        x = grouped[pl.ds(8 * half, 8)].reshape(512, CHANS).astype(F32)
        proj[...] = mm(layer_norm(x), wqkv_ref[...]).astype(BF16)
        for g in range(8):
            rows = slice(64 * g, 64 * g + 64)
            for at in range(0, CHANS, 128):
                query = proj[rows, at : at + 128]
                keys = jnp.concatenate([proj[rows, CHANS + at : CHANS + at + 128]] * 4, axis=0) * mask
                values = jnp.concatenate([proj[rows, 2 * CHANS + at : 2 * CHANS + at + 128]] * 4, axis=0) * mask
                scores = mm_nt(query, keys)
                weights = jnp.exp2((scores - segment_max(scores)) * SCALE_LOG2).astype(BF16)
                both = mm(weights, jnp.concatenate([values, mask], axis=1))
                context[rows, at : at + 128] = (both[:, :128] / both[:, 128:]).astype(BF16)
        emit(half, x + mm(context[...], wo_ref[...]))
        return carry

    lax.fori_loop(0, 2, one, 0, unroll=unroll)


def grid_kernel(x_ref, wqkv_hbm, wo_hbm, *rest):
    out_ref, grouped, proj, context, turn_ref, mask_ref, wqkv_ref, wo_ref, sems = rest[-9:]
    copies = fetch(sems, (wqkv_hbm, wqkv_ref), (wo_hbm, wo_ref))
    turn_ref[...] = turn_matrix()
    mask_ref[...] = head_mask()
    for t in range(4):
        moved = mm(turn_ref[...], x_ref[16 * t : 16 * t + 16].reshape(256, CHANS))
        grouped[:, 16 * t : 16 * t + 16] = moved.astype(BF16).reshape(16, 16, CHANS)

    def emit(half, rows):
        grouped[pl.ds(8 * half, 8)] = rows.astype(BF16).reshape(8, 64, CHANS)

    for copy in copies:
        copy.wait()
    attention(grouped, wqkv_ref, wo_ref, mask_ref, proj, context, emit, 2)
    for t in range(4):
        moved = mm(turn_ref[...], grouped[:, 16 * t : 16 * t + 16].reshape(256, CHANS))
        moved = moved.astype(BF16).reshape(8, 2, 16, CHANS)
        if len(rest) == 9:
            out_ref[8 * t : 8 * t + 8] = moved
        else:
            out_ref[8 * t : 8 * t + 8, 1] = moved
    if len(rest) > 9:
        out_ref[:, 0] = rest[0][...]


def attention_scratch():
    return [
        pltpu.VMEM((16, 64, CHANS), BF16),
        pltpu.VMEM((512, 3 * CHANS), BF16),
        pltpu.VMEM((512, CHANS), BF16),
        pltpu.VMEM((256, 256), BF16),
        pltpu.VMEM((256, 128), BF16),
        pltpu.VMEM((CHANS, 3 * CHANS), BF16),
        pltpu.VMEM((CHANS, CHANS), BF16),
    ]


def grid_attention(x, qkv, out_proj, *earlier):
    shape = (32, 2, 2, 16, CHANS) if earlier else (32, 2, 16, CHANS)
    return pl.pallas_call(
        grid_kernel,
        in_specs=[in_vmem(), *in_hbm(2), *[in_vmem() for _ in earlier]],
        out_specs=in_vmem(),
        out_shape=jax.ShapeDtypeStruct(shape, BF16),
        scratch_shapes=[*attention_scratch(), pltpu.SemaphoreType.DMA((2,))],
        compiler_params=params(),
        cost_estimate=pl.CostEstimate(
            flops=8 * 1024 * CHANS * CHANS, bytes_accessed=4 * 2**20, transcendentals=2**20
        ),
        name="grid_attention",
    )(x, *kept_in_hbm(qkv, out_proj), *earlier)


def prepare_kernel(x_ref, _, normed_ref, xp_ref):
    spread = spread_matrix()
    for pair in range(4):
        moved = mm(spread, x_ref[:, 2 * pair : 2 * pair + 2].reshape(256, CHANS))
        xp_ref[256 * pair : 256 * pair + 256] = moved.astype(BF16)
        normed_ref[256 * pair : 256 * pair + 256] = layer_norm(moved)


def prepare(field, after):
    return pl.pallas_call(
        prepare_kernel,
        grid=(2,),
        in_specs=[
            pl.BlockSpec((2, 8, 64, CHANS), lambda k: (0, k, 0, 0)),
            pl.BlockSpec(memory_space=pl.ANY),
        ],
        out_specs=[pl.BlockSpec((1024, CHANS), lambda k: (k, 0))] * 2,
        out_shape=[pltpu.HBM((2048, CHANS), BF16)] * 2,
        compiler_params=params(),
        cost_estimate=pl.CostEstimate(flops=10**10, bytes_accessed=16 * 2**20, transcendentals=0),
        name="prepare",
    )(kept_in_hbm(field.reshape(2, 16, 64, CHANS))[0], after)


def local_kernel(
    part, rim_ref, left_ref, right_ref, normed_hbm, xp_hbm, we_hbm, dw_hbm, wp_hbm, wqkv_hbm, wo_hbm, out_ref,
    normed_ref, outer, special_ref, xp_ref, we_ref, dw_ref, wp_ref, pad, rim, spatial, acc,
    grouped, proj, context, turn_ref, mask_ref, wqkv_ref, wo_ref, sems,
):
    before, after = ((15, 8), (7, 0))[part]
    special, plain = ((before, after), (after, before))[part]
    plain_at = (128, 0)[part]
    first = fetch(
        sems.at[0],
        (normed_hbm.at[128 * special : 128 * special + 128], special_ref),
        (normed_hbm.at[1024 * part : 1024 * part + 1024], normed_ref),
        (normed_hbm.at[128 * plain : 128 * plain + 128], outer.at[plain_at : plain_at + 128]),
    )


    def fetch_block(s):
        lanes = slice(CB * s, CB * s + CB)
        return fetch(
            sems.at[1 + s],
            (we_hbm.at[:, lanes], we_ref.at[s]),
            (dw_hbm.at[:, :, lanes], dw_ref.at[s]),
            (wp_hbm.at[lanes], wp_ref.at[s]),
        )

    blocks = [fetch_block(0)]
    turn_ref[...] = turn_matrix()
    mask_ref[...] = head_mask()
    outer[256:304] = layer_norm(left_ref[...].astype(F32))
    outer[304:352] = layer_norm(right_ref[...].astype(F32))
    acc[...] = jnp.zeros_like(acc)
    first[0].wait()
    source = jnp.concatenate([special_ref[...], layer_norm(rim_ref[...].astype(F32))], axis=0)
    outer[128 - plain_at : 256 - plain_at] = mm(edge_matrix(part), source).astype(BF16)
    for copy in first[1:]:
        copy.wait()

    sub = lax.broadcasted_iota(jnp.int32, (8, CB), 0)

    def block(s):
        blocks[s][0].wait()
        for at in range(0, CB, 256):
            made = gelu(mm(normed_ref[...], we_ref[s, :, at : at + 256]).astype(BF16))
            pad[1:9, 1:9, :, at : at + 256] = made.reshape(8, 8, 16, 256)
            made = gelu(mm(outer[...], we_ref[s, :, at : at + 256]).astype(BF16))
            pad[0, 1:9, :, at : at + 256] = made[0:128].reshape(8, 16, 256)
            pad[9, 1:9, :, at : at + 256] = made[128:256].reshape(8, 16, 256)
            rim[:, at : at + 256] = made[256:352].astype(F32)
        for row in range(10):
            at = 8 * part + row
            far = pad[row, 8].astype(F32)
            near = pad[row, 1].astype(F32)
            west, east = [], []
            for b in range(2):
                turned = pltpu.roll(far[8 * b : 8 * b + 8], 1, 0)
                west.append(jnp.where(sub == 0, rim[at + 16 * b : at + 16 * b + 1], turned))
                turned = pltpu.roll(near[8 * b : 8 * b + 8], 7, 0)
                east.append(jnp.where(sub == 7, rim[at + 48 + 16 * b : at + 48 + 16 * b + 1], turned))
            pad[row, 0] = jnp.concatenate(west, axis=0).astype(BF16)
            pad[row, 9] = jnp.concatenate(east, axis=0).astype(BF16)

        if s + 1 < BLOCKS:
            blocks.append(fetch_block(s + 1))
        for copy in blocks[s][1:]:
            copy.wait()
        taps = [[jnp.broadcast_to(dw_ref[s, a, b : b + 1].astype(BF16), (16, CB)) for b in range(3)] for a in range(3)]

        def pair_of_rows(pair, carry):
            for i in range(2):
                for j in range(8):
                    sums = [
                        pad[2 * pair + i + a, j] * taps[a][0]
                        + pad[2 * pair + i + a, j + 1] * taps[a][1]
                        + pad[2 * pair + i + a, j + 2] * taps[a][2]
                        for a in range(3)
                    ]
                    total = sums[0] + sums[1] + sums[2]
                    spatial[2 * pair + i, j] = gelu(total)
            rows = pl.ds(pl.multiple_of(256 * pair, 256), 256)
            acc[rows] += mm(spatial[pl.ds(2 * pair, 2)].reshape(256, CB), wp_ref[s])
            return carry

        lax.fori_loop(0, 4, pair_of_rows, 0, unroll=PAIRS)

    for s in range(BLOCKS):
        if s == BLOCKS - 1:
            last = fetch(
                sems.at[1 + BLOCKS],
                (xp_hbm.at[1024 * part : 1024 * part + 1024], xp_ref),
                (wqkv_hbm, wqkv_ref),
                (wo_hbm, wo_ref),
            )
        block(s)
    for copy in last:
        copy.wait()
    for pair in range(4):
        rows = slice(256 * pair, 256 * pair + 256)
        mixed = (xp_ref[rows].astype(F32) + acc[rows]).astype(BF16)
        grouped[:, 16 * pair : 16 * pair + 16] = mm(turn_ref[...], mixed).astype(BF16).reshape(16, 16, CHANS)

    def emit(half, rows):
        rows = rows.reshape(4, 2, 8, 8, CHANS)
        for i in range(8):
            out_ref[i, :, half] = rows[:, :, i].reshape(4, 16, CHANS).astype(BF16)

    attention(grouped, wqkv_ref, wo_ref, mask_ref, proj, context, emit, 2)


def local_part(part, rims, *arrays):
    top, bottom, left, right = rims
    return pl.pallas_call(
        functools.partial(local_kernel, part),
        in_specs=[*[in_vmem() for _ in range(3)], *in_hbm(len(arrays))],
        out_specs=in_vmem(),
        out_shape=jax.ShapeDtypeStruct((8, 4, 2, 16, CHANS), BF16),
        scratch_shapes=[
            pltpu.VMEM((1024, CHANS), BF16),
            pltpu.VMEM((352, CHANS), BF16),
            pltpu.VMEM((128, CHANS), BF16),
            pltpu.VMEM((1024, CHANS), BF16),
            pltpu.VMEM((BLOCKS, CHANS, CB), BF16),
            pltpu.VMEM((BLOCKS, 3, 3, CB), F32),
            pltpu.VMEM((BLOCKS, CB, CHANS), BF16),
            pltpu.VMEM((10, 10, 16, CB), BF16),
            pltpu.VMEM((96, CB), F32),
            pltpu.VMEM((8, 8, 16, CB), BF16),
            pltpu.VMEM((1024, CHANS), F32),
            *attention_scratch(),
            pltpu.SemaphoreType.DMA((2 + BLOCKS, 3)),
        ],
        compiler_params=params(),
        cost_estimate=pl.CostEstimate(
            flops=4 * 1024 * CHANS * WIDE, bytes_accessed=8 * 2**20, transcendentals=2048 * WIDE
        ),
        name="local_part",
    )((top, bottom)[part], left, right, *kept_in_hbm(*arrays))


def exchange(blocks, groups):
    return lax.all_to_all(blocks, ("row", "col"), 0, 0, axis_index_groups=groups, tiled=True)


def on_device(field, w_expand, dw_kernel, w_project, qkv_block, out_block, qkv_grid, out_grid):
    n_row, n_col = lax.axis_size("row"), lax.axis_size("col")
    down = [(i, i + 1) for i in range(n_row - 1)]
    up = [(i + 1, i) for i in range(n_row - 1)]
    top = lax.ppermute(field[31], "row", down)
    bottom = lax.ppermute(field[0], "row", up)
    fill = jnp.zeros((14, CHANS), BF16)

    def rim(column):
        return jnp.concatenate([top[column : column + 1], field[:, column], bottom[column : column + 1], fill], axis=0)

    east, west = rim(63), rim(0)
    left = lax.ppermute(east, "col", [(i, i + 1) for i in range(n_col - 1)])
    right = lax.ppermute(west, "col", [(i + 1, i) for i in range(n_col - 1)])
    normed, xp = prepare(field, east)
    groups = [[32 * row + 4 * j + c for row in range(n_row) for j in range(8)] for c in range(4)]
    gathered = []
    for part in range(2):
        blocked = local_part(
            part, (top, bottom, left, right), normed, xp, w_expand, dw_kernel, w_project, qkv_block, out_block
        )
        gathered.append(exchange(blocked.reshape(32, 2, 16, CHANS), groups).reshape(64, 16, CHANS))
    attended = grid_attention(gathered[0], qkv_grid, out_grid)
    attended = grid_attention(gathered[1], qkv_grid, out_grid, attended)
    home = exchange(attended, groups).reshape(8, 4, 2, 2, 16, CHANS)
    return home.transpose(3, 2, 0, 1, 4, 5).reshape(32, 64, CHANS)


def solution(mesh):
    placed = (P("row", "col", None), P(), P(), P(), P(), P(), P(), P())
    return jax.shard_map(
        on_device, mesh=mesh, in_specs=placed, out_specs=P("row", "col", None), check_vma=False
    )
```
